128 devices in a mesh: tp: 16 (over z, y), ep: 8 (over x, core).
Axes of the slice: x: 4, y: 4, z: 4, core: 2. Of those that a mesh axis runs over, the one named last changes fastest.
Arguments:
- attn_out: bfloat16 [16384, 8192], P('ep', 'tp'), may hold values from -6 to 6
- residual: bfloat16 [16384, 7168], P(('ep', 'tp')), may hold values from -6 to 6
- w_out: bfloat16 [8192, 7168], P('tp'), may hold values from -0.0625 to 0.0625
- norm_gain: bfloat16 [7168], replicated, may hold values from 0.5 to 1.5
- router: bfloat16 [7168, 256], P(None, 'tp'), may hold values from -0.0625 to 0.0625
- router_bias: float32 [256], replicated, may hold values from -3 to 3
- choices: int32 [16384, 8], P(('ep', 'tp')), may hold values from 0 to 255, as said below
- w_gate: bfloat16 [16, 7168, 2048], P('tp', None, 'ep'), may hold values from -0.0625 to 0.0625
- w_up: bfloat16 [16, 7168, 2048], P('tp', None, 'ep'), may hold values from -0.0625 to 0.0625
- w_down: bfloat16 [16, 2048, 7168], P('tp', 'ep'), may hold values from -0.125 to 0.125
Outputs:
- hidden_out: bfloat16 [16384, 7168], P(('ep', 'tp'))
- moe_out: bfloat16 [16384, 7168], P(('ep', 'tp'))
- load: float32 [256], replicated
- bias_next: float32 [256], replicated
The draws below stay inside these ranges and needn't reach their ends.
Inputs may be any that keep to these rules, and one draw needn't show every extreme that they name: `choices`: each row names 8 different experts. Among the rows of one device no expert below 16 is named by more than 2 rows; one such expert is named by exactly 2 rows of every device.
All inputs are finite; a program needn't handle non-finite values.
Results may differ from the reference program's by a relative error of at most 0.034.
Values may be sent and summed in bfloat16 or wider, within the bound.
A program may use at most 128 MiB of HBM per device.

```python
import jax
import jax.numpy as jnp
from jax import lax

D = 7168
HEADS = 64
HD = 128
FF = 2048
ROUTED = 256
TOP = 8
TOK_DEV = 128
CAP = 2
FLIGHT = 16
TOKENS = 16384
N_TP = 16
N_EP = 8


def draw_choices(key, part):
    key = jax.random.fold_in(key, 7)
    key_hot, key_level, key_count, key_order, key_rest, key_favour, key_pull, key_group, key_lean = jax.random.split(key, 9)
    blocks = TOKENS // TOK_DEV
    hottest = jax.random.randint(key_hot, (), 0, FLIGHT)
    rising = 1 + 3 * jnp.arange(blocks, dtype=jnp.int32) // blocks
    levels = jax.random.randint(key_level, (FLIGHT,), 1, 5)
    ceiling = jnp.minimum(CAP, levels[None, :] * rising[:, None] * CAP // 8 + 1)
    counts = jax.random.randint(key_count, (blocks, FLIGHT), 0, ceiling + 1)
    counts = jnp.where(jnp.arange(FLIGHT)[None, :] == hottest, CAP, counts)
    orders = jax.random.permutation(key_order, jnp.broadcast_to(jnp.arange(TOK_DEV, dtype=jnp.int32), (blocks, TOK_DEV)), axis=1, independent=True)
    shifted = (orders[:, :, None] - CAP * jnp.arange(FLIGHT, dtype=jnp.int32)[None, None, :]) % TOK_DEV
    member = (shifted < counts[:, None, :]).reshape(TOKENS, FLIGHT)
    window_ids = jnp.where(member, jnp.arange(FLIGHT, dtype=jnp.int32)[None, :], ROUTED + FLIGHT)
    window_ids = jnp.sort(window_ids, axis=1)
    chosen_count = jnp.sum(member.astype(jnp.int32), axis=1)
    ranking = jax.random.randint(key_rest, (TOKENS, ROUTED), 0, 1048576) * ROUTED + jnp.arange(ROUTED, dtype=jnp.int32)[None, :]
    block_ids = jnp.arange(blocks, dtype=jnp.int32)
    blocks_ep = blocks // FLIGHT
    position = block_ids % FLIGHT * blocks_ep + block_ids // FLIGHT
    token_block = jnp.arange(TOKENS, dtype=jnp.int32) // TOK_DEV
    expert_ids = jnp.arange(ROUTED, dtype=jnp.int32)
    rest_order = jax.random.permutation(key_group, ROUTED - FLIGHT).astype(jnp.int32)
    coin = jax.random.randint(jax.random.fold_in(key_group, 1), (ROUTED - FLIGHT,), 0, 2)
    rest_group = jnp.where(rest_order < TOP, 1, jnp.where(rest_order < 2 * TOP, 0, coin))
    group = jnp.concatenate([jnp.zeros((FLIGHT,), jnp.int32), rest_group.astype(jnp.int32)])
    lean_level = 1 + 8 * position // blocks
    lean = (jax.random.randint(key_lean, (TOKENS,), 0, 10) < lean_level[token_block]).astype(jnp.int32)
    ranking = ranking + jnp.where(group[None, :] == lean[:, None], 268435456, 0)
    ranking = jnp.where(expert_ids[None, :] < FLIGHT, -1, ranking)
    favoured = jax.random.randint(key_favour, (), FLIGHT, ROUTED)
    threshold = 1 + 9 * position // (2 * blocks)
    pulled = jax.random.randint(key_pull, (TOKENS,), 0, 12) < threshold[token_block]
    boost = jnp.where(pulled[:, None] & (expert_ids[None, :] == favoured), 1073741824, 0)
    ranking = jnp.where(boost > 0, boost, ranking)
    others = lax.top_k(ranking, TOP)[1].astype(jnp.int32)
    joined = jnp.concatenate([window_ids[:, :TOP].astype(jnp.int32), others], axis=1)
    place = jnp.arange(TOP, dtype=jnp.int32)[None, :]
    pick = jnp.where(place < chosen_count[:, None], place, TOP + place - chosen_count[:, None])
    return jnp.take_along_axis(joined, pick, axis=1).astype(jnp.int32)


def shard_levels(key, dims, shards, smallest, high):
    factor_of = 1.0
    for dim, shards_of in shards:
        steps = jax.random.uniform(jax.random.fold_in(jax.random.fold_in(key, 6), dim), (shards_of,), jnp.float32, smallest / len(shards), high / len(shards))
        factor_of = factor_of * jnp.repeat(jnp.exp(steps), dims[dim] // shards_of).reshape((-1,) + (1,) * (len(dims) - 1 - dim))
    return factor_of


def noise(own_key, dims, spread, bound, cuts=(), kind=jnp.bfloat16):
    drawn = spread * jax.random.normal(own_key, dims, jnp.float32)
    if cuts:
        drawn = drawn * shard_levels(own_key, dims, cuts, -0.22, 0.18)
    return jnp.clip(drawn, -bound, bound).astype(kind)


def setup_inputs(seed: int = 0) -> dict:
    splits = jax.random.split(jax.random.key(seed), 11)
    attn_out = noise(splits[0], (TOKENS, HEADS * HD), 1.0, 6.0, ((0, 8), (1, 16)))
    residual = noise(splits[1], (TOKENS, D), 1.0, 6.0, ((0, 128),))
    w_out = noise(splits[2], (HEADS * HD, D), (HEADS * HD) ** -0.5, 0.0625, ((0, 16),))
    norm_gain = jnp.clip(1.0 + 0.1 * jax.random.normal(splits[3], (D,), jnp.float32), 0.5, 1.5).astype(jnp.bfloat16)
    router = noise(splits[4], (D, ROUTED), D ** -0.5, 0.0625, ((1, 16),))
    router_bias = noise(splits[5], (ROUTED,), 0.2, 3.0, (), jnp.float32)
    choices = draw_choices(jax.random.fold_in(splits[10], 71), 0)
    w_gate = noise(splits[7], (FLIGHT, D, FF), D ** -0.5, 0.0625, ((0, 16), (2, 8)))
    w_up = noise(splits[8], (FLIGHT, D, FF), D ** -0.5, 0.0625, ((0, 16), (2, 8)))
    w_down = noise(splits[9], (FLIGHT, FF, D), FF ** -0.5, 0.125, ((0, 16), (1, 8)))
    return {"attn_out": attn_out, "residual": residual, "w_out": w_out, "norm_gain": norm_gain, "router": router, "router_bias": router_bias, "choices": choices, "w_gate": w_gate, "w_up": w_up, "w_down": w_down}


norm_eps = 1e-06
route_scale = 2.5
bias_rate = 0.001

def reference(attn_out, residual, w_out, norm_gain, router, router_bias, choices, w_gate, w_up, w_down):
    head_cols = HEADS * HD // N_TP
    projected = jnp.zeros(residual.shape, jnp.float32)
    for head_group in range(N_TP):
        part_cols = attn_out[:, head_group * head_cols:(head_group + 1) * head_cols]
        part_rows = w_out[head_group * head_cols:(head_group + 1) * head_cols]
        partial_value = jnp.dot(part_cols, part_rows, preferred_element_type=jnp.float32).astype(jnp.bfloat16)
        partial_value = lax.optimization_barrier(partial_value)
        projected = projected + partial_value.astype(jnp.float32)
    hidden_out = (residual.astype(jnp.float32) + projected).astype(jnp.bfloat16)
    stream = hidden_out.astype(jnp.float32)
    scaled = stream * lax.rsqrt(lax.optimization_barrier(jnp.mean(stream * stream, axis=-1, keepdims=True)) + norm_eps)
    normed = (scaled * norm_gain.astype(jnp.float32)).astype(jnp.bfloat16)
    scores = jax.nn.sigmoid(jnp.dot(normed, router, preferred_element_type=jnp.float32))
    chosen = jnp.take_along_axis(scores, choices, axis=1)
    weights = route_scale * chosen / lax.optimization_barrier(jnp.sum(chosen, axis=-1, keepdims=True))
    flight_ids = jnp.arange(FLIGHT, dtype=jnp.int32)
    matches = choices[:, :, None] == flight_ids[None, None, :]
    expert_weight = lax.optimization_barrier(jnp.sum(jnp.where(matches, weights[:, :, None], 0.0), axis=1))
    member = jnp.any(matches, axis=1).astype(jnp.int32)
    devices = N_TP * N_EP
    slots = devices * CAP
    blocked = member.reshape(devices, TOK_DEV, FLIGHT)
    slot_rank = (jnp.cumsum(blocked, axis=1) - blocked).reshape(TOKENS, FLIGHT)
    block_of = jnp.arange(TOKENS, dtype=jnp.int32) // TOK_DEV
    mixed = jnp.zeros(residual.shape, jnp.float32)
    for expert in range(FLIGHT):
        target = jnp.where(member[:, expert] == 1, block_of * CAP + slot_rank[:, expert], slots).astype(jnp.int32)
        buffer = jnp.zeros((slots + 1, D), jnp.bfloat16).at[target].set(normed)[:slots]
        gate_val = jnp.dot(buffer, w_gate[expert], preferred_element_type=jnp.float32)
        up_val = jnp.dot(buffer, w_up[expert], preferred_element_type=jnp.float32)
        active = (jax.nn.silu(gate_val) * up_val).astype(jnp.bfloat16)
        output = jnp.dot(active, w_down[expert], preferred_element_type=jnp.float32).astype(jnp.bfloat16)
        fetched = jnp.concatenate([output, jnp.zeros((1, D), jnp.bfloat16)], axis=0)[target]
        mixed = mixed + expert_weight[:, expert:expert + 1] * fetched.astype(jnp.float32)
    moe_out = mixed.astype(jnp.bfloat16)
    counts = jnp.zeros((ROUTED,), jnp.int32).at[choices.reshape(-1)].add(1)
    load = counts.astype(jnp.float32) * ROUTED / (TOKENS * TOP)
    bias_next = router_bias + bias_rate * jnp.sign(TOKENS * TOP - counts * ROUTED).astype(jnp.float32)
    return (hidden_out, moe_out, load, bias_next)
```

```python
import jax
import jax.numpy as jnp
from jax import lax
from jax.experimental import pallas as pl
from jax.experimental.pallas import tpu as pltpu
from jax.sharding import PartitionSpec as P

TOP = 8
CAP = 2


norm_eps = 1e-06
route_scale = 2.5
bias_rate = 0.001


MESH = pl.DeviceIdType.MESH
VMEM = pltpu.VMEM
ROUNDS = 7
CH = 256


def ring(i):
    return lax.rem(i + 8, 4)


def place():
    tp = lax.axis_index("tp")
    ep = lax.axis_index("ep")
    return lax.div(tp, 4), lax.rem(tp, 4), lax.div(ep, 2), lax.rem(ep, 2)


def at(z, y, x, c):
    return (ring(z) * 4 + ring(y), ring(x) * 2 + lax.rem(c, 2))


def greet(peers):
    barrier = pltpu.get_barrier_semaphore()
    for peer in peers:
        pl.semaphore_signal(barrier, inc=1, device_id=peer, device_id_type=MESH)
    pl.semaphore_wait(barrier, len(peers))


def remote(src, dst, send, recv, peer):
    return pltpu.make_async_remote_copy(
        src_ref=src, dst_ref=dst, send_sem=send, recv_sem=recv, device_id=peer, device_id_type=MESH
    )


def project_kernel(
    a_ref, w_ref, res_ref, out_ref,
    ag, wown, wbuf, pbuf, rbuf, resv,
    loc, a_s, a_r, y_s, y_r, x_s, x_r, f_s, f_r, c_s, c_r, z_s, z_r,
):
    z, y, x, c = place()
    half = pl.multiple_of(c * 256, 256)
    own_a = pltpu.make_async_copy(a_ref.at[:, y], ag.at[0], loc.at[0])
    own_w = pltpu.make_async_copy(w_ref, wown, loc.at[1])
    own_res = pltpu.make_async_copy(res_ref, resv, loc.at[2])
    own_a.start()
    own_w.start()
    own_res.start()
    greet(
        [at(z, y + e, x, c) for e in (1, 2, 3)]
        + [at(z + e, y, x, c) for e in (1, 2, 3)]
        + [at(z, y, x + 1, c), at(z, y, x - 1, c), at(z, y, x, c + 1)]
    )
    sib = at(z, y, x, c + 1)

    def chunk(dx, r):
        return ring(x + dx) * ROUNDS + r

    def y_copy(r, e):
        n = chunk(0, r)
        cols = pl.ds(pl.multiple_of(n * CH, CH), CH)
        return remote(
            w_ref.at[pl.ds(half, 256), cols], wbuf.at[n, 3 - e, pl.ds(half, 256), :],
            y_s.at[r, e - 1], y_r.at[r, 3 - e], at(z, y + e, x, c),
        )

    def a_copy(e):
        return remote(a_ref.at[:, ring(y + e)], ag.at[4 - e], a_s.at[e - 1], a_r.at[3 - e], at(z, y + e, x, c))

    def x_copy(r, way):
        part = wbuf.at[chunk(0, r), :, pl.ds(half, 256), :]
        return remote(part, part, x_s.at[r, way], x_r.at[r, way], at(z, y, x + 1 - 2 * way, c))

    def x_land(r, way):
        part = wbuf.at[chunk(2 * way - 1, r), :, pl.ds(half, 256), :]
        return remote(part, part, x_s.at[r, way], x_r.at[r, way], at(z, y, x + 1 - 2 * way, c))

    def f_part(dx, r, way):
        return wbuf.at[chunk(dx, r), :, pl.ds(pl.multiple_of(half + 128 * way, 128), 128), :]

    def f_copy(r, way):
        part = f_part(2 * way - 1, r, way)
        return remote(part, part, f_s.at[r, way], f_r.at[r, way], at(z, y, x + 1 - 2 * way, c))

    def f_land(r, way):
        part = f_part(2, r, way)
        return remote(part, part, f_s.at[r, way], f_r.at[r, way], at(z, y, x + 1 - 2 * way, c))

    def hop(q):
        return (0, 3, 1, 2)[q]

    def c_copy(r, q):
        part = wbuf.at[chunk(hop(q), r), :, pl.ds(half, 256), :]
        return remote(part, part, c_s.at[r, q], c_r.at[r, q], sib)

    def c_land(n, r, q):
        other = pl.multiple_of(256 - half, 256)
        part = wbuf.at[n, :, pl.ds(other, 256), :]
        return remote(part, part, c_s.at[r, q], c_r.at[r, q], sib)

    def z_copy(n, e):
        return remote(pbuf.at[n, ring(z + e)], rbuf.at[n, 3 - e], z_s.at[n, e - 1], z_r.at[n, 3 - e], at(z + e, y, x, c))

    def z_land(n, k):
        return remote(pbuf.at[n, 0], rbuf.at[n, k], z_s.at[n, k], z_r.at[n, k], at(z + 1, y, x, c))

    def y_land(r, k):
        n = chunk(0, r)
        part = wbuf.at[n, k, pl.ds(half, 256), :]
        return remote(part, part, y_s.at[r, k], y_r.at[r, k], at(z, y + 1, x, c))

    def start_y(r):
        for e in (1, 3, 2):
            y_copy(r, e).start()

    def first(r):
        for k in range(3):
            y_land(r, k).wait_recv()
        x_copy(r, 0).start()
        x_copy(r, 1).start()
        c_copy(r, 0).start()

        @pl.when(r + 2 < ROUNDS)
        def _():
            start_y(r + 2)

    def multiply(r):
        @pl.loop(0, 4)
        def _(q):
            dx = q + lax.div(q, 2) - 2 * lax.div(q, 3)
            slot = q + lax.rem(q, 3) - 3 * lax.div(q, 2) + 3 * lax.div(q, 3)
            n = chunk(dx, r)
            c_land(n, r, slot).wait_recv()
            cols = pl.ds(pl.multiple_of(n * CH, CH), CH)
            total = jnp.dot(ag[0].reshape(512, 512), wown[:, cols], preferred_element_type=jnp.float32)
            for k in range(3):
                total += jnp.dot(ag[k + 1].reshape(512, 512), wbuf[n, k], preferred_element_type=jnp.float32)
            pbuf[n] = total.astype(jnp.bfloat16).reshape(4, 128, CH)
            for e in (2, 1, 3):
                z_copy(n, e).start()

    def finish(r):
        @pl.loop(0, 4)
        def _(q):
            dx = q + lax.div(q, 2) - 2 * lax.div(q, 3)
            n = chunk(dx, r)
            for k in range(3):
                z_land(n, k).wait_recv()
            cols = pl.ds(pl.multiple_of(n * CH, CH), CH)
            total = pbuf[n, z].astype(jnp.float32)
            for k in range(3):
                total += rbuf[n, k].astype(jnp.float32)
            out_ref[:, cols] = (resv[:, cols].astype(jnp.float32) + total).astype(jnp.bfloat16)

    start_y(0)
    for e in (2, 1, 3):
        a_copy(e).start()
    start_y(1)
    first(0)
    first(1)
    own_a.wait()
    own_w.wait()
    own_res.wait()

    @pl.loop(0, ROUNDS + 4)
    def _(r):
        @pl.when(r < ROUNDS)
        def _():
            for way in (0, 1):
                x_land(r, way).wait_recv()
                f_copy(r, way).start()
                c_copy(r, 1 + way).start()

        @pl.when(r + 2 < ROUNDS)
        def _():
            first(r + 2)

        @pl.when(r == 1)
        def _():
            for k in range(3):
                remote(ag.at[k + 1], ag.at[k + 1], a_s.at[k], a_r.at[k], at(z, y + 1, x, c)).wait_recv()

        @pl.when((r >= 1) & (r <= ROUNDS))
        def _():
            for way in (0, 1):
                f_land(r - 1, way).wait_recv()
            c_copy(r - 1, 3).start()
            multiply(r - 1)

        @pl.when(r >= 4)
        def _():
            finish(r - 4)

    for e in (1, 2, 3):
        a_copy(e).wait_send()

    @pl.loop(0, ROUNDS)
    def _(r):
        for e in (1, 2, 3):
            y_copy(r, e).wait_send()
        for way in (0, 1):
            x_copy(r, way).wait_send()
            f_copy(r, way).wait_send()
        for q in range(4):
            c_copy(r, q).wait_send()

    @pl.loop(0, 4 * ROUNDS)
    def _(n):
        for e in (1, 2, 3):
            z_copy(n, e).wait_send()


def project(attn_out, w_out, residual):
    dma = pltpu.SemaphoreType.DMA
    anywhere = pl.BlockSpec(memory_space=pl.ANY)
    return pl.pallas_call(
        project_kernel,
        name="project",
        out_shape=jax.ShapeDtypeStruct((128, 7168), jnp.bfloat16),
        in_specs=[anywhere] * 3,
        out_specs=pl.BlockSpec(memory_space=VMEM),
        scratch_shapes=[
            VMEM((4, 4, 128, 512), jnp.bfloat16),
            VMEM((512, 7168), jnp.bfloat16),
            VMEM((28, 3, 512, CH), jnp.bfloat16),
            VMEM((28, 4, 128, CH), jnp.bfloat16),
            VMEM((28, 3, 128, CH), jnp.bfloat16),
            VMEM((128, 7168), jnp.bfloat16),
            dma((3,)), dma((3,)), dma((3,)), dma((7, 3)), dma((7, 3)), dma((7, 2)), dma((7, 2)),
            dma((7, 2)), dma((7, 2)), dma((7, 4)), dma((7, 4)), dma((28, 3)), dma((28, 3)),
        ],
        compiler_params=pltpu.CompilerParams(
            collective_id=0, has_side_effects=True, vmem_limit_bytes=58 * 1024 * 1024
        ),
    )(attn_out.reshape(4, 4, 128, 512), w_out, residual)


def on_device(
    attn_out, residual, w_out, norm_gain, router, router_bias, choices, w_gate, w_up, w_down
):
    tp_count = lax.axis_size("tp")
    ep_count = lax.axis_size("ep")
    tok_rows = residual.shape[0]
    width = residual.shape[1]
    routed = router_bias.shape[0]
    hidden_out = project(attn_out, w_out, residual)
    stream = hidden_out.astype(jnp.float32)
    scaled = stream * lax.rsqrt(jnp.mean(stream * stream, axis=-1, keepdims=True) + norm_eps)
    normed = (scaled * norm_gain.astype(jnp.float32)).astype(jnp.bfloat16)
    logits = jnp.dot(
        normed, lax.all_gather(router, "tp", axis=1, tiled=True), preferred_element_type=jnp.float32
    )
    scores = jax.nn.sigmoid(logits)
    onehot = choices[:, :, None] == jnp.arange(routed, dtype=jnp.int32)[None, None, :]
    chosen = jnp.sum(jnp.where(onehot, scores[:, None, :], 0.0), axis=-1)
    weights = route_scale * chosen / jnp.sum(chosen, axis=-1, keepdims=True)
    window = onehot[:, :, :tp_count]
    expert_weight = jnp.sum(jnp.where(window, weights[:, :, None], 0.0), axis=1)
    member = jnp.any(window, axis=1).astype(jnp.int32)
    slot_rank = jnp.cumsum(member, axis=0) - member
    slot_ids = jnp.arange(CAP, dtype=jnp.int32)[None, :, None]
    slot_pick = (member.T[:, None, :] == 1) & (slot_rank.T[:, None, :] == slot_ids)
    outgoing = jnp.einsum(
        "wcr,rd->wcd", slot_pick.astype(jnp.bfloat16), normed, preferred_element_type=jnp.float32
    ).astype(jnp.bfloat16)
    landed = lax.all_to_all(outgoing, "tp", split_axis=0, concat_axis=0, tiled=True)
    arrived = lax.all_gather(landed[:, None], "ep", axis=1, tiled=True)
    group_rows = tp_count * CAP
    picked = arrived
    picked = jnp.swapaxes(picked, 0, 1).reshape(lax.axis_size("ep") * group_rows, width)
    gate_val = jnp.dot(picked, w_gate[0], preferred_element_type=jnp.float32)
    up_val = jnp.dot(picked, w_up[0], preferred_element_type=jnp.float32)
    active = (jax.nn.silu(gate_val) * up_val).astype(jnp.bfloat16)
    summed = lax.psum_scatter(
        jnp.dot(active, w_down[0], preferred_element_type=jnp.float32).astype(jnp.bfloat16),
        "ep",
        scatter_dimension=0,
        tiled=True,
    )
    outbound = summed.reshape(tp_count, CAP, width)
    returned = lax.all_to_all(outbound, "tp", split_axis=0, concat_axis=0, tiled=True)
    coeff = jnp.where(slot_pick, expert_weight.T[:, None, :], 0.0)
    mixed = jnp.einsum(
        "wcr,wcd->rd", coeff, returned.astype(jnp.float32), precision=lax.Precision.HIGHEST
    )
    moe_out = mixed.astype(jnp.bfloat16)
    local_counts = jnp.sum(onehot.astype(jnp.int32), axis=(0, 1))
    counts = lax.psum(local_counts, ("tp", "ep"))
    all_slots = tok_rows * tp_count * ep_count * TOP
    load = counts.astype(jnp.float32) * routed / all_slots
    bias_next = router_bias + bias_rate * jnp.sign(all_slots - counts * routed).astype(jnp.float32)
    return (hidden_out, moe_out, load, bias_next)


def solution(mesh):
    placed = (
        P("ep", "tp"),
        P(("ep", "tp"), None),
        P("tp", None),
        P(),
        P(None, "tp"),
        P(),
        P(("ep", "tp"), None),
        P("tp", None, "ep"),
        P("tp", None, "ep"),
        P("tp", "ep", None),
    )
    return jax.shard_map(
        on_device,
        mesh=mesh,
        in_specs=placed,
        out_specs=(P(("ep", "tp"), None), P(("ep", "tp"), None), P(), P()),
        check_vma=False,
    )
```

```python
import jax
import jax.numpy as jnp
from jax import lax
from jax.experimental import pallas as pl
from jax.experimental.pallas import tpu as pltpu
from jax.sharding import PartitionSpec as P

TOP = 8


norm_eps = 1e-06
route_scale = 2.5
bias_rate = 0.001


MESH = pl.DeviceIdType.MESH
VMEM = pltpu.VMEM
ROUNDS = 7
CH = 256


def ring(i):
    return lax.rem(i + 8, 4)


def place():
    tp = lax.axis_index("tp")
    ep = lax.axis_index("ep")
    return lax.div(tp, 4), lax.rem(tp, 4), lax.div(ep, 2), lax.rem(ep, 2)


def at(z, y, x, c):
    return (ring(z) * 4 + ring(y), ring(x) * 2 + lax.rem(c, 2))


def greet(peers):
    barrier = pltpu.get_barrier_semaphore()
    for peer in peers:
        pl.semaphore_signal(barrier, inc=1, device_id=peer, device_id_type=MESH)
    pl.semaphore_wait(barrier, len(peers))


def remote(src, dst, send, recv, peer):
    return pltpu.make_async_remote_copy(
        src_ref=src, dst_ref=dst, send_sem=send, recv_sem=recv, device_id=peer, device_id_type=MESH
    )


def project_kernel(
    a_ref, w_ref, res_ref, out_ref,
    ag, wown, wbuf, pbuf, rbuf, resv,
    loc, a_s, a_r, y_s, y_r, x_s, x_r, f_s, f_r, c_s, c_r, z_s, z_r,
):
    z, y, x, c = place()
    half = pl.multiple_of(c * 256, 256)
    own_a = pltpu.make_async_copy(a_ref.at[:, y], ag.at[0], loc.at[0])
    own_w = pltpu.make_async_copy(w_ref, wown, loc.at[1])
    own_res = pltpu.make_async_copy(res_ref, resv, loc.at[2])
    own_a.start()
    own_w.start()
    own_res.start()
    greet(
        [at(z, y + e, x, c) for e in (1, 2, 3)]
        + [at(z + e, y, x, c) for e in (1, 2, 3)]
        + [at(z, y, x + 1, c), at(z, y, x - 1, c), at(z, y, x, c + 1)]
    )
    sib = at(z, y, x, c + 1)

    def chunk(dx, r):
        return ring(x + dx) * ROUNDS + r

    def y_copy(r, e):
        n = chunk(0, r)
        cols = pl.ds(pl.multiple_of(n * CH, CH), CH)
        return remote(
            w_ref.at[pl.ds(half, 256), cols], wbuf.at[n, 3 - e, pl.ds(half, 256), :],
            y_s.at[r, e - 1], y_r.at[r, 3 - e], at(z, y + e, x, c),
        )

    def a_copy(e):
        return remote(a_ref.at[:, ring(y + e)], ag.at[4 - e], a_s.at[e - 1], a_r.at[3 - e], at(z, y + e, x, c))

    def x_copy(r, way):
        part = wbuf.at[chunk(0, r), :, pl.ds(half, 256), :]
        return remote(part, part, x_s.at[r, way], x_r.at[r, way], at(z, y, x + 1 - 2 * way, c))

    def x_land(r, way):
        part = wbuf.at[chunk(2 * way - 1, r), :, pl.ds(half, 256), :]
        return remote(part, part, x_s.at[r, way], x_r.at[r, way], at(z, y, x + 1 - 2 * way, c))

    def f_part(dx, r, way):
        return wbuf.at[chunk(dx, r), :, pl.ds(pl.multiple_of(half + 128 * way, 128), 128), :]

    def f_copy(r, way):
        part = f_part(2 * way - 1, r, way)
        return remote(part, part, f_s.at[r, way], f_r.at[r, way], at(z, y, x + 1 - 2 * way, c))

    def f_land(r, way):
        part = f_part(2, r, way)
        return remote(part, part, f_s.at[r, way], f_r.at[r, way], at(z, y, x + 1 - 2 * way, c))

    def hop(q):
        return (0, 3, 1, 2)[q]

    def c_copy(r, q):
        part = wbuf.at[chunk(hop(q), r), :, pl.ds(half, 256), :]
        return remote(part, part, c_s.at[r, q], c_r.at[r, q], sib)

    def c_land(n, r, q):
        other = pl.multiple_of(256 - half, 256)
        part = wbuf.at[n, :, pl.ds(other, 256), :]
        return remote(part, part, c_s.at[r, q], c_r.at[r, q], sib)

    def z_copy(n, e):
        return remote(pbuf.at[n, ring(z + e)], rbuf.at[n, 3 - e], z_s.at[n, e - 1], z_r.at[n, 3 - e], at(z + e, y, x, c))

    def z_land(n, k):
        return remote(pbuf.at[n, 0], rbuf.at[n, k], z_s.at[n, k], z_r.at[n, k], at(z + 1, y, x, c))

    def y_land(r, k):
        n = chunk(0, r)
        part = wbuf.at[n, k, pl.ds(half, 256), :]
        return remote(part, part, y_s.at[r, k], y_r.at[r, k], at(z, y + 1, x, c))

    def start_y(r):
        for e in (1, 3, 2):
            y_copy(r, e).start()

    def first(r):
        for k in range(3):
            y_land(r, k).wait_recv()
        x_copy(r, 0).start()
        x_copy(r, 1).start()
        c_copy(r, 0).start()

        @pl.when(r + 2 < ROUNDS)
        def _():
            start_y(r + 2)

    def multiply(r):
        @pl.loop(0, 4)
        def _(q):
            dx = q + lax.div(q, 2) - 2 * lax.div(q, 3)
            slot = q + lax.rem(q, 3) - 3 * lax.div(q, 2) + 3 * lax.div(q, 3)
            n = chunk(dx, r)
            c_land(n, r, slot).wait_recv()
            cols = pl.ds(pl.multiple_of(n * CH, CH), CH)
            total = jnp.dot(ag[0].reshape(512, 512), wown[:, cols], preferred_element_type=jnp.float32)
            for k in range(3):
                total += jnp.dot(ag[k + 1].reshape(512, 512), wbuf[n, k], preferred_element_type=jnp.float32)
            pbuf[n] = total.astype(jnp.bfloat16).reshape(4, 128, CH)
            for e in (2, 1, 3):
                z_copy(n, e).start()

    def finish(r):
        @pl.loop(0, 4)
        def _(q):
            dx = q + lax.div(q, 2) - 2 * lax.div(q, 3)
            n = chunk(dx, r)
            for k in range(3):
                z_land(n, k).wait_recv()
            cols = pl.ds(pl.multiple_of(n * CH, CH), CH)
            total = pbuf[n, z].astype(jnp.float32)
            for k in range(3):
                total += rbuf[n, k].astype(jnp.float32)
            out_ref[:, cols] = (resv[:, cols].astype(jnp.float32) + total).astype(jnp.bfloat16)

    start_y(0)
    for e in (2, 1, 3):
        a_copy(e).start()
    start_y(1)
    first(0)
    first(1)
    own_a.wait()
    own_w.wait()
    own_res.wait()

    @pl.loop(0, ROUNDS + 4)
    def _(r):
        @pl.when(r < ROUNDS)
        def _():
            for way in (0, 1):
                x_land(r, way).wait_recv()
                f_copy(r, way).start()
                c_copy(r, 1 + way).start()

        @pl.when(r + 2 < ROUNDS)
        def _():
            first(r + 2)

        @pl.when(r == 1)
        def _():
            for k in range(3):
                remote(ag.at[k + 1], ag.at[k + 1], a_s.at[k], a_r.at[k], at(z, y + 1, x, c)).wait_recv()

        @pl.when((r >= 1) & (r <= ROUNDS))
        def _():
            for way in (0, 1):
                f_land(r - 1, way).wait_recv()
            c_copy(r - 1, 3).start()
            multiply(r - 1)

        @pl.when(r >= 4)
        def _():
            finish(r - 4)

    for e in (1, 2, 3):
        a_copy(e).wait_send()

    @pl.loop(0, ROUNDS)
    def _(r):
        for e in (1, 2, 3):
            y_copy(r, e).wait_send()
        for way in (0, 1):
            x_copy(r, way).wait_send()
            f_copy(r, way).wait_send()
        for q in range(4):
            c_copy(r, q).wait_send()

    @pl.loop(0, 4 * ROUNDS)
    def _(n):
        for e in (1, 2, 3):
            z_copy(n, e).wait_send()


def project(attn_out, w_out, residual):
    dma = pltpu.SemaphoreType.DMA
    anywhere = pl.BlockSpec(memory_space=pl.ANY)
    return pl.pallas_call(
        project_kernel,
        name="project",
        out_shape=jax.ShapeDtypeStruct((128, 7168), jnp.bfloat16),
        in_specs=[anywhere] * 3,
        out_specs=pl.BlockSpec(memory_space=VMEM),
        scratch_shapes=[
            VMEM((4, 4, 128, 512), jnp.bfloat16),
            VMEM((512, 7168), jnp.bfloat16),
            VMEM((28, 3, 512, CH), jnp.bfloat16),
            VMEM((28, 4, 128, CH), jnp.bfloat16),
            VMEM((28, 3, 128, CH), jnp.bfloat16),
            VMEM((128, 7168), jnp.bfloat16),
            dma((3,)), dma((3,)), dma((3,)), dma((7, 3)), dma((7, 3)), dma((7, 2)), dma((7, 2)),
            dma((7, 2)), dma((7, 2)), dma((7, 4)), dma((7, 4)), dma((28, 3)), dma((28, 3)),
        ],
        compiler_params=pltpu.CompilerParams(
            collective_id=0, has_side_effects=True, vmem_limit_bytes=58 * 1024 * 1024
        ),
    )(attn_out.reshape(4, 4, 128, 512), w_out, residual)


LANE = 896
GROUPS = ((0, 0), (1, 1), (2, 3), (3, 2))


def moe_kernel(
    hid_ref, gain_ref, rout_ref, bias_ref, cho_ref, wg_ref, wu_ref, wd_ref,
    moe_ref, load_ref, next_ref,
    wg, wu, wd, rt, normed, snd, land, rows, ybuf, r1, sbuf, r2, rsend, ret, cnt, cnt_tp, cnt_ep,
    loc, d_s, d_r, ax_s, ax_r, ac_s, ac_r, k_s, k_r, l_s, l_r, rt_s, rt_r, rs_s, rs_r,
    p_s, p_r, q_s, q_r, b_s, b_r,
):
    z, y, x, c = place()
    tp = z * 4 + y
    ep = x * 2 + c
    sib = at(z, y, x, c + 1)
    width = hid_ref.shape[1]
    half = pl.ds(pl.multiple_of(c * (width // 2), width // 2), width // 2)
    loads = [pltpu.make_async_copy(s, d, loc.at[i]) for i, (s, d) in enumerate(((wg_ref, wg), (wu_ref, wu), (wd_ref, wd)))]
    for load in loads:
        load.start()
    tp_peers = [(dz, dy) for dz in (0, 1, 3, 2) for dy in (1, 3, 2, 0) if (dz, dy) != (0, 0)]
    ep_peers = [(dx, dc) for dx in (0, 1, 3, 2) for dc in (0, 1) if (dx, dc) != (0, 0)]

    def tp_at(dz, dy):
        return ring(z + dz) * 4 + ring(y + dy)

    def ep_at(dx, dc):
        return ring(x + dx) * 2 + lax.rem(c + dc, 2)

    barrier = pltpu.get_barrier_semaphore()
    for p in tp_peers:
        pl.semaphore_signal(barrier, inc=1, device_id=(tp_at(*p), ep), device_id_type=MESH)
    for p in ep_peers:
        pl.semaphore_signal(barrier, inc=1, device_id=(tp, ep_at(*p)), device_id_type=MESH)

    def cut(j):
        return slice(j * LANE, (j + 1) * LANE)

    ssq = jnp.zeros((128, 1), jnp.float32)
    for j in range(8):
        h = hid_ref[:, cut(j)].astype(jnp.float32)
        ssq += jnp.sum(h * h, axis=1, keepdims=True)
    scale = lax.rsqrt(ssq / width + norm_eps)
    for j in range(8):
        h = hid_ref[:, cut(j)].astype(jnp.float32)
        normed[:, cut(j)] = (h * scale * gain_ref[:, cut(j)].astype(jnp.float32)).astype(jnp.bfloat16)

    row = lax.broadcasted_iota(jnp.int32, (256, 128), 0)
    lane = lax.broadcasted_iota(jnp.int32, (256, 128), 1)
    expert = row // 16
    member = jnp.zeros((256, 128), jnp.float32)
    named = jnp.zeros((256, 128), jnp.float32)
    for k in range(TOP):
        ck = cho_ref[k : k + 1, :]
        member += jnp.where(ck == expert, 1.0, 0.0)
        named += jnp.where(ck == row, 1.0, 0.0)
    before = jnp.where(row[:128] < lane[:128], 1.0, 0.0).astype(jnp.bfloat16)
    rank = jnp.dot(member.astype(jnp.bfloat16), before, preferred_element_type=jnp.float32)
    slot = ((row // 8) % 2).astype(jnp.float32)
    pick = jnp.where(rank == slot, member, 0.0)
    feature = row % 8
    outgoing = jnp.zeros((256, LANE), jnp.float32)
    for j in range(8):
        pj = jnp.where(feature == j, pick, 0.0).astype(jnp.bfloat16)
        outgoing += jnp.dot(pj, normed[:, cut(j)], preferred_element_type=jnp.float32)
    snd[...] = outgoing.astype(jnp.bfloat16).reshape(16, 16, LANE)
    contract_last = (((1,), (1,)), ((), ()))
    cnt[...] = lax.dot_general(
        jnp.ones((8, 128), jnp.bfloat16), named.astype(jnp.bfloat16), contract_last, preferred_element_type=jnp.float32
    )
    pl.semaphore_wait(barrier, len(tp_peers) + len(ep_peers))

    def d_copy(p):
        peer = tp_at(*p)
        return remote(snd.at[peer], land.at[ep, tp], d_s.at[peer], d_r.at[tp], (peer, ep))

    own_rows = pltpu.make_async_copy(snd.at[tp], land.at[ep, tp], loc.at[3])
    own_rows.start()
    for p in tp_peers:
        d_copy(p).start()

    def k_copy(p):
        peer = tp_at(*p)
        return remote(cnt, cnt_tp.at[tp], k_s.at[peer], k_r.at[tp], (peer, ep))

    for p in tp_peers:
        k_copy(p).start()

    def group(dz):
        return pl.ds(pl.multiple_of(ring(z + dz) * 4, 4), 4)

    def x_copy(g, dz, e):
        part = land.at[ep, group(dz)]
        return remote(part, part, ax_s.at[g, e - 1], ax_r.at[g, 3 - e], (tp, ep_at(e, 0)))

    def x_land(g, dz, k):
        part = land.at[ep_at(k + 1, 0), group(dz)]
        return remote(part, part, ax_s.at[g, k], ax_r.at[g, k], (tp, ep_at(1, 0)))

    def c_copy(g, dz, q):
        part = land.at[ep_at(q, 0), group(dz)]
        return remote(part, part, ac_s.at[g, q], ac_r.at[g, q], sib)

    def c_land(g, dz, q):
        part = land.at[ep_at(q, 1), group(dz)]
        return remote(part, part, ac_s.at[g, q], ac_r.at[g, q], sib)

    def d_land(p):
        src = tp_at(*p)
        return remote(snd.at[src], land.at[ep, src], d_s.at[src], d_r.at[src], (src, ep))

    for g, dz in GROUPS:
        for p in tp_peers:
            if p[0] == dz:
                d_land(p).wait_recv()
        if dz == 0:
            own_rows.wait()
        for e in (1, 3, 2):
            x_copy(g, dz, e).start()
        c_copy(g, dz, 0).start()

    def rt_copy(p):
        peer = tp_at(*p)
        return remote(rout_ref.at[:, half], rt.at[tp, :, half], rt_s.at[peer], rt_r.at[tp], (peer, ep))

    own_rt = pltpu.make_async_copy(rout_ref.at[:, half], rt.at[tp, :, half], loc.at[4])
    own_rt.start()
    for p in tp_peers:
        rt_copy(p).start()

    for p in tp_peers:
        src = tp_at(*p)
        remote(cnt, cnt_tp.at[src], k_s.at[src], k_r.at[src], (src, ep)).wait_recv()
    cnt_tp[tp] = cnt[...]
    part_sum = cnt_tp[0]
    for i in range(1, 16):
        part_sum += cnt_tp[i]
    cnt_ep[ep] = part_sum

    def l_copy(p):
        peer = ep_at(*p)
        return remote(cnt_ep.at[ep], cnt_ep.at[ep], l_s.at[peer], l_r.at[ep], (tp, peer))

    for p in ep_peers:
        l_copy(p).start()

    for g, dz in GROUPS:
        for k in (0, 2, 1):
            x_land(g, dz, k).wait_recv()
            c_copy(g, dz, k + 1).start()
    for g, dz in GROUPS:
        for q in range(4):
            c_land(g, dz, q).wait_recv()
    out_row = lax.broadcasted_iota(jnp.int32, (128, 128), 0)
    in_row = lax.broadcasted_iota(jnp.int32, (128, 128), 1)
    source = ((out_row % 16) // 2) * 16 + (out_row % 2) * 8 + out_row // 16
    perm = jnp.where(in_row == source, 1.0, 0.0).astype(jnp.bfloat16)

    @pl.loop(0, 16)
    def _(i):
        group_of, part = lax.div(i, 2), lax.rem(i, 2)
        block = land[group_of, pl.ds(pl.multiple_of(part * 8, 8), 8)].reshape(128, LANE)
        turned = jnp.dot(perm, block, preferred_element_type=jnp.float32).astype(jnp.bfloat16)
        rows[:, pl.ds(pl.multiple_of(i * 16, 16), 16), :] = turned.reshape(8, 16, LANE)

    for load in loads:
        load.wait()
    gate_val = jnp.zeros((256, 256), jnp.float32)
    up_val = jnp.zeros((256, 256), jnp.float32)
    for j in range(8):
        gate_val += jnp.dot(rows[j], wg[cut(j), :], preferred_element_type=jnp.float32)
        up_val += jnp.dot(rows[j], wu[cut(j), :], preferred_element_type=jnp.float32)
    active = (gate_val / (1.0 + jnp.exp(-gate_val)) * up_val).astype(jnp.bfloat16)

    def p_copy(n):
        return remote(ybuf.at[n, :, 1 - c], r1.at[n], p_s.at[n], p_r.at[n], sib)

    def q_copy(n, e):
        return remote(sbuf.at[n, ring(x + e)], r2.at[n, 3 - e], q_s.at[n, e - 1], q_r.at[n, 3 - e], (tp, ep_at(e, 0)))

    def q_land(n, k):
        return remote(r2.at[n, k], r2.at[n, k], q_s.at[n, k], q_r.at[n, k], (tp, ep_at(1, 0)))

    for n in range(4):
        part = jnp.dot(active, wd[:, n * 2 * LANE : (n + 1) * 2 * LANE], preferred_element_type=jnp.float32)
        ybuf[n] = part.astype(jnp.bfloat16).reshape(4, 2, 32, 2 * LANE)
        p_copy(n).start()
    for n in range(4):
        p_copy(n).wait_recv()
        for i in range(4):
            both = ybuf[n, i, c].astype(jnp.float32) + r1[n, i].astype(jnp.float32)
            sbuf[n, i] = both.astype(jnp.bfloat16)
        for e in (1, 3, 2):
            q_copy(n, e).start()

    for p in ep_peers:
        peer = ep_at(*p)
        remote(cnt_ep.at[peer], cnt_ep.at[peer], l_s.at[peer], l_r.at[peer], (tp, peer)).wait_recv()
    counts = cnt_ep[0]
    for i in range(1, 8):
        counts += cnt_ep[i]
    counts = counts[0:1]
    slots = 128.0 * 128.0 * TOP
    load_ref[...] = counts * 256.0 / slots
    gap = slots - counts * 256.0
    sign = jnp.where(gap > 0.0, 1.0, jnp.where(gap < 0.0, -1.0, 0.0))
    next_ref[...] = bias_ref[...] + bias_rate * sign

    for p in tp_peers:
        src = tp_at(*p)
        remote(rout_ref.at[:, half], rt.at[src, :, half], rt_s.at[src], rt_r.at[src], (src, ep)).wait_recv()
    own_rt.wait()
    mine = rt.at[:, :, half]
    rt_sib = remote(mine, mine, rs_s.at[0], rs_r.at[0], sib)
    rt_sib.start()
    other = rt.at[:, :, pl.ds(pl.multiple_of((1 - c) * (width // 2), width // 2), width // 2)]
    remote(other, other, rs_s.at[0], rs_r.at[0], sib).wait_recv()
    logits = jnp.zeros((256, 128), jnp.float32)
    for j in range(8):
        logits += lax.dot_general(
            rt[:, :, cut(j)].reshape(256, LANE), normed[:, cut(j)], contract_last, preferred_element_type=jnp.float32
        )
    scores = 1.0 / (1.0 + jnp.exp(-logits))
    chosen = []
    for k in range(TOP):
        hit = cho_ref[k : k + 1, :] == row
        chosen.append(jnp.sum(jnp.where(hit, scores, 0.0), axis=0, keepdims=True))
    norm_by = chosen[0]
    for k in range(1, TOP):
        norm_by = norm_by + chosen[k]
    weight = jnp.zeros((256, 128), jnp.float32)
    for k in range(TOP):
        weight += jnp.where(cho_ref[k : k + 1, :] == expert, route_scale * chosen[k] / norm_by, 0.0)
    coeff = jnp.where(pick > 0.0, weight, 0.0).T
    lane_cut = lax.broadcasted_iota(jnp.int32, (128, 256), 1) % 8

    back_row = lax.broadcasted_iota(jnp.int32, (256, 32), 0)
    back_col = lax.broadcasted_iota(jnp.int32, (256, 32), 1)
    returned = jnp.zeros((256, LANE), jnp.float32)
    for n in range(4):
        for k in (0, 2, 1):
            q_land(n, k).wait_recv()
        total = sbuf[n, x].astype(jnp.float32)
        for k in range(3):
            total += r2[n, k].astype(jnp.float32)
        total = total.astype(jnp.bfloat16)
        for i in range(2):
            turn = jnp.where((back_row // 8 == back_col) & (back_row % 8 == 2 * n + i), 1.0, 0.0).astype(jnp.bfloat16)
            returned += jnp.dot(turn, total[:, cut(i)], preferred_element_type=jnp.float32)
    rsend[...] = returned.astype(jnp.bfloat16).reshape(16, 16, LANE)

    def b_copy(p):
        peer = tp_at(*p)
        return remote(rsend.at[peer], ret.at[tp], b_s.at[peer], b_r.at[tp], (peer, ep))

    own_back = pltpu.make_async_copy(rsend.at[tp], ret.at[tp], loc.at[5])
    own_back.start()
    for p in tp_peers:
        b_copy(p).start()
    high = coeff.astype(jnp.bfloat16)
    low = (coeff - high.astype(jnp.float32)).astype(jnp.bfloat16)
    own_back.wait()
    for p in tp_peers:
        src = tp_at(*p)
        remote(rsend.at[src], ret.at[src], b_s.at[src], b_r.at[src], (src, ep)).wait_recv()
    back = ret[...].reshape(256, LANE)
    for j in range(8):
        mixed = jnp.dot(jnp.where(lane_cut == j, high, 0.0).astype(jnp.bfloat16), back, preferred_element_type=jnp.float32)
        mixed += jnp.dot(jnp.where(lane_cut == j, low, 0.0).astype(jnp.bfloat16), back, preferred_element_type=jnp.float32)
        moe_ref[:, cut(j)] = mixed.astype(jnp.bfloat16)

    for p in tp_peers:
        d_copy(p).wait_send()
        k_copy(p).wait_send()
        rt_copy(p).wait_send()
        b_copy(p).wait_send()
    for p in ep_peers:
        l_copy(p).wait_send()
    rt_sib.wait_send()
    for g, dz in GROUPS:
        for e in (1, 2, 3):
            x_copy(g, dz, e).wait_send()
        for q in range(4):
            c_copy(g, dz, q).wait_send()
    for n in range(4):
        p_copy(n).wait_send()
        for e in (1, 2, 3):
            q_copy(n, e).wait_send()


def experts(hidden_out, norm_gain, router, router_bias, choices, w_gate, w_up, w_down):
    dma = pltpu.SemaphoreType.DMA
    bf16, f32 = jnp.bfloat16, jnp.float32
    vmem = pl.BlockSpec(memory_space=VMEM)
    anywhere = pl.BlockSpec(memory_space=pl.ANY)
    moe_out, load, bias_next = pl.pallas_call(
        moe_kernel,
        name="experts",
        out_shape=(
            jax.ShapeDtypeStruct((128, 7168), bf16),
            jax.ShapeDtypeStruct((1, 256), f32),
            jax.ShapeDtypeStruct((1, 256), f32),
        ),
        in_specs=[vmem] * 5 + [anywhere] * 3,
        out_specs=(vmem,) * 3,
        scratch_shapes=[
            VMEM((7168, 256), bf16), VMEM((7168, 256), bf16), VMEM((256, 7168), bf16),
            VMEM((16, 16, 7168), bf16), VMEM((128, 7168), bf16), VMEM((16, 16, LANE), bf16),
            VMEM((8, 16, 16, LANE), bf16), VMEM((8, 256, LANE), bf16),
            VMEM((4, 4, 2, 32, 2 * LANE), bf16), VMEM((4, 4, 32, 2 * LANE), bf16),
            VMEM((4, 4, 32, 2 * LANE), bf16), VMEM((4, 3, 32, 2 * LANE), bf16),
            VMEM((16, 16, LANE), bf16), VMEM((16, 16, LANE), bf16),
            VMEM((8, 256), f32), VMEM((16, 8, 256), f32), VMEM((8, 8, 256), f32),
            dma((6,)), dma((16,)), dma((16,)), dma((4, 3)), dma((4, 3)), dma((4, 4)), dma((4, 4)),
            dma((16,)), dma((16,)), dma((8,)), dma((8,)), dma((16,)), dma((16,)), dma((1,)), dma((1,)),
            dma((4,)), dma((4,)), dma((4, 3)), dma((4, 3)), dma((16,)), dma((16,)),
        ],
        compiler_params=pltpu.CompilerParams(
            collective_id=1, has_side_effects=True, vmem_limit_bytes=56 * 1024 * 1024
        ),
    )(
        hidden_out, norm_gain.reshape(1, -1), router.T, router_bias.reshape(1, -1), choices.T,
        w_gate[0], w_up[0], w_down[0],
    )
    return moe_out, load.reshape(-1), bias_next.reshape(-1)


def on_device(
    attn_out, residual, w_out, norm_gain, router, router_bias, choices, w_gate, w_up, w_down
):
    hidden_out = project(attn_out, w_out, residual)
    moe_out, load, bias_next = experts(
        hidden_out, norm_gain, router, router_bias, choices, w_gate, w_up, w_down
    )
    return (hidden_out, moe_out, load, bias_next)


def solution(mesh):
    placed = (
        P("ep", "tp"),
        P(("ep", "tp"), None),
        P("tp", None),
        P(),
        P(None, "tp"),
        P(),
        P(("ep", "tp"), None),
        P("tp", None, "ep"),
        P("tp", None, "ep"),
        P("tp", "ep", None),
    )
    return jax.shard_map(
        on_device,
        mesh=mesh,
        in_specs=placed,
        out_specs=(P(("ep", "tp"), None), P(("ep", "tp"), None), P(), P()),
        check_vma=False,
    )
```

```python
import jax
import jax.numpy as jnp
from jax import lax
from jax.experimental import pallas as pl
from jax.experimental.pallas import tpu as pltpu
from jax.sharding import PartitionSpec as P

TOP = 8


norm_eps = 1e-06
route_scale = 2.5
bias_rate = 0.001


MESH = pl.DeviceIdType.MESH
VMEM = pltpu.VMEM
ROUNDS = 7
SHARED = 6
CH = 256


def ring(i):
    return lax.rem(i + 8, 4)


def place():
    tp = lax.axis_index("tp")
    ep = lax.axis_index("ep")
    return lax.div(tp, 4), lax.rem(tp, 4), lax.div(ep, 2), lax.rem(ep, 2)


def at(z, y, x, c):
    return (ring(z) * 4 + ring(y), ring(x) * 2 + lax.rem(c, 2))


def greet(peers):
    barrier = pltpu.get_barrier_semaphore()
    for peer in peers:
        pl.semaphore_signal(barrier, inc=1, device_id=peer, device_id_type=MESH)
    pl.semaphore_wait(barrier, len(peers))


def remote(src, dst, send, recv, peer):
    return pltpu.make_async_remote_copy(
        src_ref=src, dst_ref=dst, send_sem=send, recv_sem=recv, device_id=peer, device_id_type=MESH
    )


def project_kernel(
    a_ref, w_ref, res_ref, out_ref,
    ag, wown, wbuf, pbuf, half_in, full_in, resv,
    loc, a_s, a_r, y_s, y_r, g_s, g_r, v_s, v_r, x_s, x_r, f_s, f_r, c_s, c_r, h_s, h_r, z_s, z_r,
):
    z, y, x, c = place()
    half = pl.multiple_of(c * 256, 256)
    own_a = pltpu.make_async_copy(a_ref.at[:, y], ag.at[0], loc.at[0])
    own_w = pltpu.make_async_copy(w_ref, wown, loc.at[1])
    own_res = pltpu.make_async_copy(res_ref, resv, loc.at[2])
    own_a.start()
    own_w.start()
    own_res.start()
    greet(
        [at(z, y + e, x, c) for e in (1, 2, 3)]
        + [at(z + e, y, x, c) for e in (1, 2, 3)]
        + [at(z, y, x + 1, c), at(z, y, x - 1, c), at(z, y, x, c + 1)]
    )
    sib = at(z, y, x, c + 1)

    def chunk(dx, r):
        return ring(x + dx) * ROUNDS + r

    def y_copy(i, n, way):
        cols = pl.ds(pl.multiple_of(n * CH, CH), CH)
        return remote(
            w_ref.at[pl.ds(half, 256), cols], wbuf.at[n, 2 - 2 * way, pl.ds(half, 256), :],
            y_s.at[i, way], y_r.at[i, way], at(z, y + 1 - 2 * way, x, c),
        )

    def y_land(i, n, way):
        part = wbuf.at[n, 2 - 2 * way, pl.ds(half, 256), :]
        return remote(part, part, y_s.at[i, way], y_r.at[i, way], at(z, y + 1, x, c))

    def g_copy(i, n, way):
        rows = pl.ds(pl.multiple_of(half + 128 * way, 128), 128)
        return remote(
            wbuf.at[n, 2 - 2 * way, rows, :], wbuf.at[n, 1, rows, :],
            g_s.at[i, way], g_r.at[i, way], at(z, y + 1 - 2 * way, x, c),
        )

    def common(u):
        return u * ROUNDS + SHARED

    def v_copy(u):
        part = wbuf.at[common(u), :, pl.ds(half, 256), :]
        return remote(part, part, v_s.at[u], v_r.at[u], sib)

    def v_land(u):
        part = wbuf.at[common(u), :, pl.ds(pl.multiple_of(256 - half, 256), 256), :]
        return remote(part, part, v_s.at[u], v_r.at[u], sib)

    def a_copy(g, e):
        return remote(a_ref.at[g, ring(y + e)], ag.at[4 - e, g], a_s.at[g, e - 1], a_r.at[g, 3 - e], at(z, y + e, x, c))

    def x_copy(r, way):
        part = wbuf.at[chunk(0, r), :, pl.ds(half, 256), :]
        return remote(part, part, x_s.at[r, way], x_r.at[r, way], at(z, y, x + 1 - 2 * way, c))

    def x_land(r, way):
        part = wbuf.at[chunk(2 * way - 1, r), :, pl.ds(half, 256), :]
        return remote(part, part, x_s.at[r, way], x_r.at[r, way], at(z, y, x + 1 - 2 * way, c))

    def f_part(dx, r, way):
        return wbuf.at[chunk(dx, r), :, pl.ds(pl.multiple_of(half + 128 * way, 128), 128), :]

    def f_copy(r, way):
        part = f_part(2 * way - 1, r, way)
        return remote(part, part, f_s.at[r, way], f_r.at[r, way], at(z, y, x + 1 - 2 * way, c))

    def f_land(r, way):
        part = f_part(2, r, way)
        return remote(part, part, f_s.at[r, way], f_r.at[r, way], at(z, y, x + 1 - 2 * way, c))

    def hop(q):
        return (0, 3, 1, 2)[q]

    def c_copy(r, q):
        part = wbuf.at[chunk(hop(q), r), :, pl.ds(half, 256), :]
        return remote(part, part, c_s.at[r, q], c_r.at[r, q], sib)

    def c_land(n, r, q):
        other = pl.multiple_of(256 - half, 256)
        part = wbuf.at[n, :, pl.ds(other, 256), :]
        return remote(part, part, c_s.at[r, q], c_r.at[r, q], sib)

    def halves(way):
        return pl.ds(64 * way, 64)

    def h_copy(n, way):
        return remote(
            pbuf.at[n, ring(z + 2), halves(way)], half_in.at[n, way],
            h_s.at[n, way], h_r.at[n, way], at(z + 1 - 2 * way, y, x, c),
        )

    def z_copy(n, way):
        to = z + 1 - 2 * way
        return remote(pbuf.at[n, ring(to)], full_in.at[n, way], z_s.at[n, way], z_r.at[n, way], at(to, y, x, c))

    def start_y(i, n):
        for way in (0, 1):
            y_copy(i, n, way).start()

    def start_a(g):
        for e in (2, 1, 3):
            a_copy(g, e).start()

    def pass_on(i, n):
        for way in (0, 1):
            y_land(i, n, way).wait_recv()
            g_copy(i, n, way).start()

    def first(r):
        for way in (0, 1):
            g_copy(r, chunk(0, r), way).wait_recv()
        x_copy(r, 0).start()
        x_copy(r, 1).start()
        c_copy(r, 0).start()

    def multiply(n):
        cols = pl.ds(pl.multiple_of(n * CH, CH), CH)
        total = jnp.dot(ag[0].reshape(512, 512), wown[:, cols], preferred_element_type=jnp.float32)
        for k in range(3):
            total += jnp.dot(ag[k + 1].reshape(512, 512), wbuf[n, k], preferred_element_type=jnp.float32)
        pbuf[n] = total.astype(jnp.bfloat16).reshape(4, 128, CH)
        for way in (0, 1):
            h_copy(n, way).start()

    def combine(n):
        for way in (0, 1):
            to = ring(z + 1 - 2 * way)
            h_copy(n, way).wait_recv()
            both = pbuf[n, to, halves(way)].astype(jnp.float32) + half_in[n, way].astype(jnp.float32)
            pbuf[n, to, halves(way)] = both.astype(jnp.bfloat16)
            z_copy(n, way).start()

    def finish(n):
        cols = pl.ds(pl.multiple_of(n * CH, CH), CH)
        total = pbuf[n, z].astype(jnp.float32)
        for way in (0, 1):
            z_copy(n, way).wait_recv()
            total += full_in[n, way].astype(jnp.float32)
        out_ref[:, cols] = (resv[:, cols].astype(jnp.float32) + total).astype(jnp.bfloat16)

    def near(q, r):
        return chunk(q + lax.div(q, 2), r)

    def step(work, r):
        @pl.when((r >= 0) & (r < SHARED))
        def _():
            @pl.loop(0, 3)
            def _(q):
                work(near(q, r))

        @pl.when((r >= 3) & (r < 7))
        def _():
            work(common(r - 3))

        @pl.when((r >= 1) & (r <= SHARED))
        def _():
            work(chunk(2, r - 1))

    start_y(0, chunk(0, 0))
    start_y(1, chunk(0, 1))
    pass_on(0, chunk(0, 0))
    start_a(0)
    start_a(1)
    pass_on(1, chunk(0, 1))
    start_y(2, chunk(0, 2))
    first(0)
    first(1)
    start_a(2)
    start_a(3)
    own_a.wait()
    own_w.wait()
    own_res.wait()

    def multiply_near(r):
        @pl.loop(0, 3)
        def _(q):
            n = near(q, r)
            c_land(n, r, lax.rem(3 - q, 3)).wait_recv()
            multiply(n)

    @pl.loop(0, SHARED + 4)
    def _(r):
        @pl.when(r < SHARED)
        def _():
            for way in (0, 1):
                x_land(r, way).wait_recv()
                f_copy(r, way).start()
                c_copy(r, 1 + way).start()

        @pl.when(r + 2 < SHARED)
        def _():
            pass_on(r + 2, chunk(0, r + 2))

        @pl.when(r + 3 < SHARED)
        def _():
            start_y(r + 3, chunk(0, r + 3))

        @pl.when(r < 4)
        def _():
            start_y(SHARED + r, common(r))

        @pl.when(r + 2 < SHARED)
        def _():
            first(r + 2)

        @pl.when((r >= 1) & (r < 5))
        def _():
            pass_on(SHARED + r - 1, common(r - 1))

        @pl.when((r >= 2) & (r < 6))
        def _():
            for way in (0, 1):
                g_copy(SHARED + r - 2, common(r - 2), way).wait_recv()
            v_copy(r - 2).start()

        @pl.when(r == 1)
        def _():
            for g in range(4):
                for k in range(3):
                    part = ag.at[k + 1, g]
                    remote(part, part, a_s.at[g, k], a_r.at[g, k], at(z, y + 1, x, c)).wait_recv()
            multiply_near(0)

        @pl.when(r >= 2)
        def _():
            step(combine, r - 1)

        @pl.when((r >= 1) & (r < SHARED))
        def _():
            multiply_near(r)

        @pl.when((r >= 3) & (r < 7))
        def _():
            v_land(r - 3).wait_recv()
            multiply(common(r - 3))

        @pl.when((r >= 1) & (r <= SHARED))
        def _():
            for way in (0, 1):
                f_land(r - 1, way).wait_recv()
            c_copy(r - 1, 3).start()
            c_land(chunk(2, r - 1), r - 1, 3).wait_recv()
            multiply(chunk(2, r - 1))

        @pl.when(r == 2)
        def _():
            @pl.loop(0, 3)
            def _(q):
                combine(near(q, 0))

        @pl.when(r >= 3)
        def _():
            step(finish, r - 3)

    for g in range(4):
        for e in (1, 2, 3):
            a_copy(g, e).wait_send()

    @pl.loop(0, SHARED)
    def _(r):
        for way in (0, 1):
            y_copy(r, chunk(0, r), way).wait_send()
            g_copy(r, chunk(0, r), way).wait_send()
            x_copy(r, way).wait_send()
            f_copy(r, way).wait_send()
        for q in range(4):
            c_copy(r, q).wait_send()

    @pl.loop(0, 4)
    def _(u):
        for way in (0, 1):
            y_copy(SHARED + u, common(u), way).wait_send()
            g_copy(SHARED + u, common(u), way).wait_send()
        v_copy(u).wait_send()

    @pl.loop(0, 4 * ROUNDS)
    def _(n):
        for way in (0, 1):
            h_copy(n, way).wait_send()
            z_copy(n, way).wait_send()


def project(attn_out, w_out, residual):
    dma = pltpu.SemaphoreType.DMA
    anywhere = pl.BlockSpec(memory_space=pl.ANY)
    return pl.pallas_call(
        project_kernel,
        name="project",
        out_shape=jax.ShapeDtypeStruct((128, 7168), jnp.bfloat16),
        in_specs=[anywhere] * 3,
        out_specs=pl.BlockSpec(memory_space=VMEM),
        scratch_shapes=[
            VMEM((4, 4, 128, 512), jnp.bfloat16),
            VMEM((512, 7168), jnp.bfloat16),
            VMEM((28, 3, 512, CH), jnp.bfloat16),
            VMEM((28, 4, 128, CH), jnp.bfloat16),
            VMEM((28, 2, 64, CH), jnp.bfloat16),
            VMEM((28, 2, 128, CH), jnp.bfloat16),
            VMEM((128, 7168), jnp.bfloat16),
            dma((3,)), dma((4, 3)), dma((4, 3)), dma((10, 2)), dma((10, 2)), dma((10, 2)), dma((10, 2)),
            dma((4,)), dma((4,)), dma((6, 2)), dma((6, 2)), dma((6, 2)), dma((6, 2)), dma((6, 4)), dma((6, 4)),
            dma((28, 2)), dma((28, 2)), dma((28, 2)), dma((28, 2)),
        ],
        compiler_params=pltpu.CompilerParams(
            collective_id=0, has_side_effects=True, vmem_limit_bytes=58 * 1024 * 1024
        ),
    )(attn_out.reshape(4, 4, 128, 512), w_out, residual)


LANE = 896
GROUPS = ((0, 0), (1, 1), (2, 3), (3, 2))


def moe_kernel(
    hid_ref, gain_ref, rout_ref, bias_ref, cho_ref, wg_ref, wu_ref, wd_ref,
    moe_ref, load_ref, next_ref,
    wg, wu, wd, rt, normed, snd, land, rows, ybuf, r1, sbuf, r2, rsend, ret, cnt, cnt_tp, cnt_ep,
    loc, d_s, d_r, ax_s, ax_r, ac_s, ac_r, k_s, k_r, l_s, l_r, rt_s, rt_r, rs_s, rs_r,
    p_s, p_r, q_s, q_r, b_s, b_r,
):
    z, y, x, c = place()
    tp = z * 4 + y
    ep = x * 2 + c
    sib = at(z, y, x, c + 1)
    width = hid_ref.shape[1]
    half = pl.ds(pl.multiple_of(c * (width // 2), width // 2), width // 2)
    loads = [pltpu.make_async_copy(s, d, loc.at[i]) for i, (s, d) in enumerate(((wg_ref, wg), (wu_ref, wu), (wd_ref, wd)))]
    for load in loads:
        load.start()
    tp_peers = [(dz, dy) for dz in (0, 1, 3, 2) for dy in (1, 3, 2, 0) if (dz, dy) != (0, 0)]
    ep_peers = [(dx, dc) for dx in (0, 1, 3, 2) for dc in (0, 1) if (dx, dc) != (0, 0)]

    def tp_at(dz, dy):
        return ring(z + dz) * 4 + ring(y + dy)

    def ep_at(dx, dc):
        return ring(x + dx) * 2 + lax.rem(c + dc, 2)

    barrier = pltpu.get_barrier_semaphore()
    for p in tp_peers:
        pl.semaphore_signal(barrier, inc=1, device_id=(tp_at(*p), ep), device_id_type=MESH)
    for p in ep_peers:
        pl.semaphore_signal(barrier, inc=1, device_id=(tp, ep_at(*p)), device_id_type=MESH)

    def cut(j):
        return slice(j * LANE, (j + 1) * LANE)

    ssq = jnp.zeros((128, 1), jnp.float32)
    for j in range(8):
        h = hid_ref[:, cut(j)].astype(jnp.float32)
        ssq += jnp.sum(h * h, axis=1, keepdims=True)
    scale = lax.rsqrt(ssq / width + norm_eps)
    for j in range(8):
        h = hid_ref[:, cut(j)].astype(jnp.float32)
        normed[:, cut(j)] = (h * scale * gain_ref[:, cut(j)].astype(jnp.float32)).astype(jnp.bfloat16)

    row = lax.broadcasted_iota(jnp.int32, (256, 128), 0)
    lane = lax.broadcasted_iota(jnp.int32, (256, 128), 1)
    expert = row // 16
    member = jnp.zeros((256, 128), jnp.float32)
    named = jnp.zeros((256, 128), jnp.float32)
    for k in range(TOP):
        ck = cho_ref[k : k + 1, :]
        member += jnp.where(ck == expert, 1.0, 0.0)
        named += jnp.where(ck == row, 1.0, 0.0)
    before = jnp.where(row[:128] < lane[:128], 1.0, 0.0).astype(jnp.bfloat16)
    rank = jnp.dot(member.astype(jnp.bfloat16), before, preferred_element_type=jnp.float32)
    slot = ((row // 8) % 2).astype(jnp.float32)
    pick = jnp.where(rank == slot, member, 0.0)
    feature = row % 8
    outgoing = jnp.zeros((256, LANE), jnp.float32)
    for j in range(8):
        pj = jnp.where(feature == j, pick, 0.0).astype(jnp.bfloat16)
        outgoing += jnp.dot(pj, normed[:, cut(j)], preferred_element_type=jnp.float32)
    snd[...] = outgoing.astype(jnp.bfloat16).reshape(16, 16, LANE)
    contract_last = (((1,), (1,)), ((), ()))
    cnt[...] = lax.dot_general(
        jnp.ones((8, 128), jnp.bfloat16), named.astype(jnp.bfloat16), contract_last, preferred_element_type=jnp.float32
    )
    pl.semaphore_wait(barrier, len(tp_peers) + len(ep_peers))

    def d_copy(p):
        peer = tp_at(*p)
        return remote(snd.at[peer], land.at[ep, tp], d_s.at[peer], d_r.at[tp], (peer, ep))

    own_rows = pltpu.make_async_copy(snd.at[tp], land.at[ep, tp], loc.at[3])
    own_rows.start()
    for p in tp_peers:
        d_copy(p).start()

    def k_copy(p):
        peer = tp_at(*p)
        return remote(cnt, cnt_tp.at[tp], k_s.at[peer], k_r.at[tp], (peer, ep))

    for p in tp_peers:
        k_copy(p).start()

    def group(dz):
        return pl.ds(pl.multiple_of(ring(z + dz) * 4, 4), 4)

    def x_copy(g, dz, e):
        part = land.at[ep, group(dz)]
        return remote(part, part, ax_s.at[g, e - 1], ax_r.at[g, 3 - e], (tp, ep_at(e, 0)))

    def x_land(g, dz, k):
        part = land.at[ep_at(k + 1, 0), group(dz)]
        return remote(part, part, ax_s.at[g, k], ax_r.at[g, k], (tp, ep_at(1, 0)))

    def c_copy(g, dz, q):
        part = land.at[ep_at(q, 0), group(dz)]
        return remote(part, part, ac_s.at[g, q], ac_r.at[g, q], sib)

    def c_land(g, dz, q):
        part = land.at[ep_at(q, 1), group(dz)]
        return remote(part, part, ac_s.at[g, q], ac_r.at[g, q], sib)

    def d_land(p):
        src = tp_at(*p)
        return remote(snd.at[src], land.at[ep, src], d_s.at[src], d_r.at[src], (src, ep))

    for g, dz in GROUPS:
        for p in tp_peers:
            if p[0] == dz:
                d_land(p).wait_recv()
        if dz == 0:
            own_rows.wait()
        for e in (1, 3, 2):
            x_copy(g, dz, e).start()
        c_copy(g, dz, 0).start()

    def rt_copy(p):
        peer = tp_at(*p)
        return remote(rout_ref.at[:, half], rt.at[tp, :, half], rt_s.at[peer], rt_r.at[tp], (peer, ep))

    own_rt = pltpu.make_async_copy(rout_ref.at[:, half], rt.at[tp, :, half], loc.at[4])
    own_rt.start()
    for p in tp_peers:
        rt_copy(p).start()

    for p in tp_peers:
        src = tp_at(*p)
        remote(cnt, cnt_tp.at[src], k_s.at[src], k_r.at[src], (src, ep)).wait_recv()
    cnt_tp[tp] = cnt[...]
    part_sum = cnt_tp[0]
    for i in range(1, 16):
        part_sum += cnt_tp[i]
    cnt_ep[ep] = part_sum

    def l_copy(p):
        peer = ep_at(*p)
        return remote(cnt_ep.at[ep], cnt_ep.at[ep], l_s.at[peer], l_r.at[ep], (tp, peer))

    for p in ep_peers:
        l_copy(p).start()

    for g, dz in GROUPS:
        for k in (0, 2, 1):
            x_land(g, dz, k).wait_recv()
            c_copy(g, dz, k + 1).start()
    for g, dz in GROUPS:
        for q in range(4):
            c_land(g, dz, q).wait_recv()
    out_row = lax.broadcasted_iota(jnp.int32, (128, 128), 0)
    in_row = lax.broadcasted_iota(jnp.int32, (128, 128), 1)
    source = ((out_row % 16) // 2) * 16 + (out_row % 2) * 8 + out_row // 16
    perm = jnp.where(in_row == source, 1.0, 0.0).astype(jnp.bfloat16)

    @pl.loop(0, 16)
    def _(i):
        group_of, part = lax.div(i, 2), lax.rem(i, 2)
        block = land[group_of, pl.ds(pl.multiple_of(part * 8, 8), 8)].reshape(128, LANE)
        turned = jnp.dot(perm, block, preferred_element_type=jnp.float32).astype(jnp.bfloat16)
        rows[:, pl.ds(pl.multiple_of(i * 16, 16), 16), :] = turned.reshape(8, 16, LANE)

    for load in loads:
        load.wait()
    gate_val = jnp.zeros((256, 256), jnp.float32)
    up_val = jnp.zeros((256, 256), jnp.float32)
    for j in range(8):
        gate_val += jnp.dot(rows[j], wg[cut(j), :], preferred_element_type=jnp.float32)
        up_val += jnp.dot(rows[j], wu[cut(j), :], preferred_element_type=jnp.float32)
    active = (gate_val / (1.0 + jnp.exp(-gate_val)) * up_val).astype(jnp.bfloat16)

    def p_copy(n):
        return remote(ybuf.at[n, :, 1 - c], r1.at[n], p_s.at[n], p_r.at[n], sib)

    def q_copy(n, e):
        return remote(sbuf.at[n, ring(x + e)], r2.at[n, 3 - e], q_s.at[n, e - 1], q_r.at[n, 3 - e], (tp, ep_at(e, 0)))

    def q_land(n, k):
        return remote(r2.at[n, k], r2.at[n, k], q_s.at[n, k], q_r.at[n, k], (tp, ep_at(1, 0)))

    for n in range(4):
        part = jnp.dot(active, wd[:, n * 2 * LANE : (n + 1) * 2 * LANE], preferred_element_type=jnp.float32)
        ybuf[n] = part.astype(jnp.bfloat16).reshape(4, 2, 32, 2 * LANE)
        p_copy(n).start()
    for n in range(4):
        p_copy(n).wait_recv()
        for i in range(4):
            both = ybuf[n, i, c].astype(jnp.float32) + r1[n, i].astype(jnp.float32)
            sbuf[n, i] = both.astype(jnp.bfloat16)
        for e in (1, 3, 2):
            q_copy(n, e).start()

    for p in ep_peers:
        peer = ep_at(*p)
        remote(cnt_ep.at[peer], cnt_ep.at[peer], l_s.at[peer], l_r.at[peer], (tp, peer)).wait_recv()
    counts = cnt_ep[0]
    for i in range(1, 8):
        counts += cnt_ep[i]
    counts = counts[0:1]
    slots = 128.0 * 128.0 * TOP
    load_ref[...] = counts * 256.0 / slots
    gap = slots - counts * 256.0
    sign = jnp.where(gap > 0.0, 1.0, jnp.where(gap < 0.0, -1.0, 0.0))
    next_ref[...] = bias_ref[...] + bias_rate * sign

    for p in tp_peers:
        src = tp_at(*p)
        remote(rout_ref.at[:, half], rt.at[src, :, half], rt_s.at[src], rt_r.at[src], (src, ep)).wait_recv()
    own_rt.wait()
    mine = rt.at[:, :, half]
    rt_sib = remote(mine, mine, rs_s.at[0], rs_r.at[0], sib)
    rt_sib.start()
    other = rt.at[:, :, pl.ds(pl.multiple_of((1 - c) * (width // 2), width // 2), width // 2)]
    remote(other, other, rs_s.at[0], rs_r.at[0], sib).wait_recv()
    logits = jnp.zeros((256, 128), jnp.float32)
    for j in range(8):
        logits += lax.dot_general(
            rt[:, :, cut(j)].reshape(256, LANE), normed[:, cut(j)], contract_last, preferred_element_type=jnp.float32
        )
    scores = 1.0 / (1.0 + jnp.exp(-logits))
    chosen = []
    for k in range(TOP):
        hit = cho_ref[k : k + 1, :] == row
        chosen.append(jnp.sum(jnp.where(hit, scores, 0.0), axis=0, keepdims=True))
    norm_by = chosen[0]
    for k in range(1, TOP):
        norm_by = norm_by + chosen[k]
    weight = jnp.zeros((256, 128), jnp.float32)
    for k in range(TOP):
        weight += jnp.where(cho_ref[k : k + 1, :] == expert, route_scale * chosen[k] / norm_by, 0.0)
    coeff = jnp.where(pick > 0.0, weight, 0.0).T
    lane_cut = lax.broadcasted_iota(jnp.int32, (128, 256), 1) % 8

    back_row = lax.broadcasted_iota(jnp.int32, (256, 32), 0)
    back_col = lax.broadcasted_iota(jnp.int32, (256, 32), 1)
    returned = jnp.zeros((256, LANE), jnp.float32)
    for n in range(4):
        for k in (0, 2, 1):
            q_land(n, k).wait_recv()
        total = sbuf[n, x].astype(jnp.float32)
        for k in range(3):
            total += r2[n, k].astype(jnp.float32)
        total = total.astype(jnp.bfloat16)
        for i in range(2):
            turn = jnp.where((back_row // 8 == back_col) & (back_row % 8 == 2 * n + i), 1.0, 0.0).astype(jnp.bfloat16)
            returned += jnp.dot(turn, total[:, cut(i)], preferred_element_type=jnp.float32)
    rsend[...] = returned.astype(jnp.bfloat16).reshape(16, 16, LANE)

    def b_copy(p):
        peer = tp_at(*p)
        return remote(rsend.at[peer], ret.at[tp], b_s.at[peer], b_r.at[tp], (peer, ep))

    own_back = pltpu.make_async_copy(rsend.at[tp], ret.at[tp], loc.at[5])
    own_back.start()
    for p in tp_peers:
        b_copy(p).start()
    high = coeff.astype(jnp.bfloat16)
    low = (coeff - high.astype(jnp.float32)).astype(jnp.bfloat16)
    own_back.wait()
    for p in tp_peers:
        src = tp_at(*p)
        remote(rsend.at[src], ret.at[src], b_s.at[src], b_r.at[src], (src, ep)).wait_recv()
    back = ret[...].reshape(256, LANE)
    for j in range(8):
        mixed = jnp.dot(jnp.where(lane_cut == j, high, 0.0).astype(jnp.bfloat16), back, preferred_element_type=jnp.float32)
        mixed += jnp.dot(jnp.where(lane_cut == j, low, 0.0).astype(jnp.bfloat16), back, preferred_element_type=jnp.float32)
        moe_ref[:, cut(j)] = mixed.astype(jnp.bfloat16)

    for p in tp_peers:
        d_copy(p).wait_send()
        k_copy(p).wait_send()
        rt_copy(p).wait_send()
        b_copy(p).wait_send()
    for p in ep_peers:
        l_copy(p).wait_send()
    rt_sib.wait_send()
    for g, dz in GROUPS:
        for e in (1, 2, 3):
            x_copy(g, dz, e).wait_send()
        for q in range(4):
            c_copy(g, dz, q).wait_send()
    for n in range(4):
        p_copy(n).wait_send()
        for e in (1, 2, 3):
            q_copy(n, e).wait_send()


def experts(hidden_out, norm_gain, router, router_bias, choices, w_gate, w_up, w_down):
    dma = pltpu.SemaphoreType.DMA
    bf16, f32 = jnp.bfloat16, jnp.float32
    vmem = pl.BlockSpec(memory_space=VMEM)
    anywhere = pl.BlockSpec(memory_space=pl.ANY)
    moe_out, load, bias_next = pl.pallas_call(
        moe_kernel,
        name="experts",
        out_shape=(
            jax.ShapeDtypeStruct((128, 7168), bf16),
            jax.ShapeDtypeStruct((1, 256), f32),
            jax.ShapeDtypeStruct((1, 256), f32),
        ),
        in_specs=[vmem] * 5 + [anywhere] * 3,
        out_specs=(vmem,) * 3,
        scratch_shapes=[
            VMEM((7168, 256), bf16), VMEM((7168, 256), bf16), VMEM((256, 7168), bf16),
            VMEM((16, 16, 7168), bf16), VMEM((128, 7168), bf16), VMEM((16, 16, LANE), bf16),
            VMEM((8, 16, 16, LANE), bf16), VMEM((8, 256, LANE), bf16),
            VMEM((4, 4, 2, 32, 2 * LANE), bf16), VMEM((4, 4, 32, 2 * LANE), bf16),
            VMEM((4, 4, 32, 2 * LANE), bf16), VMEM((4, 3, 32, 2 * LANE), bf16),
            VMEM((16, 16, LANE), bf16), VMEM((16, 16, LANE), bf16),
            VMEM((8, 256), f32), VMEM((16, 8, 256), f32), VMEM((8, 8, 256), f32),
            dma((6,)), dma((16,)), dma((16,)), dma((4, 3)), dma((4, 3)), dma((4, 4)), dma((4, 4)),
            dma((16,)), dma((16,)), dma((8,)), dma((8,)), dma((16,)), dma((16,)), dma((1,)), dma((1,)),
            dma((4,)), dma((4,)), dma((4, 3)), dma((4, 3)), dma((16,)), dma((16,)),
        ],
        compiler_params=pltpu.CompilerParams(
            collective_id=1, has_side_effects=True, vmem_limit_bytes=56 * 1024 * 1024
        ),
    )(
        hidden_out, norm_gain.reshape(1, -1), router.T, router_bias.reshape(1, -1), choices.T,
        w_gate[0], w_up[0], w_down[0],
    )
    return moe_out, load.reshape(-1), bias_next.reshape(-1)


def on_device(
    attn_out, residual, w_out, norm_gain, router, router_bias, choices, w_gate, w_up, w_down
):
    hidden_out = project(attn_out, w_out, residual)
    moe_out, load, bias_next = experts(
        hidden_out, norm_gain, router, router_bias, choices, w_gate, w_up, w_down
    )
    return (hidden_out, moe_out, load, bias_next)


def solution(mesh):
    placed = (
        P("ep", "tp"),
        P(("ep", "tp"), None),
        P("tp", None),
        P(),
        P(None, "tp"),
        P(),
        P(("ep", "tp"), None),
        P("tp", None, "ep"),
        P("tp", None, "ep"),
        P("tp", "ep", None),
    )
    return jax.shard_map(
        on_device,
        mesh=mesh,
        in_specs=placed,
        out_specs=(P(("ep", "tp"), None), P(("ep", "tp"), None), P(), P()),
        check_vma=False,
    )
```

```python
import jax
import jax.numpy as jnp
from jax import lax
from jax.experimental import pallas as pl
from jax.experimental.pallas import tpu as pltpu
from jax.sharding import PartitionSpec as P

TOP = 8


norm_eps = 1e-06
route_scale = 2.5
bias_rate = 0.001


MESH = pl.DeviceIdType.MESH
VMEM = pltpu.VMEM
ROUNDS = 7
SHARED = 6
CH = 256


def ring(i):
    return lax.rem(i + 8, 4)


def place():
    tp = lax.axis_index("tp")
    ep = lax.axis_index("ep")
    return lax.div(tp, 4), lax.rem(tp, 4), lax.div(ep, 2), lax.rem(ep, 2)


def at(z, y, x, c):
    return (ring(z) * 4 + ring(y), ring(x) * 2 + lax.rem(c, 2))


def greet(peers):
    barrier = pltpu.get_barrier_semaphore()
    for peer in peers:
        pl.semaphore_signal(barrier, inc=1, device_id=peer, device_id_type=MESH)
    pl.semaphore_wait(barrier, len(peers))


def remote(src, dst, send, recv, peer):
    return pltpu.make_async_remote_copy(
        src_ref=src, dst_ref=dst, send_sem=send, recv_sem=recv, device_id=peer, device_id_type=MESH
    )


def project_kernel(
    a_ref, w_ref, res_ref, out_ref,
    ag, wown, wbuf, pbuf, half_in, full_in, resv,
    loc, a_s, a_r, y_s, y_r, g_s, g_r, v_s, v_r, x_s, x_r, f_s, f_r, c_s, c_r, h_s, h_r, z_s, z_r,
):
    z, y, x, c = place()
    half = pl.multiple_of(c * 256, 256)
    own_a = pltpu.make_async_copy(a_ref.at[:, y], ag.at[0], loc.at[0])
    own_w = pltpu.make_async_copy(w_ref, wown, loc.at[1])
    own_res = pltpu.make_async_copy(res_ref, resv, loc.at[2])
    own_a.start()
    own_w.start()
    own_res.start()
    greet(
        [at(z, y + e, x, c) for e in (1, 2, 3)]
        + [at(z + e, y, x, c) for e in (1, 2, 3)]
        + [at(z, y, x + 1, c), at(z, y, x - 1, c), at(z, y, x, c + 1)]
    )
    sib = at(z, y, x, c + 1)

    def chunk(dx, r):
        return ring(x + dx) * ROUNDS + r

    def y_copy(i, n, way):
        cols = pl.ds(pl.multiple_of(n * CH, CH), CH)
        return remote(
            w_ref.at[pl.ds(half, 256), cols], wbuf.at[n, 2 - 2 * way, pl.ds(half, 256), :],
            y_s.at[i, way], y_r.at[i, way], at(z, y + 1 - 2 * way, x, c),
        )

    def y_land(i, n, way):
        part = wbuf.at[n, 2 - 2 * way, pl.ds(half, 256), :]
        return remote(part, part, y_s.at[i, way], y_r.at[i, way], at(z, y + 1, x, c))

    def g_copy(i, n, way):
        rows = pl.ds(pl.multiple_of(half + 128 * way, 128), 128)
        return remote(
            wbuf.at[n, 2 - 2 * way, rows, :], wbuf.at[n, 1, rows, :],
            g_s.at[i, way], g_r.at[i, way], at(z, y + 1 - 2 * way, x, c),
        )

    def common(u):
        return u * ROUNDS + SHARED

    def v_copy(u):
        part = wbuf.at[common(u), :, pl.ds(half, 256), :]
        return remote(part, part, v_s.at[u], v_r.at[u], sib)

    def v_land(u):
        part = wbuf.at[common(u), :, pl.ds(pl.multiple_of(256 - half, 256), 256), :]
        return remote(part, part, v_s.at[u], v_r.at[u], sib)

    def a_copy(g, e):
        return remote(a_ref.at[g, ring(y + e)], ag.at[4 - e, g], a_s.at[g, e - 1], a_r.at[g, 3 - e], at(z, y + e, x, c))

    def x_copy(r, way):
        part = wbuf.at[chunk(0, r), :, pl.ds(half, 256), :]
        return remote(part, part, x_s.at[r, way], x_r.at[r, way], at(z, y, x + 1 - 2 * way, c))

    def x_land(r, way):
        part = wbuf.at[chunk(2 * way - 1, r), :, pl.ds(half, 256), :]
        return remote(part, part, x_s.at[r, way], x_r.at[r, way], at(z, y, x + 1 - 2 * way, c))

    def f_part(dx, r, way):
        return wbuf.at[chunk(dx, r), :, pl.ds(pl.multiple_of(half + 128 * way, 128), 128), :]

    def f_copy(r, way):
        part = f_part(2 * way - 1, r, way)
        return remote(part, part, f_s.at[r, way], f_r.at[r, way], at(z, y, x + 1 - 2 * way, c))

    def f_land(r, way):
        part = f_part(2, r, way)
        return remote(part, part, f_s.at[r, way], f_r.at[r, way], at(z, y, x + 1 - 2 * way, c))

    def hop(q):
        return (0, 3, 1, 2)[q]

    def c_copy(r, q):
        part = wbuf.at[chunk(hop(q), r), :, pl.ds(half, 256), :]
        return remote(part, part, c_s.at[r, q], c_r.at[r, q], sib)

    def c_land(n, r, q):
        other = pl.multiple_of(256 - half, 256)
        part = wbuf.at[n, :, pl.ds(other, 256), :]
        return remote(part, part, c_s.at[r, q], c_r.at[r, q], sib)

    def halves(way):
        return pl.ds(64 * way, 64)

    def h_copy(n, way):
        return remote(
            pbuf.at[n, ring(z + 2), halves(way)], half_in.at[n, way],
            h_s.at[n, way], h_r.at[n, way], at(z + 1 - 2 * way, y, x, c),
        )

    def z_copy(n, way):
        to = z + 1 - 2 * way
        return remote(pbuf.at[n, ring(to)], full_in.at[n, way], z_s.at[n, way], z_r.at[n, way], at(to, y, x, c))

    def start_y(i, n):
        for way in (0, 1):
            y_copy(i, n, way).start()

    def start_a(g):
        for e in (2, 1, 3):
            a_copy(g, e).start()

    def pass_on(i, n):
        for way in (0, 1):
            y_land(i, n, way).wait_recv()
            g_copy(i, n, way).start()

    def first(r):
        for way in (0, 1):
            g_copy(r, chunk(0, r), way).wait_recv()
        x_copy(r, 0).start()
        x_copy(r, 1).start()
        c_copy(r, 0).start()

    def multiply(n):
        cols = pl.ds(pl.multiple_of(n * CH, CH), CH)
        total = jnp.dot(ag[0].reshape(512, 512), wown[:, cols], preferred_element_type=jnp.float32)
        for k in range(3):
            total += jnp.dot(ag[k + 1].reshape(512, 512), wbuf[n, k], preferred_element_type=jnp.float32)
        pbuf[n] = total.astype(jnp.bfloat16).reshape(4, 128, CH)
        for way in (0, 1):
            h_copy(n, way).start()

    def combine(n):
        for way in (0, 1):
            to = ring(z + 1 - 2 * way)
            h_copy(n, way).wait_recv()
            both = pbuf[n, to, halves(way)].astype(jnp.float32) + half_in[n, way].astype(jnp.float32)
            pbuf[n, to, halves(way)] = both.astype(jnp.bfloat16)
            z_copy(n, way).start()

    def finish(n):
        cols = pl.ds(pl.multiple_of(n * CH, CH), CH)
        total = pbuf[n, z].astype(jnp.float32)
        for way in (0, 1):
            z_copy(n, way).wait_recv()
            total += full_in[n, way].astype(jnp.float32)
        out_ref[:, cols] = (resv[:, cols].astype(jnp.float32) + total).astype(jnp.bfloat16)

    def near(q, r):
        return chunk(q + lax.div(q, 2), r)

    def step(work, r):
        @pl.when((r >= 0) & (r < SHARED))
        def _():
            @pl.loop(0, 3)
            def _(q):
                work(near(q, r))

        @pl.when((r >= 3) & (r < 7))
        def _():
            work(common(r - 3))

        @pl.when((r >= 1) & (r <= SHARED))
        def _():
            work(chunk(2, r - 1))

    start_y(0, chunk(0, 0))
    start_y(1, chunk(0, 1))
    pass_on(0, chunk(0, 0))
    start_a(0)
    start_a(1)
    pass_on(1, chunk(0, 1))
    start_y(2, chunk(0, 2))
    first(0)
    first(1)
    start_a(2)
    start_a(3)
    own_a.wait()
    own_w.wait()
    own_res.wait()

    def multiply_near(r):
        @pl.loop(0, 3)
        def _(q):
            n = near(q, r)
            c_land(n, r, lax.rem(3 - q, 3)).wait_recv()
            multiply(n)

    @pl.loop(0, SHARED + 4)
    def _(r):
        @pl.when(r < SHARED)
        def _():
            for way in (0, 1):
                x_land(r, way).wait_recv()
                f_copy(r, way).start()
                c_copy(r, 1 + way).start()

        @pl.when(r + 2 < SHARED)
        def _():
            pass_on(r + 2, chunk(0, r + 2))

        @pl.when(r + 3 < SHARED)
        def _():
            start_y(r + 3, chunk(0, r + 3))

        @pl.when(r < 4)
        def _():
            start_y(SHARED + r, common(r))

        @pl.when(r + 2 < SHARED)
        def _():
            first(r + 2)

        @pl.when((r >= 1) & (r < 5))
        def _():
            pass_on(SHARED + r - 1, common(r - 1))

        @pl.when((r >= 2) & (r < 6))
        def _():
            for way in (0, 1):
                g_copy(SHARED + r - 2, common(r - 2), way).wait_recv()
            v_copy(r - 2).start()

        @pl.when(r == 1)
        def _():
            for g in range(4):
                for k in range(3):
                    part = ag.at[k + 1, g]
                    remote(part, part, a_s.at[g, k], a_r.at[g, k], at(z, y + 1, x, c)).wait_recv()
            multiply_near(0)

        @pl.when(r >= 2)
        def _():
            step(combine, r - 1)

        @pl.when((r >= 1) & (r < SHARED))
        def _():
            multiply_near(r)

        @pl.when((r >= 3) & (r < 7))
        def _():
            v_land(r - 3).wait_recv()
            multiply(common(r - 3))

        @pl.when((r >= 1) & (r <= SHARED))
        def _():
            for way in (0, 1):
                f_land(r - 1, way).wait_recv()
            c_copy(r - 1, 3).start()
            c_land(chunk(2, r - 1), r - 1, 3).wait_recv()
            multiply(chunk(2, r - 1))

        @pl.when(r == 2)
        def _():
            @pl.loop(0, 3)
            def _(q):
                combine(near(q, 0))

        @pl.when(r >= 3)
        def _():
            step(finish, r - 3)

    for g in range(4):
        for e in (1, 2, 3):
            a_copy(g, e).wait_send()

    @pl.loop(0, SHARED)
    def _(r):
        for way in (0, 1):
            y_copy(r, chunk(0, r), way).wait_send()
            g_copy(r, chunk(0, r), way).wait_send()
            x_copy(r, way).wait_send()
            f_copy(r, way).wait_send()
        for q in range(4):
            c_copy(r, q).wait_send()

    @pl.loop(0, 4)
    def _(u):
        for way in (0, 1):
            y_copy(SHARED + u, common(u), way).wait_send()
            g_copy(SHARED + u, common(u), way).wait_send()
        v_copy(u).wait_send()

    @pl.loop(0, 4 * ROUNDS)
    def _(n):
        for way in (0, 1):
            h_copy(n, way).wait_send()
            z_copy(n, way).wait_send()


def project(attn_out, w_out, residual):
    dma = pltpu.SemaphoreType.DMA
    anywhere = pl.BlockSpec(memory_space=pl.ANY)
    return pl.pallas_call(
        project_kernel,
        name="project",
        out_shape=jax.ShapeDtypeStruct((128, 7168), jnp.bfloat16),
        in_specs=[anywhere] * 3,
        out_specs=pl.BlockSpec(memory_space=VMEM),
        scratch_shapes=[
            VMEM((4, 4, 128, 512), jnp.bfloat16),
            VMEM((512, 7168), jnp.bfloat16),
            VMEM((28, 3, 512, CH), jnp.bfloat16),
            VMEM((28, 4, 128, CH), jnp.bfloat16),
            VMEM((28, 2, 64, CH), jnp.bfloat16),
            VMEM((28, 2, 128, CH), jnp.bfloat16),
            VMEM((128, 7168), jnp.bfloat16),
            dma((3,)), dma((4, 3)), dma((4, 3)), dma((10, 2)), dma((10, 2)), dma((10, 2)), dma((10, 2)),
            dma((4,)), dma((4,)), dma((6, 2)), dma((6, 2)), dma((6, 2)), dma((6, 2)), dma((6, 4)), dma((6, 4)),
            dma((28, 2)), dma((28, 2)), dma((28, 2)), dma((28, 2)),
        ],
        compiler_params=pltpu.CompilerParams(
            collective_id=0, has_side_effects=True, vmem_limit_bytes=58 * 1024 * 1024
        ),
    )(attn_out.reshape(4, 4, 128, 512), w_out, residual)


LANE = 896
GROUPS = ((0, 0), (1, 1), (2, 3), (3, 2))


def moe_kernel(
    hid_ref, gain_ref, rout_ref, bias_ref, cho_ref, wg_ref, wu_ref, wd_ref,
    moe_ref, load_ref, next_ref,
    wg, wu, wd, rt, normed, gain, snd, land, rows, ybuf, r1, sbuf, half_in, full_in, rsend, ret, cnt, cnt_tp, cnt_ep,
    loc, d_s, d_r, ax_s, ax_r, af_s, af_r, ac_s, ac_r, k_s, k_r, l_s, l_r, rt_s, rt_r, rs_s, rs_r,
    p_s, p_r, h_s, h_r, q_s, q_r, b_s, b_r,
):
    z, y, x, c = place()
    tp = z * 4 + y
    ep = x * 2 + c
    sib = at(z, y, x, c + 1)
    width = hid_ref.shape[1]
    half = pl.ds(pl.multiple_of(c * (width // 2), width // 2), width // 2)
    loads = [pltpu.make_async_copy(s, d, loc.at[i]) for i, (s, d) in enumerate(((wg_ref, wg), (wu_ref, wu), (wd_ref, wd)))]
    for load in loads:
        load.start()
    tp_peers = [(dz, dy) for dz in (0, 1, 3, 2) for dy in (1, 3, 2, 0) if (dz, dy) != (0, 0)]
    ep_peers = [(dx, dc) for dx in (0, 1, 3, 2) for dc in (0, 1) if (dx, dc) != (0, 0)]

    def tp_at(dz, dy):
        return ring(z + dz) * 4 + ring(y + dy)

    def ep_at(dx, dc):
        return ring(x + dx) * 2 + lax.rem(c + dc, 2)

    barrier = pltpu.get_barrier_semaphore()
    for p in tp_peers:
        pl.semaphore_signal(barrier, inc=1, device_id=(tp_at(*p), ep), device_id_type=MESH)
    for p in ep_peers:
        pl.semaphore_signal(barrier, inc=1, device_id=(tp, ep_at(*p)), device_id_type=MESH)

    def cut(j):
        return slice(j * LANE, (j + 1) * LANE)

    row = lax.broadcasted_iota(jnp.int32, (256, 128), 0)
    lane = lax.broadcasted_iota(jnp.int32, (256, 128), 1)
    expert = row // 16
    member = jnp.zeros((256, 128), jnp.float32)
    named = jnp.zeros((256, 128), jnp.float32)
    for k in range(TOP):
        ck = cho_ref[k : k + 1, :]
        member += jnp.where(ck == expert, 1.0, 0.0)
        named += jnp.where(ck == row, 1.0, 0.0)
    before = jnp.where(row[:128] < lane[:128], 1.0, 0.0).astype(jnp.bfloat16)
    rank = jnp.dot(member.astype(jnp.bfloat16), before, preferred_element_type=jnp.float32)
    slot = ((row // 8) % 2).astype(jnp.float32)
    pick = jnp.where(rank == slot, member, 0.0)
    feature = row % 8
    picked = jnp.zeros((256, LANE), jnp.float32)
    for j in range(8):
        pj = jnp.where(feature == j, pick, 0.0).astype(jnp.bfloat16)
        picked += jnp.dot(pj, hid_ref[:, cut(j)], preferred_element_type=jnp.float32)
    gains = gain_ref[...].astype(jnp.float32)
    for j in range(8):
        for i in range(7):
            gain[j : j + 1, i * 128 : (i + 1) * 128] = gains[j * 7 + i : j * 7 + i + 1, :]
    picked = picked.reshape(32, 8, LANE)
    ssq = jnp.sum(jnp.sum(picked * picked, axis=2, keepdims=True), axis=1, keepdims=True)
    outgoing = picked * lax.rsqrt(ssq / width + norm_eps) * gain[...][None]
    snd[...] = outgoing.astype(jnp.bfloat16).reshape(16, 16, LANE)
    contract_last = (((1,), (1,)), ((), ()))
    cnt[...] = lax.dot_general(
        jnp.ones((8, 128), jnp.bfloat16), named.astype(jnp.bfloat16), contract_last, preferred_element_type=jnp.float32
    )
    pl.semaphore_wait(barrier, len(tp_peers) + len(ep_peers))

    def d_copy(p):
        peer = tp_at(*p)
        return remote(snd.at[peer], land.at[ep, tp], d_s.at[peer], d_r.at[tp], (peer, ep))

    own_rows = pltpu.make_async_copy(snd.at[tp], land.at[ep, tp], loc.at[3])
    own_rows.start()
    for p in tp_peers:
        d_copy(p).start()

    def k_copy(p):
        peer = tp_at(*p)
        return remote(cnt, cnt_tp.at[tp], k_s.at[peer], k_r.at[tp], (peer, ep))

    for p in tp_peers:
        k_copy(p).start()

    def group(dz):
        return pl.ds(pl.multiple_of(ring(z + dz) * 4, 4), 4)

    def x_copy(g, dz, way):
        part = land.at[ep, group(dz)]
        return remote(part, part, ax_s.at[g, way], ax_r.at[g, way], (tp, ep_at(1 - 2 * way, 0)))

    def x_land(g, dz, way):
        part = land.at[ep_at(2 * way - 1, 0), group(dz)]
        return remote(part, part, ax_s.at[g, way], ax_r.at[g, way], (tp, ep_at(1, 0)))

    def f_rows(dx, dz, way):
        return land.at[ep_at(dx, 0), pl.ds(pl.multiple_of(ring(z + dz) * 4 + 2 * way, 2), 2)]

    def f_copy(g, dz, way):
        part = f_rows(2 * way - 1, dz, way)
        return remote(part, part, af_s.at[g, way], af_r.at[g, way], (tp, ep_at(1 - 2 * way, 0)))

    def f_land(g, dz, way):
        part = f_rows(2, dz, way)
        return remote(part, part, af_s.at[g, way], af_r.at[g, way], (tp, ep_at(1, 0)))

    def c_copy(g, dz, q):
        part = land.at[ep_at(q, 0), group(dz)]
        return remote(part, part, ac_s.at[g, q], ac_r.at[g, q], sib)

    def c_land(g, dz, q):
        part = land.at[ep_at(q, 1), group(dz)]
        return remote(part, part, ac_s.at[g, q], ac_r.at[g, q], sib)

    def d_land(p):
        src = tp_at(*p)
        return remote(snd.at[src], land.at[ep, src], d_s.at[src], d_r.at[src], (src, ep))

    for g, dz in GROUPS:
        for p in tp_peers:
            if p[0] == dz:
                d_land(p).wait_recv()
        if dz == 0:
            own_rows.wait()
        for way in (0, 1):
            x_copy(g, dz, way).start()
        c_copy(g, dz, 0).start()

    def rt_copy(p):
        peer = tp_at(*p)
        return remote(rout_ref.at[:, half], rt.at[tp, :, half], rt_s.at[peer], rt_r.at[tp], (peer, ep))

    own_rt = pltpu.make_async_copy(rout_ref.at[:, half], rt.at[tp, :, half], loc.at[4])
    own_rt.start()
    for p in tp_peers:
        rt_copy(p).start()

    for p in tp_peers:
        src = tp_at(*p)
        remote(cnt, cnt_tp.at[src], k_s.at[src], k_r.at[src], (src, ep)).wait_recv()
    cnt_tp[tp] = cnt[...]
    part_sum = cnt_tp[0]
    for i in range(1, 16):
        part_sum += cnt_tp[i]
    cnt_ep[ep] = part_sum

    def l_copy(p):
        peer = ep_at(*p)
        return remote(cnt_ep.at[ep], cnt_ep.at[ep], l_s.at[peer], l_r.at[ep], (tp, peer))

    for p in ep_peers:
        l_copy(p).start()

    out_row = lax.broadcasted_iota(jnp.int32, (128, 128), 0)
    in_row = lax.broadcasted_iota(jnp.int32, (128, 128), 1)
    source = ((out_row % 16) // 2) * 16 + (out_row % 2) * 8 + out_row // 16
    perm = jnp.where(in_row == source, 1.0, 0.0).astype(jnp.bfloat16)

    def turn_rows(group_of):
        for part in range(2):
            block = land[group_of, part * 8 : part * 8 + 8].reshape(128, LANE)
            turned = jnp.dot(perm, block, preferred_element_type=jnp.float32).astype(jnp.bfloat16)
            to = pl.ds(pl.multiple_of(group_of * 32 + part * 16, 16), 16)
            rows[:, to, :] = turned.reshape(8, 16, LANE)

    turn_rows(ep)
    for g, dz in GROUPS:
        for way in (0, 1):
            x_land(g, dz, way).wait_recv()
            f_copy(g, dz, way).start()
            c_copy(g, dz, 3 - 2 * way).start()
    for q in (0, 3, 1):
        if q:
            turn_rows(ep_at(q, 0))
        if q == 1:
            for g, dz in GROUPS:
                for way in (0, 1):
                    f_land(g, dz, way).wait_recv()
                c_copy(g, dz, 2).start()
        for g, dz in GROUPS:
            c_land(g, dz, q).wait_recv()
        turn_rows(ep_at(q, 1))
    turn_rows(ep_at(2, 0))
    for g, dz in GROUPS:
        c_land(g, dz, 2).wait_recv()
    turn_rows(ep_at(2, 1))

    for load in loads:
        load.wait()
    gate_val = jnp.zeros((256, 256), jnp.float32)
    up_val = jnp.zeros((256, 256), jnp.float32)
    for j in range(8):
        gate_val += jnp.dot(rows[j], wg[cut(j), :], preferred_element_type=jnp.float32)
        up_val += jnp.dot(rows[j], wu[cut(j), :], preferred_element_type=jnp.float32)
    active = (gate_val / (1.0 + jnp.exp(-gate_val)) * up_val).astype(jnp.bfloat16)

    def p_copy(n):
        return remote(ybuf.at[n, :, 1 - c], r1.at[n], p_s.at[n], p_r.at[n], sib)

    def h_copy(n, way):
        rows_of = pl.ds(16 * way, 16)
        return remote(
            sbuf.at[n, ring(x + 2), rows_of], half_in.at[n, way],
            h_s.at[n, way], h_r.at[n, way], (tp, ep_at(1 - 2 * way, 0)),
        )

    def q_copy(n, way):
        to = 1 - 2 * way
        return remote(
            sbuf.at[n, ring(x + to)], full_in.at[n, way], q_s.at[n, way], q_r.at[n, way], (tp, ep_at(to, 0))
        )

    def forward(n):
        for way in (0, 1):
            to = ring(x + 1 - 2 * way)
            h_copy(n, way).wait_recv()
            rows_of = slice(16 * way, 16 * way + 16)
            both = sbuf[n, to, rows_of].astype(jnp.float32) + half_in[n, way].astype(jnp.float32)
            sbuf[n, to, rows_of] = both.astype(jnp.bfloat16)
            q_copy(n, way).start()

    for n in range(4):
        part = jnp.dot(active, wd[:, n * 2 * LANE : (n + 1) * 2 * LANE], preferred_element_type=jnp.float32)
        ybuf[n] = part.astype(jnp.bfloat16).reshape(4, 2, 32, 2 * LANE)
        p_copy(n).start()
    for n in range(4):
        p_copy(n).wait_recv()
        for i in range(4):
            both = ybuf[n, i, c].astype(jnp.float32) + r1[n, i].astype(jnp.float32)
            sbuf[n, i] = both.astype(jnp.bfloat16)
        for way in (0, 1):
            h_copy(n, way).start()
        if n:
            forward(n - 1)
    forward(3)

    for p in ep_peers:
        peer = ep_at(*p)
        remote(cnt_ep.at[peer], cnt_ep.at[peer], l_s.at[peer], l_r.at[peer], (tp, peer)).wait_recv()
    counts = cnt_ep[0]
    for i in range(1, 8):
        counts += cnt_ep[i]
    counts = counts[0:1]
    slots = 128.0 * 128.0 * TOP
    load_ref[...] = counts * 256.0 / slots
    gap = slots - counts * 256.0
    sign = jnp.where(gap > 0.0, 1.0, jnp.where(gap < 0.0, -1.0, 0.0))
    next_ref[...] = bias_ref[...] + bias_rate * sign

    for p in tp_peers:
        src = tp_at(*p)
        remote(rout_ref.at[:, half], rt.at[src, :, half], rt_s.at[src], rt_r.at[src], (src, ep)).wait_recv()
    own_rt.wait()
    mine = rt.at[:, :, half]
    rt_sib = remote(mine, mine, rs_s.at[0], rs_r.at[0], sib)
    rt_sib.start()
    other = rt.at[:, :, pl.ds(pl.multiple_of((1 - c) * (width // 2), width // 2), width // 2)]
    ssq = jnp.zeros((128, 1), jnp.float32)
    for j in range(8):
        h = hid_ref[:, cut(j)].astype(jnp.float32)
        ssq += jnp.sum(h * h, axis=1, keepdims=True)
    scale = lax.rsqrt(ssq / width + norm_eps)
    for j in range(8):
        h = hid_ref[:, cut(j)].astype(jnp.float32)
        normed[:, cut(j)] = (h * scale * gain[j : j + 1, :]).astype(jnp.bfloat16)
    remote(other, other, rs_s.at[0], rs_r.at[0], sib).wait_recv()
    logits = jnp.zeros((256, 128), jnp.float32)
    for j in range(8):
        logits += lax.dot_general(
            rt[:, :, cut(j)].reshape(256, LANE), normed[:, cut(j)], contract_last, preferred_element_type=jnp.float32
        )
    scores = 1.0 / (1.0 + jnp.exp(-logits))
    chosen = []
    for k in range(TOP):
        hit = cho_ref[k : k + 1, :] == row
        chosen.append(jnp.sum(jnp.where(hit, scores, 0.0), axis=0, keepdims=True))
    norm_by = chosen[0]
    for k in range(1, TOP):
        norm_by = norm_by + chosen[k]
    weight = jnp.zeros((256, 128), jnp.float32)
    for k in range(TOP):
        weight += jnp.where(cho_ref[k : k + 1, :] == expert, route_scale * chosen[k] / norm_by, 0.0)
    coeff = jnp.where(pick > 0.0, weight, 0.0).T
    lane_cut = lax.broadcasted_iota(jnp.int32, (128, 256), 1) % 8

    back_row = lax.broadcasted_iota(jnp.int32, (256, 32), 0)
    back_col = lax.broadcasted_iota(jnp.int32, (256, 32), 1)
    returned = jnp.zeros((256, LANE), jnp.float32)
    for n in range(4):
        total = sbuf[n, x].astype(jnp.float32)
        for way in (0, 1):
            q_copy(n, way).wait_recv()
            total += full_in[n, way].astype(jnp.float32)
        total = total.astype(jnp.bfloat16)
        for i in range(2):
            turn = jnp.where((back_row // 8 == back_col) & (back_row % 8 == 2 * n + i), 1.0, 0.0).astype(jnp.bfloat16)
            returned += jnp.dot(turn, total[:, cut(i)], preferred_element_type=jnp.float32)
    rsend[...] = returned.astype(jnp.bfloat16).reshape(16, 16, LANE)

    def b_copy(p):
        peer = tp_at(*p)
        return remote(rsend.at[peer], ret.at[tp], b_s.at[peer], b_r.at[tp], (peer, ep))

    own_back = pltpu.make_async_copy(rsend.at[tp], ret.at[tp], loc.at[5])
    own_back.start()
    for p in tp_peers:
        b_copy(p).start()
    high = coeff.astype(jnp.bfloat16)
    low = (coeff - high.astype(jnp.float32)).astype(jnp.bfloat16)
    own_back.wait()
    for p in tp_peers:
        src = tp_at(*p)
        remote(rsend.at[src], ret.at[src], b_s.at[src], b_r.at[src], (src, ep)).wait_recv()
    back = ret[...].reshape(256, LANE)
    for j in range(8):
        mixed = jnp.dot(jnp.where(lane_cut == j, high, 0.0).astype(jnp.bfloat16), back, preferred_element_type=jnp.float32)
        mixed += jnp.dot(jnp.where(lane_cut == j, low, 0.0).astype(jnp.bfloat16), back, preferred_element_type=jnp.float32)
        moe_ref[:, cut(j)] = mixed.astype(jnp.bfloat16)

    for p in tp_peers:
        d_copy(p).wait_send()
        k_copy(p).wait_send()
        rt_copy(p).wait_send()
        b_copy(p).wait_send()
    for p in ep_peers:
        l_copy(p).wait_send()
    rt_sib.wait_send()
    for g, dz in GROUPS:
        for way in (0, 1):
            x_copy(g, dz, way).wait_send()
            f_copy(g, dz, way).wait_send()
        for q in range(4):
            c_copy(g, dz, q).wait_send()
    for n in range(4):
        p_copy(n).wait_send()
        for way in (0, 1):
            h_copy(n, way).wait_send()
            q_copy(n, way).wait_send()


def experts(hidden_out, norm_gain, router, router_bias, choices, w_gate, w_up, w_down):
    dma = pltpu.SemaphoreType.DMA
    bf16, f32 = jnp.bfloat16, jnp.float32
    vmem = pl.BlockSpec(memory_space=VMEM)
    anywhere = pl.BlockSpec(memory_space=pl.ANY)
    moe_out, load, bias_next = pl.pallas_call(
        moe_kernel,
        name="experts",
        out_shape=(
            jax.ShapeDtypeStruct((128, 7168), bf16),
            jax.ShapeDtypeStruct((1, 256), f32),
            jax.ShapeDtypeStruct((1, 256), f32),
        ),
        in_specs=[vmem] * 5 + [anywhere] * 3,
        out_specs=(vmem,) * 3,
        scratch_shapes=[
            VMEM((7168, 256), bf16), VMEM((7168, 256), bf16), VMEM((256, 7168), bf16),
            VMEM((16, 16, 7168), bf16), VMEM((128, 7168), bf16), VMEM((8, LANE), f32), VMEM((16, 16, LANE), bf16),
            VMEM((8, 16, 16, LANE), bf16), VMEM((8, 256, LANE), bf16),
            VMEM((4, 4, 2, 32, 2 * LANE), bf16), VMEM((4, 4, 32, 2 * LANE), bf16),
            VMEM((4, 4, 32, 2 * LANE), bf16), VMEM((4, 2, 16, 2 * LANE), bf16), VMEM((4, 2, 32, 2 * LANE), bf16),
            VMEM((16, 16, LANE), bf16), VMEM((16, 16, LANE), bf16),
            VMEM((8, 256), f32), VMEM((16, 8, 256), f32), VMEM((8, 8, 256), f32),
            dma((6,)), dma((16,)), dma((16,)), dma((4, 2)), dma((4, 2)), dma((4, 2)), dma((4, 2)), dma((4, 4)), dma((4, 4)),
            dma((16,)), dma((16,)), dma((8,)), dma((8,)), dma((16,)), dma((16,)), dma((1,)), dma((1,)),
            dma((4,)), dma((4,)), dma((4, 2)), dma((4, 2)), dma((4, 2)), dma((4, 2)), dma((16,)), dma((16,)),
        ],
        compiler_params=pltpu.CompilerParams(
            collective_id=1, has_side_effects=True, vmem_limit_bytes=56 * 1024 * 1024
        ),
    )(
        hidden_out, norm_gain.reshape(-1, 128), router.T, router_bias.reshape(1, -1), choices.T,
        w_gate[0], w_up[0], w_down[0],
    )
    return moe_out, load.reshape(-1), bias_next.reshape(-1)


def on_device(
    attn_out, residual, w_out, norm_gain, router, router_bias, choices, w_gate, w_up, w_down
):
    hidden_out = project(attn_out, w_out, residual)
    moe_out, load, bias_next = experts(
        hidden_out, norm_gain, router, router_bias, choices, w_gate, w_up, w_down
    )
    return (hidden_out, moe_out, load, bias_next)


def solution(mesh):
    placed = (
        P("ep", "tp"),
        P(("ep", "tp"), None),
        P("tp", None),
        P(),
        P(None, "tp"),
        P(),
        P(("ep", "tp"), None),
        P("tp", None, "ep"),
        P("tp", None, "ep"),
        P("tp", "ep", None),
    )
    return jax.shard_map(
        on_device,
        mesh=mesh,
        in_specs=placed,
        out_specs=(P(("ep", "tp"), None), P(("ep", "tp"), None), P(), P()),
        check_vma=False,
    )
```

```python
import jax
import jax.numpy as jnp
from jax import lax
from jax.experimental import pallas as pl
from jax.experimental.pallas import tpu as pltpu
from jax.sharding import PartitionSpec as P

TOP = 8


norm_eps = 1e-06
route_scale = 2.5
bias_rate = 0.001


MESH = pl.DeviceIdType.MESH
VMEM = pltpu.VMEM
ROUNDS = 7
SHARED = 6
CH = 256


def ring(i):
    return lax.rem(i + 8, 4)


def place():
    tp = lax.axis_index("tp")
    ep = lax.axis_index("ep")
    return lax.div(tp, 4), lax.rem(tp, 4), lax.div(ep, 2), lax.rem(ep, 2)


def at(z, y, x, c):
    return (ring(z) * 4 + ring(y), ring(x) * 2 + lax.rem(c, 2))


def greet(peers):
    barrier = pltpu.get_barrier_semaphore()
    for peer in peers:
        pl.semaphore_signal(barrier, inc=1, device_id=peer, device_id_type=MESH)
    pl.semaphore_wait(barrier, len(peers))


def remote(src, dst, send, recv, peer):
    return pltpu.make_async_remote_copy(
        src_ref=src, dst_ref=dst, send_sem=send, recv_sem=recv, device_id=peer, device_id_type=MESH
    )


def project_kernel(
    a_ref, w_ref, res_ref, out_ref,
    ag, wown, wbuf, pbuf, half_in, full_in, resv,
    loc, a_s, a_r, y_s, y_r, g_s, g_r, v_s, v_r, x_s, x_r, f_s, f_r, c_s, c_r, h_s, h_r, z_s, z_r,
):
    z, y, x, c = place()
    half = pl.multiple_of(c * 256, 256)
    own_a = pltpu.make_async_copy(a_ref.at[:, y], ag.at[0, 0], loc.at[0])
    own_b = pltpu.make_async_copy(a_ref.at[z], ag.at[1, 0], loc.at[3])
    own_w = pltpu.make_async_copy(w_ref, wown, loc.at[1])
    own_res = pltpu.make_async_copy(res_ref, resv, loc.at[2])
    own_a.start()
    own_b.start()
    own_w.start()
    own_res.start()
    greet(
        [at(z, y + e, x, c) for e in (1, 2, 3)]
        + [at(z + e, y, x, c) for e in (1, 2, 3)]
        + [at(z, y, x + 1, c), at(z, y, x - 1, c), at(z, y, x, c + 1)]
    )
    sib = at(z, y, x, c + 1)

    def gather_at(kind, i):
        return at(z + i * kind, y + i * (1 - kind), x, c)

    def sum_at(kind, i):
        return at(z + i * (1 - kind), y + i * kind, x, c)

    def sum_place(kind):
        return z * (1 - kind) + y * kind

    def chunk(dx, r):
        return ring(x + dx) * ROUNDS + r

    def y_copy(i, n, way):
        cols = pl.ds(pl.multiple_of(n * CH, CH), CH)
        return remote(
            w_ref.at[pl.ds(half, 256), cols], wbuf.at[n, 2 - 2 * way, pl.ds(half, 256), :],
            y_s.at[i, way], y_r.at[i, way], gather_at(lax.rem(i, 2), 1 - 2 * way),
        )

    def y_land(i, n, way):
        part = wbuf.at[n, 2 - 2 * way, pl.ds(half, 256), :]
        return remote(part, part, y_s.at[i, way], y_r.at[i, way], at(z, y + 1, x, c))

    def g_copy(i, n, way):
        rows = pl.ds(pl.multiple_of(half + 128 * way, 128), 128)
        return remote(
            wbuf.at[n, 2 - 2 * way, rows, :], wbuf.at[n, 1, rows, :],
            g_s.at[i, way], g_r.at[i, way], gather_at(lax.rem(i, 2), 1 - 2 * way),
        )

    def common(u):
        return u * ROUNDS + SHARED

    def v_copy(u):
        part = wbuf.at[common(u), :, pl.ds(half, 256), :]
        return remote(part, part, v_s.at[u], v_r.at[u], sib)

    def v_land(u):
        part = wbuf.at[common(u), :, pl.ds(pl.multiple_of(256 - half, 256), 256), :]
        return remote(part, part, v_s.at[u], v_r.at[u], sib)

    def a_copy(kind, g, e):
        rows = a_ref.at[ring(z + e), g] if kind else a_ref.at[g, ring(y + e)]
        return remote(
            rows, ag.at[kind, 4 - e, g], a_s.at[kind, g, e - 1], a_r.at[kind, g, 3 - e], gather_at(kind, e)
        )

    def x_copy(r, way):
        part = wbuf.at[chunk(0, r), :, pl.ds(half, 256), :]
        return remote(part, part, x_s.at[r, way], x_r.at[r, way], at(z, y, x + 1 - 2 * way, c))

    def x_land(r, way):
        part = wbuf.at[chunk(2 * way - 1, r), :, pl.ds(half, 256), :]
        return remote(part, part, x_s.at[r, way], x_r.at[r, way], at(z, y, x + 1 - 2 * way, c))

    def f_part(dx, r, way):
        return wbuf.at[chunk(dx, r), :, pl.ds(pl.multiple_of(half + 128 * way, 128), 128), :]

    def f_copy(r, way):
        part = f_part(2 * way - 1, r, way)
        return remote(part, part, f_s.at[r, way], f_r.at[r, way], at(z, y, x + 1 - 2 * way, c))

    def f_land(r, way):
        part = f_part(2, r, way)
        return remote(part, part, f_s.at[r, way], f_r.at[r, way], at(z, y, x + 1 - 2 * way, c))

    def hop(q):
        return (0, 3, 1, 2)[q]

    def c_copy(r, q):
        part = wbuf.at[chunk(hop(q), r), :, pl.ds(half, 256), :]
        return remote(part, part, c_s.at[r, q], c_r.at[r, q], sib)

    def c_land(n, r, q):
        other = pl.multiple_of(256 - half, 256)
        part = wbuf.at[n, :, pl.ds(other, 256), :]
        return remote(part, part, c_s.at[r, q], c_r.at[r, q], sib)

    def halves(way):
        return pl.ds(64 * way, 64)

    def h_copy(n, kind, way):
        return remote(
            pbuf.at[n, ring(sum_place(kind) + 2), halves(way)], half_in.at[n, way],
            h_s.at[n, way], h_r.at[n, way], sum_at(kind, 1 - 2 * way),
        )

    def z_copy(n, kind, way):
        return remote(
            pbuf.at[n, ring(sum_place(kind) + 1 - 2 * way)], full_in.at[n, way],
            z_s.at[n, way], z_r.at[n, way], sum_at(kind, 1 - 2 * way),
        )

    def start_y(i, n):
        for way in (0, 1):
            y_copy(i, n, way).start()

    def start_a(g):
        for e in (2, 1, 3):
            for kind in (0, 1):
                a_copy(kind, g, e).start()

    def pass_on(i, n):
        for way in (0, 1):
            y_land(i, n, way).wait_recv()
            g_copy(i, n, way).start()

    def first(r):
        for way in (0, 1):
            g_copy(r, chunk(0, r), way).wait_recv()
        x_copy(r, 0).start()
        x_copy(r, 1).start()
        c_copy(r, 0).start()

    def multiply(n, kind):
        cols = pl.ds(pl.multiple_of(n * CH, CH), CH)
        total = jnp.dot(ag[kind, 0].reshape(512, 512), wown[:, cols], preferred_element_type=jnp.float32)
        for k in range(3):
            total += jnp.dot(ag[kind, k + 1].reshape(512, 512), wbuf[n, k], preferred_element_type=jnp.float32)
        pbuf[n] = total.astype(jnp.bfloat16).reshape(4, 128, CH)
        for way in (0, 1):
            h_copy(n, kind, way).start()

    def combine(n, kind):
        for way in (0, 1):
            to = ring(sum_place(kind) + 1 - 2 * way)
            h_copy(n, kind, way).wait_recv()
            both = pbuf[n, to, halves(way)].astype(jnp.float32) + half_in[n, way].astype(jnp.float32)
            pbuf[n, to, halves(way)] = both.astype(jnp.bfloat16)
            z_copy(n, kind, way).start()

    def finish(n, kind):
        cols = pl.ds(pl.multiple_of(n * CH, CH), CH)
        total = pbuf[n, sum_place(kind)].astype(jnp.float32)
        for way in (0, 1):
            z_copy(n, kind, way).wait_recv()
            total += full_in[n, way].astype(jnp.float32)
        out_ref[:, cols] = (resv[:, cols].astype(jnp.float32) + total).astype(jnp.bfloat16)

    def near(q, r):
        return chunk(q + lax.div(q, 2), r)

    def step(work, r):
        @pl.when((r >= 0) & (r < SHARED))
        def _():
            @pl.loop(0, 3)
            def _(q):
                work(near(q, r), lax.rem(r, 2))

        @pl.when((r >= 3) & (r < 7))
        def _():
            work(common(r - 3), lax.rem(r - 3, 2))

        @pl.when((r >= 1) & (r <= SHARED))
        def _():
            work(chunk(2, r - 1), lax.rem(r - 1, 2))

    start_y(0, chunk(0, 0))
    start_y(1, chunk(0, 1))
    pass_on(0, chunk(0, 0))
    pass_on(1, chunk(0, 1))
    start_a(0)
    start_a(1)
    first(0)
    first(1)
    start_a(2)
    start_y(2, chunk(0, 2))
    start_y(3, chunk(0, 3))
    start_a(3)
    own_a.wait()
    own_b.wait()
    own_w.wait()
    own_res.wait()

    def multiply_near(r):
        @pl.loop(0, 3)
        def _(q):
            n = near(q, r)
            c_land(n, r, lax.rem(3 - q, 3)).wait_recv()
            multiply(n, lax.rem(r, 2))

    @pl.loop(0, SHARED + 4)
    def _(r):
        @pl.when(r < SHARED)
        def _():
            for way in (0, 1):
                x_land(r, way).wait_recv()
                f_copy(r, way).start()
                c_copy(r, 1 + way).start()

        @pl.when(r + 2 < SHARED)
        def _():
            pass_on(r + 2, chunk(0, r + 2))

        @pl.when((r >= 1) & (r + 3 < SHARED))
        def _():
            start_y(r + 3, chunk(0, r + 3))

        @pl.when(r < 4)
        def _():
            start_y(SHARED + r, common(r))

        @pl.when(r + 2 < SHARED)
        def _():
            first(r + 2)

        @pl.when((r >= 1) & (r < 5))
        def _():
            pass_on(SHARED + r - 1, common(r - 1))

        @pl.when((r >= 2) & (r < 6))
        def _():
            for way in (0, 1):
                g_copy(SHARED + r - 2, common(r - 2), way).wait_recv()
            v_copy(r - 2).start()

        @pl.when(r == 1)
        def _():
            for g in range(4):
                for k in range(3):
                    for kind in (0, 1):
                        part = ag.at[kind, k + 1, g]
                        remote(part, part, a_s.at[kind, g, k], a_r.at[kind, g, k], at(z, y + 1, x, c)).wait_recv()
            multiply_near(0)

        @pl.when(r >= 2)
        def _():
            step(combine, r - 1)

        @pl.when((r >= 1) & (r < SHARED))
        def _():
            multiply_near(r)

        @pl.when((r >= 3) & (r < 7))
        def _():
            v_land(r - 3).wait_recv()
            multiply(common(r - 3), lax.rem(r - 3, 2))

        @pl.when((r >= 1) & (r <= SHARED))
        def _():
            for way in (0, 1):
                f_land(r - 1, way).wait_recv()
            c_copy(r - 1, 3).start()
            c_land(chunk(2, r - 1), r - 1, 3).wait_recv()
            multiply(chunk(2, r - 1), lax.rem(r - 1, 2))

        @pl.when(r == 2)
        def _():
            @pl.loop(0, 3)
            def _(q):
                combine(near(q, 0), 0)

        @pl.when(r >= 3)
        def _():
            step(finish, r - 3)

    for g in range(4):
        for e in (1, 2, 3):
            for kind in (0, 1):
                a_copy(kind, g, e).wait_send()

    @pl.loop(0, SHARED)
    def _(r):
        for way in (0, 1):
            y_copy(r, chunk(0, r), way).wait_send()
            g_copy(r, chunk(0, r), way).wait_send()
            x_copy(r, way).wait_send()
            f_copy(r, way).wait_send()
        for q in range(4):
            c_copy(r, q).wait_send()

    @pl.loop(0, 4)
    def _(u):
        for way in (0, 1):
            y_copy(SHARED + u, common(u), way).wait_send()
            g_copy(SHARED + u, common(u), way).wait_send()
        v_copy(u).wait_send()

    @pl.loop(0, 4 * ROUNDS)
    def _(n):
        for way in (0, 1):
            h_copy(n, 0, way).wait_send()
            z_copy(n, 0, way).wait_send()


def project(attn_out, w_out, residual):
    dma = pltpu.SemaphoreType.DMA
    anywhere = pl.BlockSpec(memory_space=pl.ANY)
    return pl.pallas_call(
        project_kernel,
        name="project",
        out_shape=jax.ShapeDtypeStruct((128, 7168), jnp.bfloat16),
        in_specs=[anywhere] * 3,
        out_specs=pl.BlockSpec(memory_space=VMEM),
        scratch_shapes=[
            VMEM((2, 4, 4, 128, 512), jnp.bfloat16),
            VMEM((512, 7168), jnp.bfloat16),
            VMEM((28, 3, 512, CH), jnp.bfloat16),
            VMEM((28, 4, 128, CH), jnp.bfloat16),
            VMEM((28, 2, 64, CH), jnp.bfloat16),
            VMEM((28, 2, 128, CH), jnp.bfloat16),
            VMEM((128, 7168), jnp.bfloat16),
            dma((4,)), dma((2, 4, 3)), dma((2, 4, 3)), dma((10, 2)), dma((10, 2)), dma((10, 2)), dma((10, 2)),
            dma((4,)), dma((4,)), dma((6, 2)), dma((6, 2)), dma((6, 2)), dma((6, 2)), dma((6, 4)), dma((6, 4)),
            dma((28, 2)), dma((28, 2)), dma((28, 2)), dma((28, 2)),
        ],
        compiler_params=pltpu.CompilerParams(
            collective_id=0, has_side_effects=True, vmem_limit_bytes=58 * 1024 * 1024
        ),
    )(attn_out.reshape(4, 4, 128, 512), w_out, residual)


LANE = 896
GROUPS = ((0, 0), (1, 1), (2, 3), (3, 2))


def moe_kernel(
    hid_ref, gain_ref, rout_ref, bias_ref, cho_ref, wg_ref, wu_ref, wd_ref,
    moe_ref, load_ref, next_ref,
    wg, wu, wd, rt, normed, gain, snd, land, rows, ybuf, r1, sbuf, half_in, full_in, rsend, ret, cnt, cnt_tp, cnt_ep,
    loc, d_s, d_r, ax_s, ax_r, af_s, af_r, ac_s, ac_r, k_s, k_r, l_s, l_r, rt_s, rt_r, rs_s, rs_r,
    p_s, p_r, h_s, h_r, q_s, q_r, b_s, b_r,
):
    z, y, x, c = place()
    tp = z * 4 + y
    ep = x * 2 + c
    sib = at(z, y, x, c + 1)
    width = hid_ref.shape[1]
    half = pl.ds(pl.multiple_of(c * (width // 2), width // 2), width // 2)
    loads = [pltpu.make_async_copy(s, d, loc.at[i]) for i, (s, d) in enumerate(((wg_ref, wg), (wu_ref, wu), (wd_ref, wd)))]
    for load in loads:
        load.start()
    tp_peers = [(dz, dy) for dz in (0, 1, 3, 2) for dy in (1, 3, 2, 0) if (dz, dy) != (0, 0)]
    ep_peers = [(dx, dc) for dx in (0, 1, 3, 2) for dc in (0, 1) if (dx, dc) != (0, 0)]

    def tp_at(dz, dy):
        return ring(z + dz) * 4 + ring(y + dy)

    def ep_at(dx, dc):
        return ring(x + dx) * 2 + lax.rem(c + dc, 2)

    barrier = pltpu.get_barrier_semaphore()
    for p in tp_peers:
        pl.semaphore_signal(barrier, inc=1, device_id=(tp_at(*p), ep), device_id_type=MESH)
    for p in ep_peers:
        pl.semaphore_signal(barrier, inc=1, device_id=(tp, ep_at(*p)), device_id_type=MESH)

    def cut(j):
        return slice(j * LANE, (j + 1) * LANE)

    row = lax.broadcasted_iota(jnp.int32, (256, 128), 0)
    lane = lax.broadcasted_iota(jnp.int32, (256, 128), 1)
    expert = row // 16
    member = jnp.zeros((256, 128), jnp.float32)
    named = jnp.zeros((256, 128), jnp.float32)
    for k in range(TOP):
        ck = cho_ref[k : k + 1, :]
        member += jnp.where(ck == expert, 1.0, 0.0)
        named += jnp.where(ck == row, 1.0, 0.0)
    before = jnp.where(row[:128] < lane[:128], 1.0, 0.0).astype(jnp.bfloat16)
    rank = jnp.dot(member.astype(jnp.bfloat16), before, preferred_element_type=jnp.float32)
    slot = ((row // 8) % 2).astype(jnp.float32)
    pick = jnp.where(rank == slot, member, 0.0)
    feature = row % 8
    picked = jnp.zeros((256, LANE), jnp.float32)
    for j in range(8):
        pj = jnp.where(feature == j, pick, 0.0).astype(jnp.bfloat16)
        picked += jnp.dot(pj, hid_ref[:, cut(j)], preferred_element_type=jnp.float32)
    gains = gain_ref[...].astype(jnp.float32)
    for j in range(8):
        for i in range(7):
            gain[j : j + 1, i * 128 : (i + 1) * 128] = gains[j * 7 + i : j * 7 + i + 1, :]
    picked = picked.reshape(32, 8, LANE)
    ssq = jnp.sum(jnp.sum(picked * picked, axis=2, keepdims=True), axis=1, keepdims=True)
    outgoing = picked * lax.rsqrt(ssq / width + norm_eps) * gain[...][None]
    snd[...] = outgoing.astype(jnp.bfloat16).reshape(16, 16, LANE)
    contract_last = (((1,), (1,)), ((), ()))
    cnt[...] = lax.dot_general(
        jnp.ones((8, 128), jnp.bfloat16), named.astype(jnp.bfloat16), contract_last, preferred_element_type=jnp.float32
    )
    pl.semaphore_wait(barrier, len(tp_peers) + len(ep_peers))

    def d_copy(p):
        peer = tp_at(*p)
        return remote(snd.at[peer], land.at[ep, tp], d_s.at[peer], d_r.at[tp], (peer, ep))

    own_rows = pltpu.make_async_copy(snd.at[tp], land.at[ep, tp], loc.at[3])
    own_rows.start()
    for p in tp_peers:
        d_copy(p).start()

    def k_copy(p):
        peer = tp_at(*p)
        return remote(cnt, cnt_tp.at[tp], k_s.at[peer], k_r.at[tp], (peer, ep))

    for p in tp_peers:
        k_copy(p).start()

    def group(dz):
        return pl.ds(pl.multiple_of(ring(z + dz) * 4, 4), 4)

    def x_copy(g, dz, way):
        part = land.at[ep, group(dz)]
        return remote(part, part, ax_s.at[g, way], ax_r.at[g, way], (tp, ep_at(1 - 2 * way, 0)))

    def x_land(g, dz, way):
        part = land.at[ep_at(2 * way - 1, 0), group(dz)]
        return remote(part, part, ax_s.at[g, way], ax_r.at[g, way], (tp, ep_at(1, 0)))

    def f_rows(dx, dz, way):
        return land.at[ep_at(dx, 0), pl.ds(pl.multiple_of(ring(z + dz) * 4 + 2 * way, 2), 2)]

    def f_copy(g, dz, way):
        part = f_rows(2 * way - 1, dz, way)
        return remote(part, part, af_s.at[g, way], af_r.at[g, way], (tp, ep_at(1 - 2 * way, 0)))

    def f_land(g, dz, way):
        part = f_rows(2, dz, way)
        return remote(part, part, af_s.at[g, way], af_r.at[g, way], (tp, ep_at(1, 0)))

    def c_copy(g, dz, q):
        part = land.at[ep_at(q, 0), group(dz)]
        return remote(part, part, ac_s.at[g, q], ac_r.at[g, q], sib)

    def c_land(g, dz, q):
        part = land.at[ep_at(q, 1), group(dz)]
        return remote(part, part, ac_s.at[g, q], ac_r.at[g, q], sib)

    def d_land(p):
        src = tp_at(*p)
        return remote(snd.at[src], land.at[ep, src], d_s.at[src], d_r.at[src], (src, ep))

    for g, dz in GROUPS:
        for p in tp_peers:
            if p[0] == dz:
                d_land(p).wait_recv()
        if dz == 0:
            own_rows.wait()
        for way in (0, 1):
            x_copy(g, dz, way).start()
        c_copy(g, dz, 0).start()

    def rt_copy(p):
        peer = tp_at(*p)
        return remote(rout_ref.at[:, half], rt.at[tp, :, half], rt_s.at[peer], rt_r.at[tp], (peer, ep))

    own_rt = pltpu.make_async_copy(rout_ref.at[:, half], rt.at[tp, :, half], loc.at[4])
    own_rt.start()
    for p in tp_peers:
        rt_copy(p).start()

    for p in tp_peers:
        src = tp_at(*p)
        remote(cnt, cnt_tp.at[src], k_s.at[src], k_r.at[src], (src, ep)).wait_recv()
    cnt_tp[tp] = cnt[...]
    part_sum = cnt_tp[0]
    for i in range(1, 16):
        part_sum += cnt_tp[i]
    cnt_ep[ep] = part_sum

    def l_copy(p):
        peer = ep_at(*p)
        return remote(cnt_ep.at[ep], cnt_ep.at[ep], l_s.at[peer], l_r.at[ep], (tp, peer))

    for p in ep_peers:
        l_copy(p).start()

    out_row = lax.broadcasted_iota(jnp.int32, (128, 128), 0)
    in_row = lax.broadcasted_iota(jnp.int32, (128, 128), 1)
    source = ((out_row % 16) // 2) * 16 + (out_row % 2) * 8 + out_row // 16
    perm = jnp.where(in_row == source, 1.0, 0.0).astype(jnp.bfloat16)

    def turn_rows(group_of):
        for part in range(2):
            block = land[group_of, part * 8 : part * 8 + 8].reshape(128, LANE)
            turned = jnp.dot(perm, block, preferred_element_type=jnp.float32).astype(jnp.bfloat16)
            to = pl.ds(pl.multiple_of(group_of * 32 + part * 16, 16), 16)
            rows[:, to, :] = turned.reshape(8, 16, LANE)

    turn_rows(ep)
    for g, dz in GROUPS:
        for way in (0, 1):
            x_land(g, dz, way).wait_recv()
            f_copy(g, dz, way).start()
            c_copy(g, dz, 3 - 2 * way).start()
    for q in (0, 3, 1):
        if q:
            turn_rows(ep_at(q, 0))
        if q == 1:
            for g, dz in GROUPS:
                for way in (0, 1):
                    f_land(g, dz, way).wait_recv()
                c_copy(g, dz, 2).start()
        for g, dz in GROUPS:
            c_land(g, dz, q).wait_recv()
        turn_rows(ep_at(q, 1))
    turn_rows(ep_at(2, 0))
    for g, dz in GROUPS:
        c_land(g, dz, 2).wait_recv()
    turn_rows(ep_at(2, 1))

    for load in loads:
        load.wait()
    gate_val = jnp.zeros((256, 256), jnp.float32)
    up_val = jnp.zeros((256, 256), jnp.float32)
    for j in range(8):
        gate_val += jnp.dot(rows[j], wg[cut(j), :], preferred_element_type=jnp.float32)
        up_val += jnp.dot(rows[j], wu[cut(j), :], preferred_element_type=jnp.float32)
    active = (gate_val / (1.0 + jnp.exp(-gate_val)) * up_val).astype(jnp.bfloat16)

    def p_copy(n):
        return remote(ybuf.at[n, :, 1 - c], r1.at[n], p_s.at[n], p_r.at[n], sib)

    def h_copy(n, way):
        rows_of = pl.ds(16 * way, 16)
        return remote(
            sbuf.at[n, ring(x + 2), rows_of], half_in.at[n, way],
            h_s.at[n, way], h_r.at[n, way], (tp, ep_at(1 - 2 * way, 0)),
        )

    def q_copy(n, way):
        to = 1 - 2 * way
        return remote(
            sbuf.at[n, ring(x + to)], full_in.at[n, way], q_s.at[n, way], q_r.at[n, way], (tp, ep_at(to, 0))
        )

    def forward(n):
        for way in (0, 1):
            to = ring(x + 1 - 2 * way)
            h_copy(n, way).wait_recv()
            rows_of = slice(16 * way, 16 * way + 16)
            both = sbuf[n, to, rows_of].astype(jnp.float32) + half_in[n, way].astype(jnp.float32)
            sbuf[n, to, rows_of] = both.astype(jnp.bfloat16)
            q_copy(n, way).start()

    for n in range(4):
        part = jnp.dot(active, wd[:, n * 2 * LANE : (n + 1) * 2 * LANE], preferred_element_type=jnp.float32)
        ybuf[n] = part.astype(jnp.bfloat16).reshape(4, 2, 32, 2 * LANE)
        p_copy(n).start()
    for n in range(4):
        p_copy(n).wait_recv()
        for i in range(4):
            both = ybuf[n, i, c].astype(jnp.float32) + r1[n, i].astype(jnp.float32)
            sbuf[n, i] = both.astype(jnp.bfloat16)
        for way in (0, 1):
            h_copy(n, way).start()
        if n:
            forward(n - 1)
    forward(3)

    for p in ep_peers:
        peer = ep_at(*p)
        remote(cnt_ep.at[peer], cnt_ep.at[peer], l_s.at[peer], l_r.at[peer], (tp, peer)).wait_recv()
    counts = cnt_ep[0]
    for i in range(1, 8):
        counts += cnt_ep[i]
    counts = counts[0:1]
    slots = 128.0 * 128.0 * TOP
    load_ref[...] = counts * 256.0 / slots
    gap = slots - counts * 256.0
    sign = jnp.where(gap > 0.0, 1.0, jnp.where(gap < 0.0, -1.0, 0.0))
    next_ref[...] = bias_ref[...] + bias_rate * sign

    for p in tp_peers:
        src = tp_at(*p)
        remote(rout_ref.at[:, half], rt.at[src, :, half], rt_s.at[src], rt_r.at[src], (src, ep)).wait_recv()
    own_rt.wait()
    mine = rt.at[:, :, half]
    rt_sib = remote(mine, mine, rs_s.at[0], rs_r.at[0], sib)
    rt_sib.start()
    other = rt.at[:, :, pl.ds(pl.multiple_of((1 - c) * (width // 2), width // 2), width // 2)]
    ssq = jnp.zeros((128, 1), jnp.float32)
    for j in range(8):
        h = hid_ref[:, cut(j)].astype(jnp.float32)
        ssq += jnp.sum(h * h, axis=1, keepdims=True)
    scale = lax.rsqrt(ssq / width + norm_eps)
    for j in range(8):
        h = hid_ref[:, cut(j)].astype(jnp.float32)
        normed[:, cut(j)] = (h * scale * gain[j : j + 1, :]).astype(jnp.bfloat16)
    remote(other, other, rs_s.at[0], rs_r.at[0], sib).wait_recv()
    logits = jnp.zeros((256, 128), jnp.float32)
    for j in range(8):
        logits += lax.dot_general(
            rt[:, :, cut(j)].reshape(256, LANE), normed[:, cut(j)], contract_last, preferred_element_type=jnp.float32
        )
    scores = 1.0 / (1.0 + jnp.exp(-logits))
    chosen = []
    for k in range(TOP):
        hit = cho_ref[k : k + 1, :] == row
        chosen.append(jnp.sum(jnp.where(hit, scores, 0.0), axis=0, keepdims=True))
    norm_by = chosen[0]
    for k in range(1, TOP):
        norm_by = norm_by + chosen[k]
    weight = jnp.zeros((256, 128), jnp.float32)
    for k in range(TOP):
        weight += jnp.where(cho_ref[k : k + 1, :] == expert, route_scale * chosen[k] / norm_by, 0.0)
    coeff = jnp.where(pick > 0.0, weight, 0.0).T
    lane_cut = lax.broadcasted_iota(jnp.int32, (128, 256), 1) % 8

    back_row = lax.broadcasted_iota(jnp.int32, (256, 32), 0)
    back_col = lax.broadcasted_iota(jnp.int32, (256, 32), 1)
    returned = jnp.zeros((256, LANE), jnp.float32)
    for n in range(4):
        total = sbuf[n, x].astype(jnp.float32)
        for way in (0, 1):
            q_copy(n, way).wait_recv()
            total += full_in[n, way].astype(jnp.float32)
        total = total.astype(jnp.bfloat16)
        for i in range(2):
            turn = jnp.where((back_row // 8 == back_col) & (back_row % 8 == 2 * n + i), 1.0, 0.0).astype(jnp.bfloat16)
            returned += jnp.dot(turn, total[:, cut(i)], preferred_element_type=jnp.float32)
    rsend[...] = returned.astype(jnp.bfloat16).reshape(16, 16, LANE)

    def b_copy(p):
        peer = tp_at(*p)
        return remote(rsend.at[peer], ret.at[tp], b_s.at[peer], b_r.at[tp], (peer, ep))

    own_back = pltpu.make_async_copy(rsend.at[tp], ret.at[tp], loc.at[5])
    own_back.start()
    for p in tp_peers:
        b_copy(p).start()
    high = coeff.astype(jnp.bfloat16)
    low = (coeff - high.astype(jnp.float32)).astype(jnp.bfloat16)
    own_back.wait()
    for p in tp_peers:
        src = tp_at(*p)
        remote(rsend.at[src], ret.at[src], b_s.at[src], b_r.at[src], (src, ep)).wait_recv()
    back = ret[...].reshape(256, LANE)
    for j in range(8):
        mixed = jnp.dot(jnp.where(lane_cut == j, high, 0.0).astype(jnp.bfloat16), back, preferred_element_type=jnp.float32)
        mixed += jnp.dot(jnp.where(lane_cut == j, low, 0.0).astype(jnp.bfloat16), back, preferred_element_type=jnp.float32)
        moe_ref[:, cut(j)] = mixed.astype(jnp.bfloat16)

    for p in tp_peers:
        d_copy(p).wait_send()
        k_copy(p).wait_send()
        rt_copy(p).wait_send()
        b_copy(p).wait_send()
    for p in ep_peers:
        l_copy(p).wait_send()
    rt_sib.wait_send()
    for g, dz in GROUPS:
        for way in (0, 1):
            x_copy(g, dz, way).wait_send()
            f_copy(g, dz, way).wait_send()
        for q in range(4):
            c_copy(g, dz, q).wait_send()
    for n in range(4):
        p_copy(n).wait_send()
        for way in (0, 1):
            h_copy(n, way).wait_send()
            q_copy(n, way).wait_send()


def experts(hidden_out, norm_gain, router, router_bias, choices, w_gate, w_up, w_down):
    dma = pltpu.SemaphoreType.DMA
    bf16, f32 = jnp.bfloat16, jnp.float32
    vmem = pl.BlockSpec(memory_space=VMEM)
    anywhere = pl.BlockSpec(memory_space=pl.ANY)
    moe_out, load, bias_next = pl.pallas_call(
        moe_kernel,
        name="experts",
        out_shape=(
            jax.ShapeDtypeStruct((128, 7168), bf16),
            jax.ShapeDtypeStruct((1, 256), f32),
            jax.ShapeDtypeStruct((1, 256), f32),
        ),
        in_specs=[vmem] * 5 + [anywhere] * 3,
        out_specs=(vmem,) * 3,
        scratch_shapes=[
            VMEM((7168, 256), bf16), VMEM((7168, 256), bf16), VMEM((256, 7168), bf16),
            VMEM((16, 16, 7168), bf16), VMEM((128, 7168), bf16), VMEM((8, LANE), f32), VMEM((16, 16, LANE), bf16),
            VMEM((8, 16, 16, LANE), bf16), VMEM((8, 256, LANE), bf16),
            VMEM((4, 4, 2, 32, 2 * LANE), bf16), VMEM((4, 4, 32, 2 * LANE), bf16),
            VMEM((4, 4, 32, 2 * LANE), bf16), VMEM((4, 2, 16, 2 * LANE), bf16), VMEM((4, 2, 32, 2 * LANE), bf16),
            VMEM((16, 16, LANE), bf16), VMEM((16, 16, LANE), bf16),
            VMEM((8, 256), f32), VMEM((16, 8, 256), f32), VMEM((8, 8, 256), f32),
            dma((6,)), dma((16,)), dma((16,)), dma((4, 2)), dma((4, 2)), dma((4, 2)), dma((4, 2)), dma((4, 4)), dma((4, 4)),
            dma((16,)), dma((16,)), dma((8,)), dma((8,)), dma((16,)), dma((16,)), dma((1,)), dma((1,)),
            dma((4,)), dma((4,)), dma((4, 2)), dma((4, 2)), dma((4, 2)), dma((4, 2)), dma((16,)), dma((16,)),
        ],
        compiler_params=pltpu.CompilerParams(
            collective_id=1, has_side_effects=True, vmem_limit_bytes=56 * 1024 * 1024
        ),
    )(
        hidden_out, norm_gain.reshape(-1, 128), router.T, router_bias.reshape(1, -1), choices.T,
        w_gate[0], w_up[0], w_down[0],
    )
    return moe_out, load.reshape(-1), bias_next.reshape(-1)


def on_device(
    attn_out, residual, w_out, norm_gain, router, router_bias, choices, w_gate, w_up, w_down
):
    hidden_out = project(attn_out, w_out, residual)
    moe_out, load, bias_next = experts(
        hidden_out, norm_gain, router, router_bias, choices, w_gate, w_up, w_down
    )
    return (hidden_out, moe_out, load, bias_next)


def solution(mesh):
    placed = (
        P("ep", "tp"),
        P(("ep", "tp"), None),
        P("tp", None),
        P(),
        P(None, "tp"),
        P(),
        P(("ep", "tp"), None),
        P("tp", None, "ep"),
        P("tp", None, "ep"),
        P("tp", "ep", None),
    )
    return jax.shard_map(
        on_device,
        mesh=mesh,
        in_specs=placed,
        out_specs=(P(("ep", "tp"), None), P(("ep", "tp"), None), P(), P()),
        check_vma=False,
    )
```

```python
import jax
import jax.numpy as jnp
from jax import lax
from jax.experimental import pallas as pl
from jax.experimental.pallas import tpu as pltpu
from jax.sharding import PartitionSpec as P

TOP = 8


norm_eps = 1e-06
route_scale = 2.5
bias_rate = 0.001


MESH = pl.DeviceIdType.MESH
VMEM = pltpu.VMEM
ROUNDS = 7
SHARED = 6
CH = 256


def ring(i):
    return lax.rem(i + 8, 4)


def place():
    tp = lax.axis_index("tp")
    ep = lax.axis_index("ep")
    return lax.div(tp, 4), lax.rem(tp, 4), lax.div(ep, 2), lax.rem(ep, 2)


def at(z, y, x, c):
    return (ring(z) * 4 + ring(y), ring(x) * 2 + lax.rem(c, 2))


def greet(peers):
    barrier = pltpu.get_barrier_semaphore()
    for peer in peers:
        pl.semaphore_signal(barrier, inc=1, device_id=peer, device_id_type=MESH)
    pl.semaphore_wait(barrier, len(peers))


def remote(src, dst, send, recv, peer):
    return pltpu.make_async_remote_copy(
        src_ref=src, dst_ref=dst, send_sem=send, recv_sem=recv, device_id=peer, device_id_type=MESH
    )


def project_kernel(
    a_ref, w_ref, res_ref, out_ref,
    ag, wown, wbuf, pbuf, half_in, full_in, resv,
    loc, a_s, a_r, y_s, y_r, g_s, g_r, v_s, v_r, x_s, x_r, f_s, f_r, c_s, c_r, h_s, h_r, z_s, z_r,
):
    z, y, x, c = place()
    half = pl.multiple_of(c * 256, 256)
    own_a = pltpu.make_async_copy(a_ref.at[:, y], ag.at[0, 0], loc.at[0])
    own_b = pltpu.make_async_copy(a_ref.at[z], ag.at[1, 0], loc.at[3])
    own_w = pltpu.make_async_copy(w_ref, wown, loc.at[1])
    own_res = pltpu.make_async_copy(res_ref, resv, loc.at[2])
    own_a.start()
    own_b.start()
    own_w.start()
    own_res.start()
    greet(
        [at(z, y + e, x, c) for e in (1, 2, 3)]
        + [at(z + e, y, x, c) for e in (1, 2, 3)]
        + [at(z, y, x + 1, c), at(z, y, x - 1, c), at(z, y, x, c + 1)]
    )
    sib = at(z, y, x, c + 1)

    def gather_at(kind, i):
        return at(z + i * kind, y + i * (1 - kind), x, c)

    def sum_at(kind, i):
        return at(z + i * (1 - kind), y + i * kind, x, c)

    def sum_place(kind):
        return z * (1 - kind) + y * kind

    def chunk(dx, r):
        return ring(x + dx) * ROUNDS + r

    def y_copy(i, n, way):
        cols = pl.ds(pl.multiple_of(n * CH, CH), CH)
        return remote(
            w_ref.at[pl.ds(half, 256), cols], wbuf.at[n, 2 - 2 * way, pl.ds(half, 256), :],
            y_s.at[i, way], y_r.at[i, way], gather_at(lax.rem(i, 2), 1 - 2 * way),
        )

    def y_land(i, n, way):
        part = wbuf.at[n, 2 - 2 * way, pl.ds(half, 256), :]
        return remote(part, part, y_s.at[i, way], y_r.at[i, way], at(z, y + 1, x, c))

    def g_copy(i, n, way):
        rows = pl.ds(pl.multiple_of(half + 128 * way, 128), 128)
        return remote(
            wbuf.at[n, 2 - 2 * way, rows, :], wbuf.at[n, 1, rows, :],
            g_s.at[i, way], g_r.at[i, way], gather_at(lax.rem(i, 2), 1 - 2 * way),
        )

    def common(u):
        return u * ROUNDS + SHARED

    def v_copy(u):
        part = wbuf.at[common(u), :, pl.ds(half, 256), :]
        return remote(part, part, v_s.at[u], v_r.at[u], sib)

    def v_land(u):
        part = wbuf.at[common(u), :, pl.ds(pl.multiple_of(256 - half, 256), 256), :]
        return remote(part, part, v_s.at[u], v_r.at[u], sib)

    def a_copy(kind, g, e):
        rows = a_ref.at[ring(z + e), g] if kind else a_ref.at[g, ring(y + e)]
        return remote(
            rows, ag.at[kind, 4 - e, g], a_s.at[kind, g, e - 1], a_r.at[kind, g, 3 - e], gather_at(kind, e)
        )

    def x_copy(r, way):
        part = wbuf.at[chunk(0, r), :, pl.ds(half, 256), :]
        return remote(part, part, x_s.at[r, way], x_r.at[r, way], at(z, y, x + 1 - 2 * way, c))

    def x_land(r, way):
        part = wbuf.at[chunk(2 * way - 1, r), :, pl.ds(half, 256), :]
        return remote(part, part, x_s.at[r, way], x_r.at[r, way], at(z, y, x + 1 - 2 * way, c))

    def f_part(dx, r, way):
        return wbuf.at[chunk(dx, r), :, pl.ds(pl.multiple_of(half + 128 * way, 128), 128), :]

    def f_copy(r, way):
        part = f_part(2 * way - 1, r, way)
        return remote(part, part, f_s.at[r, way], f_r.at[r, way], at(z, y, x + 1 - 2 * way, c))

    def f_land(r, way):
        part = f_part(2, r, way)
        return remote(part, part, f_s.at[r, way], f_r.at[r, way], at(z, y, x + 1 - 2 * way, c))

    def hop(q):
        return (0, 3, 1, 2)[q]

    def c_copy(r, q):
        part = wbuf.at[chunk(hop(q), r), :, pl.ds(half, 256), :]
        return remote(part, part, c_s.at[r, q], c_r.at[r, q], sib)

    def c_land(n, r, q):
        other = pl.multiple_of(256 - half, 256)
        part = wbuf.at[n, :, pl.ds(other, 256), :]
        return remote(part, part, c_s.at[r, q], c_r.at[r, q], sib)

    def halves(way):
        return pl.ds(64 * way, 64)

    def h_copy(n, kind, way):
        return remote(
            pbuf.at[n, ring(sum_place(kind) + 2), halves(way)], half_in.at[n, way],
            h_s.at[n, way], h_r.at[n, way], sum_at(kind, 1 - 2 * way),
        )

    def z_copy(n, kind, way):
        return remote(
            pbuf.at[n, ring(sum_place(kind) + 1 - 2 * way)], full_in.at[n, way],
            z_s.at[n, way], z_r.at[n, way], sum_at(kind, 1 - 2 * way),
        )

    def start_y(i, n):
        for way in (0, 1):
            y_copy(i, n, way).start()

    def start_a(g):
        for e in (2, 1, 3):
            for kind in (0, 1):
                a_copy(kind, g, e).start()

    def pass_on(i, n):
        for way in (0, 1):
            y_land(i, n, way).wait_recv()
            g_copy(i, n, way).start()

    def first(r):
        for way in (0, 1):
            g_copy(r, chunk(0, r), way).wait_recv()
        x_copy(r, 0).start()
        x_copy(r, 1).start()
        c_copy(r, 0).start()

    def multiply(n, kind):
        cols = pl.ds(pl.multiple_of(n * CH, CH), CH)
        total = jnp.dot(ag[kind, 0].reshape(512, 512), wown[:, cols], preferred_element_type=jnp.float32)
        for k in range(3):
            total += jnp.dot(ag[kind, k + 1].reshape(512, 512), wbuf[n, k], preferred_element_type=jnp.float32)
        pbuf[n] = total.astype(jnp.bfloat16).reshape(4, 128, CH)
        for way in (0, 1):
            h_copy(n, kind, way).start()

    def combine(n, kind):
        for way in (0, 1):
            to = ring(sum_place(kind) + 1 - 2 * way)
            h_copy(n, kind, way).wait_recv()
            both = pbuf[n, to, halves(way)].astype(jnp.float32) + half_in[n, way].astype(jnp.float32)
            pbuf[n, to, halves(way)] = both.astype(jnp.bfloat16)
            z_copy(n, kind, way).start()

    def finish(n, kind):
        cols = pl.ds(pl.multiple_of(n * CH, CH), CH)
        total = pbuf[n, sum_place(kind)].astype(jnp.float32)
        for way in (0, 1):
            z_copy(n, kind, way).wait_recv()
            total += full_in[n, way].astype(jnp.float32)
        out_ref[:, cols] = (resv[:, cols].astype(jnp.float32) + total).astype(jnp.bfloat16)

    def near(q, r):
        return chunk(q + lax.div(q, 2), r)

    def step(work, r):
        @pl.when((r >= 0) & (r < SHARED))
        def _():
            @pl.loop(0, 3)
            def _(q):
                work(near(q, r), lax.rem(r, 2))

        @pl.when((r >= 3) & (r < 7))
        def _():
            work(common(r - 3), lax.rem(r - 3, 2))

        @pl.when((r >= 1) & (r <= SHARED))
        def _():
            work(chunk(2, r - 1), lax.rem(r - 1, 2))

    start_y(0, chunk(0, 0))
    start_y(1, chunk(0, 1))
    pass_on(0, chunk(0, 0))
    pass_on(1, chunk(0, 1))
    start_a(0)
    start_a(1)
    first(0)
    first(1)
    start_a(2)
    start_y(2, chunk(0, 2))
    start_y(3, chunk(0, 3))
    start_a(3)
    own_a.wait()
    own_b.wait()
    own_w.wait()
    own_res.wait()

    def multiply_near(r):
        @pl.loop(0, 3)
        def _(q):
            n = near(q, r)
            c_land(n, r, lax.rem(3 - q, 3)).wait_recv()
            multiply(n, lax.rem(r, 2))

    @pl.loop(0, SHARED + 4)
    def _(r):
        @pl.when(r < SHARED)
        def _():
            for way in (0, 1):
                x_land(r, way).wait_recv()
                f_copy(r, way).start()
                c_copy(r, 1 + way).start()

        @pl.when(r == 0)
        def _():
            pass_on(2, chunk(0, 2))
            pass_on(3, chunk(0, 3))

        @pl.when((r >= 1) & (r + 3 < SHARED))
        def _():
            pass_on(r + 3, chunk(0, r + 3))

        @pl.when(r + 2 < SHARED)
        def _():
            first(r + 2)

        @pl.when(r == 0)
        def _():
            start_y(4, chunk(0, 4))
            start_y(5, chunk(0, 5))

        @pl.when(r < 4)
        def _():
            start_y(SHARED + r, common(r))

        @pl.when(r == 1)
        def _():
            for g in range(4):
                for k in range(3):
                    for kind in (0, 1):
                        part = ag.at[kind, k + 1, g]
                        remote(part, part, a_s.at[kind, g, k], a_r.at[kind, g, k], at(z, y + 1, x, c)).wait_recv()
            multiply_near(0)

        @pl.when(r >= 2)
        def _():
            step(combine, r - 1)

        @pl.when((r >= 1) & (r < SHARED))
        def _():
            multiply_near(r)

        @pl.when((r >= 1) & (r <= SHARED))
        def _():
            for way in (0, 1):
                f_land(r - 1, way).wait_recv()
            c_copy(r - 1, 3).start()

        @pl.when((r >= 1) & (r < 5))
        def _():
            pass_on(SHARED + r - 1, common(r - 1))

        @pl.when((r >= 2) & (r < 6))
        def _():
            for way in (0, 1):
                g_copy(SHARED + r - 2, common(r - 2), way).wait_recv()
            v_copy(r - 2).start()

        @pl.when((r >= 3) & (r < 7))
        def _():
            v_land(r - 3).wait_recv()
            multiply(common(r - 3), lax.rem(r - 3, 2))

        @pl.when((r >= 1) & (r <= SHARED))
        def _():
            c_land(chunk(2, r - 1), r - 1, 3).wait_recv()
            multiply(chunk(2, r - 1), lax.rem(r - 1, 2))

        @pl.when(r == 2)
        def _():
            @pl.loop(0, 3)
            def _(q):
                combine(near(q, 0), 0)

        @pl.when(r >= 3)
        def _():
            step(finish, r - 3)

    for g in range(4):
        for e in (1, 2, 3):
            for kind in (0, 1):
                a_copy(kind, g, e).wait_send()

    @pl.loop(0, SHARED)
    def _(r):
        for way in (0, 1):
            y_copy(r, chunk(0, r), way).wait_send()
            g_copy(r, chunk(0, r), way).wait_send()
            x_copy(r, way).wait_send()
            f_copy(r, way).wait_send()
        for q in range(4):
            c_copy(r, q).wait_send()

    @pl.loop(0, 4)
    def _(u):
        for way in (0, 1):
            y_copy(SHARED + u, common(u), way).wait_send()
            g_copy(SHARED + u, common(u), way).wait_send()
        v_copy(u).wait_send()

    @pl.loop(0, 4 * ROUNDS)
    def _(n):
        for way in (0, 1):
            h_copy(n, 0, way).wait_send()
            z_copy(n, 0, way).wait_send()


def project(attn_out, w_out, residual):
    dma = pltpu.SemaphoreType.DMA
    anywhere = pl.BlockSpec(memory_space=pl.ANY)
    return pl.pallas_call(
        project_kernel,
        name="project",
        out_shape=jax.ShapeDtypeStruct((128, 7168), jnp.bfloat16),
        in_specs=[anywhere] * 3,
        out_specs=pl.BlockSpec(memory_space=VMEM),
        scratch_shapes=[
            VMEM((2, 4, 4, 128, 512), jnp.bfloat16),
            VMEM((512, 7168), jnp.bfloat16),
            VMEM((28, 3, 512, CH), jnp.bfloat16),
            VMEM((28, 4, 128, CH), jnp.bfloat16),
            VMEM((28, 2, 64, CH), jnp.bfloat16),
            VMEM((28, 2, 128, CH), jnp.bfloat16),
            VMEM((128, 7168), jnp.bfloat16),
            dma((4,)), dma((2, 4, 3)), dma((2, 4, 3)), dma((10, 2)), dma((10, 2)), dma((10, 2)), dma((10, 2)),
            dma((4,)), dma((4,)), dma((6, 2)), dma((6, 2)), dma((6, 2)), dma((6, 2)), dma((6, 4)), dma((6, 4)),
            dma((28, 2)), dma((28, 2)), dma((28, 2)), dma((28, 2)),
        ],
        compiler_params=pltpu.CompilerParams(
            collective_id=0, has_side_effects=True, vmem_limit_bytes=58 * 1024 * 1024
        ),
    )(attn_out.reshape(4, 4, 128, 512), w_out, residual)


LANE = 896
GROUPS = ((0, 0), (1, 1), (2, 3), (3, 2))


def moe_kernel(
    hid_ref, gain_ref, rout_ref, cho_ref, wg_ref, wu_ref, wd_ref,
    back_ref, coeff_ref, count_ref,
    wg, wu, wd, rt, normed, gain, snd, land, rows, ybuf, r1, sbuf, half_in, full_in, rsend, ret, cnt, cnt_tp, cnt_ep,
    loc, d_s, d_r, ax_s, ax_r, af_s, af_r, ac_s, ac_r, k_s, k_r, l_s, l_r, rt_s, rt_r, rs_s, rs_r,
    p_s, p_r, h_s, h_r, q_s, q_r, b_s, b_r,
):
    z, y, x, c = place()
    tp = z * 4 + y
    ep = x * 2 + c
    sib = at(z, y, x, c + 1)
    width = hid_ref.shape[1]
    half = pl.ds(pl.multiple_of(c * (width // 2), width // 2), width // 2)
    loads = [pltpu.make_async_copy(s, d, loc.at[i]) for i, (s, d) in enumerate(((wg_ref, wg), (wu_ref, wu), (wd_ref, wd)))]
    for load in loads:
        load.start()
    tp_peers = [(dz, dy) for dz in (0, 1, 3, 2) for dy in (1, 3, 2, 0) if (dz, dy) != (0, 0)]
    ep_peers = [(dx, dc) for dx in (0, 1, 3, 2) for dc in (0, 1) if (dx, dc) != (0, 0)]

    def tp_at(dz, dy):
        return ring(z + dz) * 4 + ring(y + dy)

    def ep_at(dx, dc):
        return ring(x + dx) * 2 + lax.rem(c + dc, 2)

    barrier = pltpu.get_barrier_semaphore()
    for p in tp_peers:
        pl.semaphore_signal(barrier, inc=1, device_id=(tp_at(*p), ep), device_id_type=MESH)
    for p in ep_peers:
        pl.semaphore_signal(barrier, inc=1, device_id=(tp, ep_at(*p)), device_id_type=MESH)

    def cut(j):
        return slice(j * LANE, (j + 1) * LANE)

    row = lax.broadcasted_iota(jnp.int32, (256, 128), 0)
    lane = lax.broadcasted_iota(jnp.int32, (256, 128), 1)
    expert = row // 16
    member = jnp.zeros((256, 128), jnp.float32)
    named = jnp.zeros((256, 128), jnp.float32)
    for k in range(TOP):
        ck = cho_ref[k : k + 1, :]
        member += jnp.where(ck == expert, 1.0, 0.0)
        named += jnp.where(ck == row, 1.0, 0.0)
    before = jnp.where(row[:128] < lane[:128], 1.0, 0.0).astype(jnp.bfloat16)
    rank = jnp.dot(member.astype(jnp.bfloat16), before, preferred_element_type=jnp.float32)
    slot = ((row // 8) % 2).astype(jnp.float32)
    pick = jnp.where(rank == slot, member, 0.0)
    feature = row % 8
    picked = jnp.zeros((256, LANE), jnp.float32)
    for j in range(8):
        pj = jnp.where(feature == j, pick, 0.0).astype(jnp.bfloat16)
        picked += jnp.dot(pj, hid_ref[:, cut(j)], preferred_element_type=jnp.float32)
    gains = gain_ref[...].astype(jnp.float32)
    for j in range(8):
        for i in range(7):
            gain[j : j + 1, i * 128 : (i + 1) * 128] = gains[j * 7 + i : j * 7 + i + 1, :]
    picked = picked.reshape(32, 8, LANE)
    ssq = jnp.sum(jnp.sum(picked * picked, axis=2, keepdims=True), axis=1, keepdims=True)
    outgoing = picked * lax.rsqrt(ssq / width + norm_eps) * gain[...][None]
    snd[...] = outgoing.astype(jnp.bfloat16).reshape(16, 16, LANE)
    contract_last = (((1,), (1,)), ((), ()))
    cnt[...] = lax.dot_general(
        jnp.ones((8, 128), jnp.bfloat16), named.astype(jnp.bfloat16), contract_last, preferred_element_type=jnp.float32
    )
    pl.semaphore_wait(barrier, len(tp_peers) + len(ep_peers))

    def d_copy(p):
        peer = tp_at(*p)
        return remote(snd.at[peer], land.at[ep, tp], d_s.at[peer], d_r.at[tp], (peer, ep))

    own_rows = pltpu.make_async_copy(snd.at[tp], land.at[ep, tp], loc.at[3])
    own_rows.start()
    for p in tp_peers:
        d_copy(p).start()

    def k_copy(p):
        peer = tp_at(*p)
        return remote(cnt, cnt_tp.at[tp], k_s.at[peer], k_r.at[tp], (peer, ep))

    for p in tp_peers:
        k_copy(p).start()

    def group(dz):
        return pl.ds(pl.multiple_of(ring(z + dz) * 4, 4), 4)

    def x_copy(g, dz, way):
        part = land.at[ep, group(dz)]
        return remote(part, part, ax_s.at[g, way], ax_r.at[g, way], (tp, ep_at(1 - 2 * way, 0)))

    def x_land(g, dz, way):
        part = land.at[ep_at(2 * way - 1, 0), group(dz)]
        return remote(part, part, ax_s.at[g, way], ax_r.at[g, way], (tp, ep_at(1, 0)))

    def f_rows(dx, dz, way):
        return land.at[ep_at(dx, 0), pl.ds(pl.multiple_of(ring(z + dz) * 4 + 2 * way, 2), 2)]

    def f_copy(g, dz, way):
        part = f_rows(2 * way - 1, dz, way)
        return remote(part, part, af_s.at[g, way], af_r.at[g, way], (tp, ep_at(1 - 2 * way, 0)))

    def f_land(g, dz, way):
        part = f_rows(2, dz, way)
        return remote(part, part, af_s.at[g, way], af_r.at[g, way], (tp, ep_at(1, 0)))

    def c_copy(g, dz, q):
        part = land.at[ep_at(q, 0), group(dz)]
        return remote(part, part, ac_s.at[g, q], ac_r.at[g, q], sib)

    def c_land(g, dz, q):
        part = land.at[ep_at(q, 1), group(dz)]
        return remote(part, part, ac_s.at[g, q], ac_r.at[g, q], sib)

    def d_land(p):
        src = tp_at(*p)
        return remote(snd.at[src], land.at[ep, src], d_s.at[src], d_r.at[src], (src, ep))

    for g, dz in GROUPS:
        for p in tp_peers:
            if p[0] == dz:
                d_land(p).wait_recv()
        if dz == 0:
            own_rows.wait()
        for way in (0, 1):
            x_copy(g, dz, way).start()
        c_copy(g, dz, 0).start()

    def rt_copy(p):
        peer = tp_at(*p)
        return remote(rout_ref.at[:, half], rt.at[tp, :, half], rt_s.at[peer], rt_r.at[tp], (peer, ep))

    own_rt = pltpu.make_async_copy(rout_ref.at[:, half], rt.at[tp, :, half], loc.at[4])
    own_rt.start()
    for p in tp_peers:
        rt_copy(p).start()

    for p in tp_peers:
        src = tp_at(*p)
        remote(cnt, cnt_tp.at[src], k_s.at[src], k_r.at[src], (src, ep)).wait_recv()
    cnt_tp[tp] = cnt[...]
    part_sum = cnt_tp[0]
    for i in range(1, 16):
        part_sum += cnt_tp[i]
    cnt_ep[ep] = part_sum

    def l_copy(p):
        peer = ep_at(*p)
        return remote(cnt_ep.at[ep], cnt_ep.at[ep], l_s.at[peer], l_r.at[ep], (tp, peer))

    for p in ep_peers:
        l_copy(p).start()

    out_row = lax.broadcasted_iota(jnp.int32, (128, 128), 0)
    in_row = lax.broadcasted_iota(jnp.int32, (128, 128), 1)
    source = ((out_row % 16) // 2) * 16 + (out_row % 2) * 8 + out_row // 16
    perm = jnp.where(in_row == source, 1.0, 0.0).astype(jnp.bfloat16)

    def turn_rows(group_of):
        for part in range(2):
            block = land[group_of, part * 8 : part * 8 + 8].reshape(128, LANE)
            turned = jnp.dot(perm, block, preferred_element_type=jnp.float32).astype(jnp.bfloat16)
            to = pl.ds(pl.multiple_of(group_of * 32 + part * 16, 16), 16)
            rows[:, to, :] = turned.reshape(8, 16, LANE)

    turn_rows(ep)
    for g, dz in GROUPS:
        for way in (0, 1):
            x_land(g, dz, way).wait_recv()
            f_copy(g, dz, way).start()
            c_copy(g, dz, 3 - 2 * way).start()
    for q in (0, 3, 1):
        if q:
            turn_rows(ep_at(q, 0))
        if q == 1:
            for g, dz in GROUPS:
                for way in (0, 1):
                    f_land(g, dz, way).wait_recv()
                c_copy(g, dz, 2).start()
        for g, dz in GROUPS:
            c_land(g, dz, q).wait_recv()
        turn_rows(ep_at(q, 1))
    turn_rows(ep_at(2, 0))
    for g, dz in GROUPS:
        c_land(g, dz, 2).wait_recv()
    turn_rows(ep_at(2, 1))

    for load in loads:
        load.wait()
    gate_val = jnp.zeros((256, 256), jnp.float32)
    up_val = jnp.zeros((256, 256), jnp.float32)
    for j in range(8):
        gate_val += jnp.dot(rows[j], wg[cut(j), :], preferred_element_type=jnp.float32)
        up_val += jnp.dot(rows[j], wu[cut(j), :], preferred_element_type=jnp.float32)
    active = (gate_val / (1.0 + jnp.exp(-gate_val)) * up_val).astype(jnp.bfloat16)

    def p_copy(n):
        return remote(ybuf.at[n, :, 1 - c], r1.at[n], p_s.at[n], p_r.at[n], sib)

    def h_copy(n, way):
        rows_of = pl.ds(16 * way, 16)
        return remote(
            sbuf.at[n, ring(x + 2), rows_of], half_in.at[n, way],
            h_s.at[n, way], h_r.at[n, way], (tp, ep_at(1 - 2 * way, 0)),
        )

    def q_copy(n, way):
        to = 1 - 2 * way
        return remote(
            sbuf.at[n, ring(x + to)], full_in.at[n, way], q_s.at[n, way], q_r.at[n, way], (tp, ep_at(to, 0))
        )

    def forward(n):
        for way in (0, 1):
            to = ring(x + 1 - 2 * way)
            h_copy(n, way).wait_recv()
            rows_of = slice(16 * way, 16 * way + 16)
            both = sbuf[n, to, rows_of].astype(jnp.float32) + half_in[n, way].astype(jnp.float32)
            sbuf[n, to, rows_of] = both.astype(jnp.bfloat16)
            q_copy(n, way).start()

    for n in range(4):
        part = jnp.dot(active, wd[:, n * 2 * LANE : (n + 1) * 2 * LANE], preferred_element_type=jnp.float32)
        ybuf[n] = part.astype(jnp.bfloat16).reshape(4, 2, 32, 2 * LANE)
        p_copy(n).start()
    for n in range(4):
        p_copy(n).wait_recv()
        for i in range(4):
            both = ybuf[n, i, c].astype(jnp.float32) + r1[n, i].astype(jnp.float32)
            sbuf[n, i] = both.astype(jnp.bfloat16)
        for way in (0, 1):
            h_copy(n, way).start()
        if n:
            forward(n - 1)
    forward(3)

    for p in ep_peers:
        peer = ep_at(*p)
        remote(cnt_ep.at[peer], cnt_ep.at[peer], l_s.at[peer], l_r.at[peer], (tp, peer)).wait_recv()
    counts = cnt_ep[0]
    for i in range(1, 8):
        counts += cnt_ep[i]
    count_ref[...] = counts

    for p in tp_peers:
        src = tp_at(*p)
        remote(rout_ref.at[:, half], rt.at[src, :, half], rt_s.at[src], rt_r.at[src], (src, ep)).wait_recv()
    own_rt.wait()
    mine = rt.at[:, :, half]
    rt_sib = remote(mine, mine, rs_s.at[0], rs_r.at[0], sib)
    rt_sib.start()
    other = rt.at[:, :, pl.ds(pl.multiple_of((1 - c) * (width // 2), width // 2), width // 2)]
    ssq = jnp.zeros((128, 1), jnp.float32)
    for j in range(8):
        h = hid_ref[:, cut(j)].astype(jnp.float32)
        ssq += jnp.sum(h * h, axis=1, keepdims=True)
    scale = lax.rsqrt(ssq / width + norm_eps)
    for j in range(8):
        h = hid_ref[:, cut(j)].astype(jnp.float32)
        normed[:, cut(j)] = (h * scale * gain[j : j + 1, :]).astype(jnp.bfloat16)
    remote(other, other, rs_s.at[0], rs_r.at[0], sib).wait_recv()
    logits = jnp.zeros((256, 128), jnp.float32)
    for j in range(8):
        logits += lax.dot_general(
            rt[:, :, cut(j)].reshape(256, LANE), normed[:, cut(j)], contract_last, preferred_element_type=jnp.float32
        )
    scores = 1.0 / (1.0 + jnp.exp(-logits))
    chosen = []
    for k in range(TOP):
        hit = cho_ref[k : k + 1, :] == row
        chosen.append(jnp.sum(jnp.where(hit, scores, 0.0), axis=0, keepdims=True))
    norm_by = chosen[0]
    for k in range(1, TOP):
        norm_by = norm_by + chosen[k]
    weight = jnp.zeros((256, 128), jnp.float32)
    for k in range(TOP):
        weight += jnp.where(cho_ref[k : k + 1, :] == expert, route_scale * chosen[k] / norm_by, 0.0)
    coeff_ref[...] = jnp.where(pick > 0.0, weight, 0.0).T

    back_row = lax.broadcasted_iota(jnp.int32, (256, 32), 0)
    back_col = lax.broadcasted_iota(jnp.int32, (256, 32), 1)
    returned = jnp.zeros((256, LANE), jnp.float32)
    for n in range(4):
        total = sbuf[n, x].astype(jnp.float32)
        for way in (0, 1):
            q_copy(n, way).wait_recv()
            total += full_in[n, way].astype(jnp.float32)
        total = total.astype(jnp.bfloat16)
        for i in range(2):
            turn = jnp.where((back_row // 8 == back_col) & (back_row % 8 == 2 * n + i), 1.0, 0.0).astype(jnp.bfloat16)
            returned += jnp.dot(turn, total[:, cut(i)], preferred_element_type=jnp.float32)
    rsend[...] = returned.astype(jnp.bfloat16).reshape(16, 16, LANE)

    def b_copy(p):
        peer = tp_at(*p)
        return remote(rsend.at[peer], ret.at[tp], b_s.at[peer], b_r.at[tp], (peer, ep))

    own_back = pltpu.make_async_copy(rsend.at[tp], ret.at[tp], loc.at[5])
    own_back.start()
    for p in tp_peers:
        b_copy(p).start()
    own_back.wait()
    for p in tp_peers:
        src = tp_at(*p)
        remote(rsend.at[src], ret.at[src], b_s.at[src], b_r.at[src], (src, ep)).wait_recv()
    back_ref[...] = ret[...]

    for p in tp_peers:
        d_copy(p).wait_send()
        k_copy(p).wait_send()
        rt_copy(p).wait_send()
        b_copy(p).wait_send()
    for p in ep_peers:
        l_copy(p).wait_send()
    rt_sib.wait_send()
    for g, dz in GROUPS:
        for way in (0, 1):
            x_copy(g, dz, way).wait_send()
            f_copy(g, dz, way).wait_send()
        for q in range(4):
            c_copy(g, dz, q).wait_send()
    for n in range(4):
        p_copy(n).wait_send()
        for way in (0, 1):
            h_copy(n, way).wait_send()
            q_copy(n, way).wait_send()


def mix_kernel(hid_ref, back_ref, coeff_ref, count_ref, bias_ref, kept_ref, moe_ref, load_ref, next_ref):
    i = pl.program_id(0)
    kept_ref[...] = hid_ref[...]

    @pl.when(i == 0)
    def _():
        slots = 128.0 * 128.0 * TOP
        for k in range(2):
            counts = count_ref[0:1, k * 128 : (k + 1) * 128]
            load_ref[k : k + 1, :] = counts * 256.0 / slots
            gap = slots - counts * 256.0
            sign = jnp.where(gap > 0.0, 1.0, jnp.where(gap < 0.0, -1.0, 0.0))
            next_ref[k : k + 1, :] = bias_ref[k : k + 1, :] + bias_rate * sign

    back = back_ref[...].reshape(256, LANE)
    coeff = coeff_ref[...]
    high = coeff.astype(jnp.bfloat16).astype(jnp.float32)
    low = coeff - high
    lane_cut = lax.broadcasted_iota(jnp.int32, (128, 256), 1) % 8
    for k in range(2):
        here = lane_cut == 2 * i + k
        mixed = jnp.dot(jnp.where(here, high, 0.0).astype(jnp.bfloat16), back, preferred_element_type=jnp.float32)
        mixed += jnp.dot(jnp.where(here, low, 0.0).astype(jnp.bfloat16), back, preferred_element_type=jnp.float32)
        moe_ref[:, k * LANE : (k + 1) * LANE] = mixed.astype(jnp.bfloat16)


def experts(hidden_out, norm_gain, router, router_bias, choices, w_gate, w_up, w_down):
    dma = pltpu.SemaphoreType.DMA
    bf16, f32 = jnp.bfloat16, jnp.float32
    vmem = pl.BlockSpec(memory_space=VMEM)
    anywhere = pl.BlockSpec(memory_space=pl.ANY)
    back, coeff, counts = pl.pallas_call(
        moe_kernel,
        name="experts",
        out_shape=(
            jax.ShapeDtypeStruct((16, 16, LANE), bf16),
            jax.ShapeDtypeStruct((128, 256), f32),
            jax.ShapeDtypeStruct((8, 256), f32),
        ),
        in_specs=[vmem] * 4 + [anywhere] * 3,
        out_specs=(vmem,) * 3,
        scratch_shapes=[
            VMEM((7168, 256), bf16), VMEM((7168, 256), bf16), VMEM((256, 7168), bf16),
            VMEM((16, 16, 7168), bf16), VMEM((128, 7168), bf16), VMEM((8, LANE), f32), VMEM((16, 16, LANE), bf16),
            VMEM((8, 16, 16, LANE), bf16), VMEM((8, 256, LANE), bf16),
            VMEM((4, 4, 2, 32, 2 * LANE), bf16), VMEM((4, 4, 32, 2 * LANE), bf16),
            VMEM((4, 4, 32, 2 * LANE), bf16), VMEM((4, 2, 16, 2 * LANE), bf16), VMEM((4, 2, 32, 2 * LANE), bf16),
            VMEM((16, 16, LANE), bf16), VMEM((16, 16, LANE), bf16),
            VMEM((8, 256), f32), VMEM((16, 8, 256), f32), VMEM((8, 8, 256), f32),
            dma((6,)), dma((16,)), dma((16,)), dma((4, 2)), dma((4, 2)), dma((4, 2)), dma((4, 2)), dma((4, 4)), dma((4, 4)),
            dma((16,)), dma((16,)), dma((8,)), dma((8,)), dma((16,)), dma((16,)), dma((1,)), dma((1,)),
            dma((4,)), dma((4,)), dma((4, 2)), dma((4, 2)), dma((4, 2)), dma((4, 2)), dma((16,)), dma((16,)),
        ],
        compiler_params=pltpu.CompilerParams(
            collective_id=1, has_side_effects=True, vmem_limit_bytes=56 * 1024 * 1024
        ),
    )(
        hidden_out, norm_gain.reshape(-1, 128), router.T, choices.T,
        w_gate[0], w_up[0], w_down[0],
    )
    block = pl.BlockSpec((128, 2 * LANE), lambda i: (0, i))
    hidden_kept, moe_out, load, bias_next = pl.pallas_call(
        mix_kernel,
        name="mix",
        grid=(4,),
        out_shape=(
            jax.ShapeDtypeStruct((128, 7168), bf16),
            jax.ShapeDtypeStruct((128, 7168), bf16),
            jax.ShapeDtypeStruct((2, 128), f32),
            jax.ShapeDtypeStruct((2, 128), f32),
        ),
        in_specs=[block] + [vmem] * 4,
        out_specs=(block, block, vmem, vmem),
    )(hidden_out, back, coeff, counts, router_bias.reshape(2, 128))
    return hidden_kept, moe_out, load.reshape(-1), bias_next.reshape(-1)


def on_device(
    attn_out, residual, w_out, norm_gain, router, router_bias, choices, w_gate, w_up, w_down
):
    hidden_out = project(attn_out, w_out, residual)
    return experts(hidden_out, norm_gain, router, router_bias, choices, w_gate, w_up, w_down)


def solution(mesh):
    placed = (
        P("ep", "tp"),
        P(("ep", "tp"), None),
        P("tp", None),
        P(),
        P(None, "tp"),
        P(),
        P(("ep", "tp"), None),
        P("tp", None, "ep"),
        P("tp", None, "ep"),
        P("tp", "ep", None),
    )
    return jax.shard_map(
        on_device,
        mesh=mesh,
        in_specs=placed,
        out_specs=(P(("ep", "tp"), None), P(("ep", "tp"), None), P(), P()),
        check_vma=False,
    )
```

```python
import jax
import jax.numpy as jnp
from jax import lax
from jax.experimental import pallas as pl
from jax.experimental.pallas import tpu as pltpu
from jax.sharding import PartitionSpec as P

TOP = 8


norm_eps = 1e-06
route_scale = 2.5
bias_rate = 0.001


MESH = pl.DeviceIdType.MESH
VMEM = pltpu.VMEM
ROUNDS = 7
SHARED = 5
CH = 256


def ring(i):
    return lax.rem(i + 8, 4)


def place():
    tp = lax.axis_index("tp")
    ep = lax.axis_index("ep")
    return lax.div(tp, 4), lax.rem(tp, 4), lax.div(ep, 2), lax.rem(ep, 2)


def at(z, y, x, c):
    return (ring(z) * 4 + ring(y), ring(x) * 2 + lax.rem(c, 2))


def greet(peers):
    barrier = pltpu.get_barrier_semaphore()
    for peer in peers:
        pl.semaphore_signal(barrier, inc=1, device_id=peer, device_id_type=MESH)
    pl.semaphore_wait(barrier, len(peers))


def remote(src, dst, send, recv, peer):
    return pltpu.make_async_remote_copy(
        src_ref=src, dst_ref=dst, send_sem=send, recv_sem=recv, device_id=peer, device_id_type=MESH
    )


def project_kernel(
    a_ref, w_ref, res_ref, out_ref,
    ag, wown, wbuf, pbuf, half_in, full_in, resv,
    loc, a_s, a_r, y_s, y_r, g_s, g_r, v_s, v_r, x_s, x_r, f_s, f_r, c_s, c_r, h_s, h_r, z_s, z_r,
):
    z, y, x, c = place()
    half = pl.multiple_of(c * 256, 256)
    own_a = pltpu.make_async_copy(a_ref.at[:, y], ag.at[0, 0], loc.at[0])
    own_b = pltpu.make_async_copy(a_ref.at[z], ag.at[1, 0], loc.at[3])
    own_w = pltpu.make_async_copy(w_ref, wown, loc.at[1])
    own_res = pltpu.make_async_copy(res_ref, resv, loc.at[2])
    own_a.start()
    own_b.start()
    own_w.start()
    own_res.start()
    greet(
        [at(z, y + e, x, c) for e in (1, 2, 3)]
        + [at(z + e, y, x, c) for e in (1, 2, 3)]
        + [at(z, y, x + 1, c), at(z, y, x - 1, c), at(z, y, x, c + 1)]
    )
    sib = at(z, y, x, c + 1)

    def gather_at(kind, i):
        return at(z + i * kind, y + i * (1 - kind), x, c)

    def sum_at(kind, i):
        return at(z + i * (1 - kind), y + i * kind, x, c)

    def sum_place(kind):
        return z * (1 - kind) + y * kind

    def chunk(dx, r):
        return ring(x + dx) * ROUNDS + r

    def y_copy(i, n, way):
        cols = pl.ds(pl.multiple_of(n * CH, CH), CH)
        return remote(
            w_ref.at[pl.ds(half, 256), cols], wbuf.at[n, 2 - 2 * way, pl.ds(half, 256), :],
            y_s.at[i, way], y_r.at[i, way], gather_at(lax.rem(i, 2), 1 - 2 * way),
        )

    def y_land(i, n, way):
        part = wbuf.at[n, 2 - 2 * way, pl.ds(half, 256), :]
        return remote(part, part, y_s.at[i, way], y_r.at[i, way], at(z, y + 1, x, c))

    def g_copy(i, n, way):
        rows = pl.ds(pl.multiple_of(half + 128 * way, 128), 128)
        return remote(
            wbuf.at[n, 2 - 2 * way, rows, :], wbuf.at[n, 1, rows, :],
            g_s.at[i, way], g_r.at[i, way], gather_at(lax.rem(i, 2), 1 - 2 * way),
        )

    def common(u):
        return lax.div(u, 2) * ROUNDS + SHARED + lax.rem(u, 2)

    def v_copy(u):
        part = wbuf.at[common(u), :, pl.ds(half, 256), :]
        return remote(part, part, v_s.at[u], v_r.at[u], sib)

    def v_land(u):
        part = wbuf.at[common(u), :, pl.ds(pl.multiple_of(256 - half, 256), 256), :]
        return remote(part, part, v_s.at[u], v_r.at[u], sib)

    def a_copy(kind, g, e):
        rows = a_ref.at[ring(z + e), g] if kind else a_ref.at[g, ring(y + e)]
        return remote(
            rows, ag.at[kind, 4 - e, g], a_s.at[kind, g, e - 1], a_r.at[kind, g, 3 - e], gather_at(kind, e)
        )

    def x_copy(r, way):
        part = wbuf.at[chunk(0, r), :, pl.ds(half, 256), :]
        return remote(part, part, x_s.at[r, way], x_r.at[r, way], at(z, y, x + 1 - 2 * way, c))

    def x_land(r, way):
        part = wbuf.at[chunk(2 * way - 1, r), :, pl.ds(half, 256), :]
        return remote(part, part, x_s.at[r, way], x_r.at[r, way], at(z, y, x + 1 - 2 * way, c))

    def f_part(dx, r, way):
        return wbuf.at[chunk(dx, r), :, pl.ds(pl.multiple_of(half + 128 * way, 128), 128), :]

    def f_copy(r, way):
        part = f_part(2 * way - 1, r, way)
        return remote(part, part, f_s.at[r, way], f_r.at[r, way], at(z, y, x + 1 - 2 * way, c))

    def f_land(r, way):
        part = f_part(2, r, way)
        return remote(part, part, f_s.at[r, way], f_r.at[r, way], at(z, y, x + 1 - 2 * way, c))

    def hop(q):
        return (0, 3, 1, 2)[q]

    def c_copy(r, q):
        part = wbuf.at[chunk(hop(q), r), :, pl.ds(half, 256), :]
        return remote(part, part, c_s.at[r, q], c_r.at[r, q], sib)

    def c_land(n, r, q):
        other = pl.multiple_of(256 - half, 256)
        part = wbuf.at[n, :, pl.ds(other, 256), :]
        return remote(part, part, c_s.at[r, q], c_r.at[r, q], sib)

    def halves(way):
        return pl.ds(64 * way, 64)

    def h_copy(n, kind, way):
        return remote(
            pbuf.at[n, ring(sum_place(kind) + 2), halves(way)], half_in.at[n, way],
            h_s.at[n, way], h_r.at[n, way], sum_at(kind, 1 - 2 * way),
        )

    def z_copy(n, kind, way):
        return remote(
            pbuf.at[n, ring(sum_place(kind) + 1 - 2 * way)], full_in.at[n, way],
            z_s.at[n, way], z_r.at[n, way], sum_at(kind, 1 - 2 * way),
        )

    def start_y(i, n):
        for way in (0, 1):
            y_copy(i, n, way).start()

    def start_a(g):
        for e in (2, 1, 3):
            for kind in (0, 1):
                a_copy(kind, g, e).start()

    def pass_on(i, n):
        for way in (0, 1):
            y_land(i, n, way).wait_recv()
            g_copy(i, n, way).start()

    def first(r):
        for way in (0, 1):
            g_copy(r, chunk(0, r), way).wait_recv()
        x_copy(r, 0).start()
        x_copy(r, 1).start()
        c_copy(r, 0).start()

    def multiply(n, kind):
        cols = pl.ds(pl.multiple_of(n * CH, CH), CH)
        total = jnp.dot(ag[kind, 0].reshape(512, 512), wown[:, cols], preferred_element_type=jnp.float32)
        for k in range(3):
            total += jnp.dot(ag[kind, k + 1].reshape(512, 512), wbuf[n, k], preferred_element_type=jnp.float32)
        pbuf[n] = total.astype(jnp.bfloat16).reshape(4, 128, CH)
        for way in (0, 1):
            h_copy(n, kind, way).start()

    def combine(n, kind):
        for way in (0, 1):
            to = ring(sum_place(kind) + 1 - 2 * way)
            h_copy(n, kind, way).wait_recv()
            both = pbuf[n, to, halves(way)].astype(jnp.float32) + half_in[n, way].astype(jnp.float32)
            pbuf[n, to, halves(way)] = both.astype(jnp.bfloat16)
            z_copy(n, kind, way).start()

    def finish(n, kind):
        cols = pl.ds(pl.multiple_of(n * CH, CH), CH)
        total = pbuf[n, sum_place(kind)].astype(jnp.float32)
        for way in (0, 1):
            z_copy(n, kind, way).wait_recv()
            total += full_in[n, way].astype(jnp.float32)
        out_ref[:, cols] = (resv[:, cols].astype(jnp.float32) + total).astype(jnp.bfloat16)

    def near(q, r):
        return chunk(q + lax.div(q, 2), r)

    def step(work, r):
        @pl.when((r >= 0) & (r < SHARED))
        def _():
            @pl.loop(0, 3)
            def _(q):
                work(near(q, r), lax.rem(r, 2))

        @pl.when((r >= 2) & (r < 6))
        def _():
            for k in (0, 1):
                work(common(2 * r - 4 + k), 1 - k)

        @pl.when((r >= 1) & (r <= SHARED))
        def _():
            work(chunk(2, r - 1), lax.rem(r - 1, 2))

    start_y(0, chunk(0, 0))
    start_y(1, chunk(0, 1))
    pass_on(0, chunk(0, 0))
    pass_on(1, chunk(0, 1))
    start_a(0)
    start_a(1)
    first(0)
    first(1)
    start_a(2)
    start_y(2, chunk(0, 2))
    start_y(3, chunk(0, 3))
    start_a(3)
    own_a.wait()
    own_b.wait()
    own_w.wait()
    own_res.wait()

    def multiply_near(r):
        @pl.loop(0, 3)
        def _(q):
            n = near(q, r)
            c_land(n, r, lax.rem(3 - q, 3)).wait_recv()
            multiply(n, lax.rem(r, 2))

    @pl.loop(0, SHARED + 4)
    def _(r):
        @pl.when(r < SHARED)
        def _():
            for way in (0, 1):
                x_land(r, way).wait_recv()
                f_copy(r, way).start()
                c_copy(r, 1 + way).start()

        @pl.when(r == 0)
        def _():
            pass_on(2, chunk(0, 2))
            pass_on(3, chunk(0, 3))

        @pl.when((r >= 1) & (r + 3 < SHARED))
        def _():
            pass_on(r + 3, chunk(0, r + 3))

        @pl.when(r + 2 < SHARED)
        def _():
            first(r + 2)

        @pl.when(r == 0)
        def _():
            start_y(4, chunk(0, 4))

        @pl.when(r < 4)
        def _():
            for k in (0, 1):
                start_y(SHARED + 2 * r + k, common(2 * r + k))

        @pl.when(r == 1)
        def _():
            for g in range(4):
                for k in range(3):
                    for kind in (0, 1):
                        part = ag.at[kind, k + 1, g]
                        remote(part, part, a_s.at[kind, g, k], a_r.at[kind, g, k], at(z, y + 1, x, c)).wait_recv()
            multiply_near(0)

        @pl.when(r >= 2)
        def _():
            step(combine, r - 1)

        @pl.when((r >= 1) & (r < SHARED))
        def _():
            multiply_near(r)

        @pl.when((r >= 1) & (r <= SHARED))
        def _():
            for way in (0, 1):
                f_land(r - 1, way).wait_recv()
            c_copy(r - 1, 3).start()

        @pl.when((r >= 1) & (r < 5))
        def _():
            for k in (0, 1):
                pass_on(SHARED + 2 * r - 2 + k, common(2 * r - 2 + k))

        @pl.when((r >= 2) & (r < 6))
        def _():
            for k in (0, 1):
                u = 2 * r - 4 + k
                for way in (0, 1):
                    g_copy(SHARED + u, common(u), way).wait_recv()
                v_copy(u).start()

        @pl.when((r >= 2) & (r < 6))
        def _():
            for k in (0, 1):
                u = 2 * r - 4 + k
                v_land(u).wait_recv()
                multiply(common(u), 1 - k)

        @pl.when((r >= 1) & (r <= SHARED))
        def _():
            c_land(chunk(2, r - 1), r - 1, 3).wait_recv()
            multiply(chunk(2, r - 1), lax.rem(r - 1, 2))

        @pl.when(r == 2)
        def _():
            @pl.loop(0, 3)
            def _(q):
                combine(near(q, 0), 0)

        @pl.when(r >= 3)
        def _():
            step(finish, r - 3)

    for g in range(4):
        for e in (1, 2, 3):
            for kind in (0, 1):
                a_copy(kind, g, e).wait_send()

    @pl.loop(0, SHARED)
    def _(r):
        for way in (0, 1):
            y_copy(r, chunk(0, r), way).wait_send()
            g_copy(r, chunk(0, r), way).wait_send()
            x_copy(r, way).wait_send()
            f_copy(r, way).wait_send()
        for q in range(4):
            c_copy(r, q).wait_send()

    @pl.loop(0, 8)
    def _(u):
        for way in (0, 1):
            y_copy(SHARED + u, common(u), way).wait_send()
            g_copy(SHARED + u, common(u), way).wait_send()
        v_copy(u).wait_send()

    @pl.loop(0, 4 * ROUNDS)
    def _(n):
        for way in (0, 1):
            h_copy(n, 0, way).wait_send()
            z_copy(n, 0, way).wait_send()


def project(attn_out, w_out, residual):
    dma = pltpu.SemaphoreType.DMA
    anywhere = pl.BlockSpec(memory_space=pl.ANY)
    return pl.pallas_call(
        project_kernel,
        name="project",
        out_shape=jax.ShapeDtypeStruct((128, 7168), jnp.bfloat16),
        in_specs=[anywhere] * 3,
        out_specs=pl.BlockSpec(memory_space=VMEM),
        scratch_shapes=[
            VMEM((2, 4, 4, 128, 512), jnp.bfloat16),
            VMEM((512, 7168), jnp.bfloat16),
            VMEM((28, 3, 512, CH), jnp.bfloat16),
            VMEM((28, 4, 128, CH), jnp.bfloat16),
            VMEM((28, 2, 64, CH), jnp.bfloat16),
            VMEM((28, 2, 128, CH), jnp.bfloat16),
            VMEM((128, 7168), jnp.bfloat16),
            dma((4,)), dma((2, 4, 3)), dma((2, 4, 3)), dma((13, 2)), dma((13, 2)), dma((13, 2)), dma((13, 2)),
            dma((8,)), dma((8,)), dma((5, 2)), dma((5, 2)), dma((5, 2)), dma((5, 2)), dma((5, 4)), dma((5, 4)),
            dma((28, 2)), dma((28, 2)), dma((28, 2)), dma((28, 2)),
        ],
        compiler_params=pltpu.CompilerParams(
            collective_id=0, has_side_effects=True, vmem_limit_bytes=58 * 1024 * 1024
        ),
    )(attn_out.reshape(4, 4, 128, 512), w_out, residual)


LANE = 896
GROUPS = ((0, 0), (1, 1), (2, 3), (3, 2))


def moe_kernel(
    hid_ref, gain_ref, rout_ref, cho_ref, wg_ref, wu_ref, wd_ref,
    back_ref, coeff_ref, count_ref,
    wg, wu, wd, rt, normed, gain, snd, land, rows, ybuf, r1, sbuf, half_in, full_in, rsend, ret, cnt, cnt_tp, cnt_ep,
    loc, d_s, d_r, ax_s, ax_r, af_s, af_r, ac_s, ac_r, k_s, k_r, l_s, l_r, rt_s, rt_r, rs_s, rs_r,
    p_s, p_r, h_s, h_r, q_s, q_r, b_s, b_r,
):
    z, y, x, c = place()
    tp = z * 4 + y
    ep = x * 2 + c
    sib = at(z, y, x, c + 1)
    width = hid_ref.shape[1]
    half = pl.ds(pl.multiple_of(c * (width // 2), width // 2), width // 2)
    loads = [pltpu.make_async_copy(s, d, loc.at[i]) for i, (s, d) in enumerate(((wg_ref, wg), (wu_ref, wu), (wd_ref, wd)))]
    for load in loads:
        load.start()
    tp_peers = [(dz, dy) for dz in (0, 1, 3, 2) for dy in (1, 3, 2, 0) if (dz, dy) != (0, 0)]
    ep_peers = [(dx, dc) for dx in (0, 1, 3, 2) for dc in (0, 1) if (dx, dc) != (0, 0)]

    def tp_at(dz, dy):
        return ring(z + dz) * 4 + ring(y + dy)

    def ep_at(dx, dc):
        return ring(x + dx) * 2 + lax.rem(c + dc, 2)

    barrier = pltpu.get_barrier_semaphore()
    for p in tp_peers:
        pl.semaphore_signal(barrier, inc=1, device_id=(tp_at(*p), ep), device_id_type=MESH)
    for p in ep_peers:
        pl.semaphore_signal(barrier, inc=1, device_id=(tp, ep_at(*p)), device_id_type=MESH)

    def cut(j):
        return slice(j * LANE, (j + 1) * LANE)

    row = lax.broadcasted_iota(jnp.int32, (256, 128), 0)
    lane = lax.broadcasted_iota(jnp.int32, (256, 128), 1)
    expert = row // 16
    member = jnp.zeros((256, 128), jnp.float32)
    named = jnp.zeros((256, 128), jnp.float32)
    for k in range(TOP):
        ck = cho_ref[k : k + 1, :]
        member += jnp.where(ck == expert, 1.0, 0.0)
        named += jnp.where(ck == row, 1.0, 0.0)
    before = jnp.where(row[:128] < lane[:128], 1.0, 0.0).astype(jnp.bfloat16)
    rank = jnp.dot(member.astype(jnp.bfloat16), before, preferred_element_type=jnp.float32)
    slot = ((row // 8) % 2).astype(jnp.float32)
    pick = jnp.where(rank == slot, member, 0.0)
    feature = row % 8
    picked = jnp.zeros((256, LANE), jnp.float32)
    for j in range(8):
        pj = jnp.where(feature == j, pick, 0.0).astype(jnp.bfloat16)
        picked += jnp.dot(pj, hid_ref[:, cut(j)], preferred_element_type=jnp.float32)
    gains = gain_ref[...].astype(jnp.float32)
    for j in range(8):
        for i in range(7):
            gain[j : j + 1, i * 128 : (i + 1) * 128] = gains[j * 7 + i : j * 7 + i + 1, :]
    picked = picked.reshape(32, 8, LANE)
    ssq = jnp.sum(jnp.sum(picked * picked, axis=2, keepdims=True), axis=1, keepdims=True)
    outgoing = picked * lax.rsqrt(ssq / width + norm_eps) * gain[...][None]
    snd[...] = outgoing.astype(jnp.bfloat16).reshape(16, 16, LANE)
    contract_last = (((1,), (1,)), ((), ()))
    cnt[...] = lax.dot_general(
        jnp.ones((8, 128), jnp.bfloat16), named.astype(jnp.bfloat16), contract_last, preferred_element_type=jnp.float32
    )
    pl.semaphore_wait(barrier, len(tp_peers) + len(ep_peers))

    def d_copy(p):
        peer = tp_at(*p)
        return remote(snd.at[peer], land.at[ep, tp], d_s.at[peer], d_r.at[tp], (peer, ep))

    own_rows = pltpu.make_async_copy(snd.at[tp], land.at[ep, tp], loc.at[3])
    own_rows.start()
    for p in tp_peers:
        d_copy(p).start()

    def k_copy(p):
        peer = tp_at(*p)
        return remote(cnt, cnt_tp.at[tp], k_s.at[peer], k_r.at[tp], (peer, ep))

    for p in tp_peers:
        k_copy(p).start()

    def group(dz):
        return pl.ds(pl.multiple_of(ring(z + dz) * 4, 4), 4)

    def x_copy(g, dz, way):
        part = land.at[ep, group(dz)]
        return remote(part, part, ax_s.at[g, way], ax_r.at[g, way], (tp, ep_at(1 - 2 * way, 0)))

    def x_land(g, dz, way):
        part = land.at[ep_at(2 * way - 1, 0), group(dz)]
        return remote(part, part, ax_s.at[g, way], ax_r.at[g, way], (tp, ep_at(1, 0)))

    def f_rows(dx, dz, way):
        return land.at[ep_at(dx, 0), pl.ds(pl.multiple_of(ring(z + dz) * 4 + 2 * way, 2), 2)]

    def f_copy(g, dz, way):
        part = f_rows(2 * way - 1, dz, way)
        return remote(part, part, af_s.at[g, way], af_r.at[g, way], (tp, ep_at(1 - 2 * way, 0)))

    def f_land(g, dz, way):
        part = f_rows(2, dz, way)
        return remote(part, part, af_s.at[g, way], af_r.at[g, way], (tp, ep_at(1, 0)))

    def c_copy(g, dz, q):
        part = land.at[ep_at(q, 0), group(dz)]
        return remote(part, part, ac_s.at[g, q], ac_r.at[g, q], sib)

    def c_land(g, dz, q):
        part = land.at[ep_at(q, 1), group(dz)]
        return remote(part, part, ac_s.at[g, q], ac_r.at[g, q], sib)

    def d_land(p):
        src = tp_at(*p)
        return remote(snd.at[src], land.at[ep, src], d_s.at[src], d_r.at[src], (src, ep))

    for g, dz in GROUPS:
        for p in tp_peers:
            if p[0] == dz:
                d_land(p).wait_recv()
        if dz == 0:
            own_rows.wait()
        for way in (0, 1):
            x_copy(g, dz, way).start()
        c_copy(g, dz, 0).start()

    def rt_copy(p):
        peer = tp_at(*p)
        return remote(rout_ref.at[:, half], rt.at[tp, :, half], rt_s.at[peer], rt_r.at[tp], (peer, ep))

    own_rt = pltpu.make_async_copy(rout_ref.at[:, half], rt.at[tp, :, half], loc.at[4])
    own_rt.start()
    for p in tp_peers:
        rt_copy(p).start()

    for p in tp_peers:
        src = tp_at(*p)
        remote(cnt, cnt_tp.at[src], k_s.at[src], k_r.at[src], (src, ep)).wait_recv()
    cnt_tp[tp] = cnt[...]
    part_sum = cnt_tp[0]
    for i in range(1, 16):
        part_sum += cnt_tp[i]
    cnt_ep[ep] = part_sum

    def l_copy(p):
        peer = ep_at(*p)
        return remote(cnt_ep.at[ep], cnt_ep.at[ep], l_s.at[peer], l_r.at[ep], (tp, peer))

    for p in ep_peers:
        l_copy(p).start()

    out_row = lax.broadcasted_iota(jnp.int32, (128, 128), 0)
    in_row = lax.broadcasted_iota(jnp.int32, (128, 128), 1)
    source = ((out_row % 16) // 2) * 16 + (out_row % 2) * 8 + out_row // 16
    perm = jnp.where(in_row == source, 1.0, 0.0).astype(jnp.bfloat16)

    def turn_rows(group_of):
        for part in range(2):
            block = land[group_of, part * 8 : part * 8 + 8].reshape(128, LANE)
            turned = jnp.dot(perm, block, preferred_element_type=jnp.float32).astype(jnp.bfloat16)
            to = pl.ds(pl.multiple_of(group_of * 32 + part * 16, 16), 16)
            rows[:, to, :] = turned.reshape(8, 16, LANE)

    turn_rows(ep)
    for g, dz in GROUPS:
        for way in (0, 1):
            x_land(g, dz, way).wait_recv()
            f_copy(g, dz, way).start()
            c_copy(g, dz, 3 - 2 * way).start()
    for q in (0, 3, 1):
        if q:
            turn_rows(ep_at(q, 0))
        if q == 1:
            for g, dz in GROUPS:
                for way in (0, 1):
                    f_land(g, dz, way).wait_recv()
                c_copy(g, dz, 2).start()
        for g, dz in GROUPS:
            c_land(g, dz, q).wait_recv()
        turn_rows(ep_at(q, 1))
    turn_rows(ep_at(2, 0))
    for g, dz in GROUPS:
        c_land(g, dz, 2).wait_recv()
    turn_rows(ep_at(2, 1))

    for load in loads:
        load.wait()
    gate_val = jnp.zeros((256, 256), jnp.float32)
    up_val = jnp.zeros((256, 256), jnp.float32)
    for j in range(8):
        gate_val += jnp.dot(rows[j], wg[cut(j), :], preferred_element_type=jnp.float32)
        up_val += jnp.dot(rows[j], wu[cut(j), :], preferred_element_type=jnp.float32)
    active = (gate_val / (1.0 + jnp.exp(-gate_val)) * up_val).astype(jnp.bfloat16)

    def p_copy(n):
        return remote(ybuf.at[n, :, 1 - c], r1.at[n], p_s.at[n], p_r.at[n], sib)

    def h_copy(n, way):
        rows_of = pl.ds(16 * way, 16)
        return remote(
            sbuf.at[n, ring(x + 2), rows_of], half_in.at[n, way],
            h_s.at[n, way], h_r.at[n, way], (tp, ep_at(1 - 2 * way, 0)),
        )

    def q_copy(n, way):
        to = 1 - 2 * way
        return remote(
            sbuf.at[n, ring(x + to)], full_in.at[n, way], q_s.at[n, way], q_r.at[n, way], (tp, ep_at(to, 0))
        )

    def forward(n):
        for way in (0, 1):
            to = ring(x + 1 - 2 * way)
            h_copy(n, way).wait_recv()
            rows_of = slice(16 * way, 16 * way + 16)
            both = sbuf[n, to, rows_of].astype(jnp.float32) + half_in[n, way].astype(jnp.float32)
            sbuf[n, to, rows_of] = both.astype(jnp.bfloat16)
            q_copy(n, way).start()

    for n in range(4):
        part = jnp.dot(active, wd[:, n * 2 * LANE : (n + 1) * 2 * LANE], preferred_element_type=jnp.float32)
        ybuf[n] = part.astype(jnp.bfloat16).reshape(4, 2, 32, 2 * LANE)
        p_copy(n).start()
    for n in range(4):
        p_copy(n).wait_recv()
        for i in range(4):
            both = ybuf[n, i, c].astype(jnp.float32) + r1[n, i].astype(jnp.float32)
            sbuf[n, i] = both.astype(jnp.bfloat16)
        for way in (0, 1):
            h_copy(n, way).start()
        if n:
            forward(n - 1)
    forward(3)

    for p in ep_peers:
        peer = ep_at(*p)
        remote(cnt_ep.at[peer], cnt_ep.at[peer], l_s.at[peer], l_r.at[peer], (tp, peer)).wait_recv()
    counts = cnt_ep[0]
    for i in range(1, 8):
        counts += cnt_ep[i]
    count_ref[...] = counts

    for p in tp_peers:
        src = tp_at(*p)
        remote(rout_ref.at[:, half], rt.at[src, :, half], rt_s.at[src], rt_r.at[src], (src, ep)).wait_recv()
    own_rt.wait()
    mine = rt.at[:, :, half]
    rt_sib = remote(mine, mine, rs_s.at[0], rs_r.at[0], sib)
    rt_sib.start()
    other = rt.at[:, :, pl.ds(pl.multiple_of((1 - c) * (width // 2), width // 2), width // 2)]
    ssq = jnp.zeros((128, 1), jnp.float32)
    for j in range(8):
        h = hid_ref[:, cut(j)].astype(jnp.float32)
        ssq += jnp.sum(h * h, axis=1, keepdims=True)
    scale = lax.rsqrt(ssq / width + norm_eps)
    for j in range(8):
        h = hid_ref[:, cut(j)].astype(jnp.float32)
        normed[:, cut(j)] = (h * scale * gain[j : j + 1, :]).astype(jnp.bfloat16)
    remote(other, other, rs_s.at[0], rs_r.at[0], sib).wait_recv()
    logits = jnp.zeros((256, 128), jnp.float32)
    for j in range(8):
        logits += lax.dot_general(
            rt[:, :, cut(j)].reshape(256, LANE), normed[:, cut(j)], contract_last, preferred_element_type=jnp.float32
        )
    scores = 1.0 / (1.0 + jnp.exp(-logits))
    chosen = []
    for k in range(TOP):
        hit = cho_ref[k : k + 1, :] == row
        chosen.append(jnp.sum(jnp.where(hit, scores, 0.0), axis=0, keepdims=True))
    norm_by = chosen[0]
    for k in range(1, TOP):
        norm_by = norm_by + chosen[k]
    weight = jnp.zeros((256, 128), jnp.float32)
    for k in range(TOP):
        weight += jnp.where(cho_ref[k : k + 1, :] == expert, route_scale * chosen[k] / norm_by, 0.0)
    coeff_ref[...] = jnp.where(pick > 0.0, weight, 0.0).T

    back_row = lax.broadcasted_iota(jnp.int32, (256, 32), 0)
    back_col = lax.broadcasted_iota(jnp.int32, (256, 32), 1)
    returned = jnp.zeros((256, LANE), jnp.float32)
    for n in range(4):
        total = sbuf[n, x].astype(jnp.float32)
        for way in (0, 1):
            q_copy(n, way).wait_recv()
            total += full_in[n, way].astype(jnp.float32)
        total = total.astype(jnp.bfloat16)
        for i in range(2):
            turn = jnp.where((back_row // 8 == back_col) & (back_row % 8 == 2 * n + i), 1.0, 0.0).astype(jnp.bfloat16)
            returned += jnp.dot(turn, total[:, cut(i)], preferred_element_type=jnp.float32)
    rsend[...] = returned.astype(jnp.bfloat16).reshape(16, 16, LANE)

    def b_copy(p):
        peer = tp_at(*p)
        return remote(rsend.at[peer], ret.at[tp], b_s.at[peer], b_r.at[tp], (peer, ep))

    own_back = pltpu.make_async_copy(rsend.at[tp], ret.at[tp], loc.at[5])
    own_back.start()
    for p in tp_peers:
        b_copy(p).start()
    own_back.wait()
    for p in tp_peers:
        src = tp_at(*p)
        remote(rsend.at[src], ret.at[src], b_s.at[src], b_r.at[src], (src, ep)).wait_recv()
    back_ref[...] = ret[...]

    for p in tp_peers:
        d_copy(p).wait_send()
        k_copy(p).wait_send()
        rt_copy(p).wait_send()
        b_copy(p).wait_send()
    for p in ep_peers:
        l_copy(p).wait_send()
    rt_sib.wait_send()
    for g, dz in GROUPS:
        for way in (0, 1):
            x_copy(g, dz, way).wait_send()
            f_copy(g, dz, way).wait_send()
        for q in range(4):
            c_copy(g, dz, q).wait_send()
    for n in range(4):
        p_copy(n).wait_send()
        for way in (0, 1):
            h_copy(n, way).wait_send()
            q_copy(n, way).wait_send()


def mix_kernel(hid_ref, back_ref, coeff_ref, count_ref, bias_ref, kept_ref, moe_ref, load_ref, next_ref):
    i = pl.program_id(0)
    kept_ref[...] = hid_ref[...]

    @pl.when(i == 0)
    def _():
        slots = 128.0 * 128.0 * TOP
        for k in range(2):
            counts = count_ref[0:1, k * 128 : (k + 1) * 128]
            load_ref[k : k + 1, :] = counts * 256.0 / slots
            gap = slots - counts * 256.0
            sign = jnp.where(gap > 0.0, 1.0, jnp.where(gap < 0.0, -1.0, 0.0))
            next_ref[k : k + 1, :] = bias_ref[k : k + 1, :] + bias_rate * sign

    back = back_ref[...].reshape(256, LANE)
    coeff = coeff_ref[...]
    lane_cut = lax.broadcasted_iota(jnp.int32, (128, 256), 1) % 8
    for k in range(2):
        here = lane_cut == 2 * i + k
        mixed = jnp.dot(jnp.where(here, coeff, 0.0).astype(jnp.bfloat16), back, preferred_element_type=jnp.float32)
        moe_ref[:, k * LANE : (k + 1) * LANE] = mixed.astype(jnp.bfloat16)


def experts(hidden_out, norm_gain, router, router_bias, choices, w_gate, w_up, w_down):
    dma = pltpu.SemaphoreType.DMA
    bf16, f32 = jnp.bfloat16, jnp.float32
    vmem = pl.BlockSpec(memory_space=VMEM)
    anywhere = pl.BlockSpec(memory_space=pl.ANY)
    back, coeff, counts = pl.pallas_call(
        moe_kernel,
        name="experts",
        out_shape=(
            jax.ShapeDtypeStruct((16, 16, LANE), bf16),
            jax.ShapeDtypeStruct((128, 256), f32),
            jax.ShapeDtypeStruct((8, 256), f32),
        ),
        in_specs=[vmem] * 4 + [anywhere] * 3,
        out_specs=(vmem,) * 3,
        scratch_shapes=[
            VMEM((7168, 256), bf16), VMEM((7168, 256), bf16), VMEM((256, 7168), bf16),
            VMEM((16, 16, 7168), bf16), VMEM((128, 7168), bf16), VMEM((8, LANE), f32), VMEM((16, 16, LANE), bf16),
            VMEM((8, 16, 16, LANE), bf16), VMEM((8, 256, LANE), bf16),
            VMEM((4, 4, 2, 32, 2 * LANE), bf16), VMEM((4, 4, 32, 2 * LANE), bf16),
            VMEM((4, 4, 32, 2 * LANE), bf16), VMEM((4, 2, 16, 2 * LANE), bf16), VMEM((4, 2, 32, 2 * LANE), bf16),
            VMEM((16, 16, LANE), bf16), VMEM((16, 16, LANE), bf16),
            VMEM((8, 256), f32), VMEM((16, 8, 256), f32), VMEM((8, 8, 256), f32),
            dma((6,)), dma((16,)), dma((16,)), dma((4, 2)), dma((4, 2)), dma((4, 2)), dma((4, 2)), dma((4, 4)), dma((4, 4)),
            dma((16,)), dma((16,)), dma((8,)), dma((8,)), dma((16,)), dma((16,)), dma((1,)), dma((1,)),
            dma((4,)), dma((4,)), dma((4, 2)), dma((4, 2)), dma((4, 2)), dma((4, 2)), dma((16,)), dma((16,)),
        ],
        compiler_params=pltpu.CompilerParams(
            collective_id=1, has_side_effects=True, vmem_limit_bytes=56 * 1024 * 1024
        ),
    )(
        hidden_out, norm_gain.reshape(-1, 128), router.T, choices.T,
        w_gate[0], w_up[0], w_down[0],
    )
    block = pl.BlockSpec((128, 2 * LANE), lambda i: (0, i))
    hidden_kept, moe_out, load, bias_next = pl.pallas_call(
        mix_kernel,
        name="mix",
        grid=(4,),
        out_shape=(
            jax.ShapeDtypeStruct((128, 7168), bf16),
            jax.ShapeDtypeStruct((128, 7168), bf16),
            jax.ShapeDtypeStruct((2, 128), f32),
            jax.ShapeDtypeStruct((2, 128), f32),
        ),
        in_specs=[block] + [vmem] * 4,
        out_specs=(block, block, vmem, vmem),
    )(hidden_out, back, coeff, counts, router_bias.reshape(2, 128))
    return hidden_kept, moe_out, load.reshape(-1), bias_next.reshape(-1)


def on_device(
    attn_out, residual, w_out, norm_gain, router, router_bias, choices, w_gate, w_up, w_down
):
    hidden_out = project(attn_out, w_out, residual)
    return experts(hidden_out, norm_gain, router, router_bias, choices, w_gate, w_up, w_down)


def solution(mesh):
    placed = (
        P("ep", "tp"),
        P(("ep", "tp"), None),
        P("tp", None),
        P(),
        P(None, "tp"),
        P(),
        P(("ep", "tp"), None),
        P("tp", None, "ep"),
        P("tp", None, "ep"),
        P("tp", "ep", None),
    )
    return jax.shard_map(
        on_device,
        mesh=mesh,
        in_specs=placed,
        out_specs=(P(("ep", "tp"), None), P(("ep", "tp"), None), P(), P()),
        check_vma=False,
    )
```

```python
import jax
import jax.numpy as jnp
from jax import lax
from jax.experimental import pallas as pl
from jax.experimental.pallas import tpu as pltpu
from jax.sharding import PartitionSpec as P

TOP = 8


norm_eps = 1e-06
route_scale = 2.5
bias_rate = 0.001


MESH = pl.DeviceIdType.MESH
VMEM = pltpu.VMEM
ROUNDS = 7
SHARED = 5
CH = 256


def ring(i):
    return lax.rem(i + 8, 4)


def place():
    tp = lax.axis_index("tp")
    ep = lax.axis_index("ep")
    return lax.div(tp, 4), lax.rem(tp, 4), lax.div(ep, 2), lax.rem(ep, 2)


def at(z, y, x, c):
    return (ring(z) * 4 + ring(y), ring(x) * 2 + lax.rem(c, 2))


def greet(peers):
    barrier = pltpu.get_barrier_semaphore()
    for peer in peers:
        pl.semaphore_signal(barrier, inc=1, device_id=peer, device_id_type=MESH)
    pl.semaphore_wait(barrier, len(peers))


def remote(src, dst, send, recv, peer):
    return pltpu.make_async_remote_copy(
        src_ref=src, dst_ref=dst, send_sem=send, recv_sem=recv, device_id=peer, device_id_type=MESH
    )


def project_kernel(
    a_ref, w_ref, res_ref, out_ref,
    ag, wown, wbuf, pbuf, half_in, full_in, resv,
    loc, a_s, a_r, y_s, y_r, g_s, g_r, v_s, v_r, x_s, x_r, f_s, f_r, c_s, c_r, h_s, h_r, z_s, z_r,
):
    z, y, x, c = place()
    half = pl.multiple_of(c * 256, 256)
    own_a = pltpu.make_async_copy(a_ref.at[:, y], ag.at[0, 0], loc.at[0])
    own_b = pltpu.make_async_copy(a_ref.at[z], ag.at[1, 0], loc.at[3])
    own_w = pltpu.make_async_copy(w_ref, wown, loc.at[1])
    own_res = pltpu.make_async_copy(res_ref, resv, loc.at[2])
    own_a.start()
    own_b.start()
    own_w.start()
    own_res.start()
    greet(
        [at(z, y + e, x, c) for e in (1, 2, 3)]
        + [at(z + e, y, x, c) for e in (1, 2, 3)]
        + [at(z, y, x + 1, c), at(z, y, x - 1, c), at(z, y, x, c + 1)]
    )
    sib = at(z, y, x, c + 1)

    def gather_at(kind, i):
        return at(z + i * kind, y + i * (1 - kind), x, c)

    def sum_at(kind, i):
        return at(z + i * (1 - kind), y + i * kind, x, c)

    def sum_place(kind):
        return z * (1 - kind) + y * kind

    def chunk(dx, r):
        return ring(x + dx) * ROUNDS + r

    def y_copy(i, n, way):
        cols = pl.ds(pl.multiple_of(n * CH, CH), CH)
        return remote(
            w_ref.at[pl.ds(half, 256), cols], wbuf.at[n, 2 - 2 * way, pl.ds(half, 256), :],
            y_s.at[i, way], y_r.at[i, way], gather_at(lax.rem(i, 2), 1 - 2 * way),
        )

    def y_land(i, n, way):
        part = wbuf.at[n, 2 - 2 * way, pl.ds(half, 256), :]
        return remote(part, part, y_s.at[i, way], y_r.at[i, way], at(z, y + 1, x, c))

    def g_copy(i, n, way):
        rows = pl.ds(pl.multiple_of(half + 128 * way, 128), 128)
        return remote(
            wbuf.at[n, 2 - 2 * way, rows, :], wbuf.at[n, 1, rows, :],
            g_s.at[i, way], g_r.at[i, way], gather_at(lax.rem(i, 2), 1 - 2 * way),
        )

    def common(u):
        return lax.div(u, 2) * ROUNDS + SHARED + lax.rem(u, 2)

    def v_copy(u):
        part = wbuf.at[common(u), :, pl.ds(half, 256), :]
        return remote(part, part, v_s.at[u], v_r.at[u], sib)

    def v_land(u):
        part = wbuf.at[common(u), :, pl.ds(pl.multiple_of(256 - half, 256), 256), :]
        return remote(part, part, v_s.at[u], v_r.at[u], sib)

    def a_copy(kind, g, e):
        rows = a_ref.at[ring(z + e), g] if kind else a_ref.at[g, ring(y + e)]
        return remote(
            rows, ag.at[kind, 4 - e, g], a_s.at[kind, g, e - 1], a_r.at[kind, g, 3 - e], gather_at(kind, e)
        )

    def x_copy(r, way):
        part = wbuf.at[chunk(0, r), :, pl.ds(half, 256), :]
        return remote(part, part, x_s.at[r, way], x_r.at[r, way], at(z, y, x + 1 - 2 * way, c))

    def x_land(r, way):
        part = wbuf.at[chunk(2 * way - 1, r), :, pl.ds(half, 256), :]
        return remote(part, part, x_s.at[r, way], x_r.at[r, way], at(z, y, x + 1 - 2 * way, c))

    def f_part(dx, r, way):
        return wbuf.at[chunk(dx, r), :, pl.ds(pl.multiple_of(half + 128 * way, 128), 128), :]

    def f_copy(r, way):
        part = f_part(2 * way - 1, r, way)
        return remote(part, part, f_s.at[r, way], f_r.at[r, way], at(z, y, x + 1 - 2 * way, c))

    def f_land(r, way):
        part = f_part(2, r, way)
        return remote(part, part, f_s.at[r, way], f_r.at[r, way], at(z, y, x + 1 - 2 * way, c))

    def hop(q):
        return (0, 3, 1, 2)[q]

    def c_copy(r, q):
        part = wbuf.at[chunk(hop(q), r), :, pl.ds(half, 256), :]
        return remote(part, part, c_s.at[r, q], c_r.at[r, q], sib)

    def c_land(n, r, q):
        other = pl.multiple_of(256 - half, 256)
        part = wbuf.at[n, :, pl.ds(other, 256), :]
        return remote(part, part, c_s.at[r, q], c_r.at[r, q], sib)

    def halves(way):
        return pl.ds(64 * way, 64)

    def h_copy(n, kind, way):
        return remote(
            pbuf.at[n, ring(sum_place(kind) + 2), halves(way)], half_in.at[n, way],
            h_s.at[n, way], h_r.at[n, way], sum_at(kind, 1 - 2 * way),
        )

    def z_copy(n, kind, way):
        return remote(
            pbuf.at[n, ring(sum_place(kind) + 1 - 2 * way)], full_in.at[n, way],
            z_s.at[n, way], z_r.at[n, way], sum_at(kind, 1 - 2 * way),
        )

    def start_y(i, n):
        for way in (0, 1):
            y_copy(i, n, way).start()

    def start_a(g):
        for e in (2, 1, 3):
            for kind in (0, 1):
                a_copy(kind, g, e).start()

    def pass_on(i, n):
        for way in (0, 1):
            y_land(i, n, way).wait_recv()
            g_copy(i, n, way).start()

    def first(r):
        for way in (0, 1):
            g_copy(r, chunk(0, r), way).wait_recv()
        x_copy(r, 0).start()
        x_copy(r, 1).start()
        c_copy(r, 0).start()

    def multiply(n, kind):
        cols = pl.ds(pl.multiple_of(n * CH, CH), CH)
        total = jnp.dot(ag[kind, 0].reshape(512, 512), wown[:, cols], preferred_element_type=jnp.float32)
        for k in range(3):
            total += jnp.dot(ag[kind, k + 1].reshape(512, 512), wbuf[n, k], preferred_element_type=jnp.float32)
        pbuf[n] = total.astype(jnp.bfloat16).reshape(4, 128, CH)
        for way in (0, 1):
            h_copy(n, kind, way).start()

    def combine(n, kind):
        for way in (0, 1):
            to = ring(sum_place(kind) + 1 - 2 * way)
            h_copy(n, kind, way).wait_recv()
            both = pbuf[n, to, halves(way)].astype(jnp.float32) + half_in[n, way].astype(jnp.float32)
            pbuf[n, to, halves(way)] = both.astype(jnp.bfloat16)
            z_copy(n, kind, way).start()

    def finish(n, kind):
        cols = pl.ds(pl.multiple_of(n * CH, CH), CH)
        total = pbuf[n, sum_place(kind)].astype(jnp.float32)
        for way in (0, 1):
            z_copy(n, kind, way).wait_recv()
            total += full_in[n, way].astype(jnp.float32)
        out_ref[:, cols] = (resv[:, cols].astype(jnp.float32) + total).astype(jnp.bfloat16)

    def near(q, r):
        return chunk(q + lax.div(q, 2), r)

    def step(work, r):
        @pl.when((r >= 0) & (r < SHARED))
        def _():
            @pl.loop(0, 3)
            def _(q):
                work(near(q, r), lax.rem(r, 2))

        @pl.when((r >= 2) & (r < 6))
        def _():
            for k in (0, 1):
                work(common(2 * r - 4 + k), 1 - k)

        @pl.when((r >= 1) & (r <= SHARED))
        def _():
            work(chunk(2, r - 1), lax.rem(r - 1, 2))

    start_y(0, chunk(0, 0))
    start_y(1, chunk(0, 1))
    pass_on(0, chunk(0, 0))
    pass_on(1, chunk(0, 1))
    start_a(0)
    start_a(1)
    first(0)
    first(1)
    start_a(2)
    start_y(2, chunk(0, 2))
    start_y(3, chunk(0, 3))
    start_a(3)
    own_a.wait()
    own_b.wait()
    own_w.wait()
    own_res.wait()

    def multiply_near(r):
        @pl.loop(0, 3)
        def _(q):
            n = near(q, r)
            c_land(n, r, lax.rem(3 - q, 3)).wait_recv()
            multiply(n, lax.rem(r, 2))

    @pl.loop(0, SHARED + 4)
    def _(r):
        @pl.when(r < SHARED)
        def _():
            for way in (0, 1):
                x_land(r, way).wait_recv()
                f_copy(r, way).start()
                c_copy(r, 1 + way).start()

        @pl.when(r == 0)
        def _():
            pass_on(2, chunk(0, 2))
            pass_on(3, chunk(0, 3))

        @pl.when((r >= 1) & (r + 3 < SHARED))
        def _():
            pass_on(r + 3, chunk(0, r + 3))

        @pl.when(r + 2 < SHARED)
        def _():
            first(r + 2)

        @pl.when(r == 0)
        def _():
            start_y(4, chunk(0, 4))

        @pl.when(r < 4)
        def _():
            for k in (0, 1):
                start_y(SHARED + 2 * r + k, common(2 * r + k))

        @pl.when((r >= 1) & (r < 5))
        def _():
            for k in (0, 1):
                pass_on(SHARED + 2 * r - 2 + k, common(2 * r - 2 + k))

        @pl.when((r >= 2) & (r < 6))
        def _():
            for k in (0, 1):
                u = 2 * r - 4 + k
                for way in (0, 1):
                    g_copy(SHARED + u, common(u), way).wait_recv()
                v_copy(u).start()

        @pl.when(r == 1)
        def _():
            for g in range(4):
                for k in range(3):
                    for kind in (0, 1):
                        part = ag.at[kind, k + 1, g]
                        remote(part, part, a_s.at[kind, g, k], a_r.at[kind, g, k], at(z, y + 1, x, c)).wait_recv()
            multiply_near(0)

        @pl.when((r >= 1) & (r < SHARED))
        def _():
            multiply_near(r)

        @pl.when((r >= 1) & (r <= SHARED))
        def _():
            for way in (0, 1):
                f_land(r - 1, way).wait_recv()
            c_copy(r - 1, 3).start()

        @pl.when(r >= 2)
        def _():
            step(combine, r - 1)

        @pl.when((r >= 2) & (r < 6))
        def _():
            for k in (0, 1):
                u = 2 * r - 4 + k
                v_land(u).wait_recv()
                multiply(common(u), 1 - k)

        @pl.when((r >= 1) & (r <= SHARED))
        def _():
            c_land(chunk(2, r - 1), r - 1, 3).wait_recv()
            multiply(chunk(2, r - 1), lax.rem(r - 1, 2))

        @pl.when(r == 2)
        def _():
            @pl.loop(0, 3)
            def _(q):
                combine(near(q, 0), 0)

        @pl.when(r >= 3)
        def _():
            step(finish, r - 3)

    for g in range(4):
        for e in (1, 2, 3):
            for kind in (0, 1):
                a_copy(kind, g, e).wait_send()

    @pl.loop(0, SHARED)
    def _(r):
        for way in (0, 1):
            y_copy(r, chunk(0, r), way).wait_send()
            g_copy(r, chunk(0, r), way).wait_send()
            x_copy(r, way).wait_send()
            f_copy(r, way).wait_send()
        for q in range(4):
            c_copy(r, q).wait_send()

    @pl.loop(0, 8)
    def _(u):
        for way in (0, 1):
            y_copy(SHARED + u, common(u), way).wait_send()
            g_copy(SHARED + u, common(u), way).wait_send()
        v_copy(u).wait_send()

    @pl.loop(0, 4 * ROUNDS)
    def _(n):
        for way in (0, 1):
            h_copy(n, 0, way).wait_send()
            z_copy(n, 0, way).wait_send()


def project(attn_out, w_out, residual):
    dma = pltpu.SemaphoreType.DMA
    anywhere = pl.BlockSpec(memory_space=pl.ANY)
    return pl.pallas_call(
        project_kernel,
        name="project",
        out_shape=jax.ShapeDtypeStruct((128, 7168), jnp.bfloat16),
        in_specs=[anywhere] * 3,
        out_specs=pl.BlockSpec(memory_space=VMEM),
        scratch_shapes=[
            VMEM((2, 4, 4, 128, 512), jnp.bfloat16),
            VMEM((512, 7168), jnp.bfloat16),
            VMEM((28, 3, 512, CH), jnp.bfloat16),
            VMEM((28, 4, 128, CH), jnp.bfloat16),
            VMEM((28, 2, 64, CH), jnp.bfloat16),
            VMEM((28, 2, 128, CH), jnp.bfloat16),
            VMEM((128, 7168), jnp.bfloat16),
            dma((4,)), dma((2, 4, 3)), dma((2, 4, 3)), dma((13, 2)), dma((13, 2)), dma((13, 2)), dma((13, 2)),
            dma((8,)), dma((8,)), dma((5, 2)), dma((5, 2)), dma((5, 2)), dma((5, 2)), dma((5, 4)), dma((5, 4)),
            dma((28, 2)), dma((28, 2)), dma((28, 2)), dma((28, 2)),
        ],
        compiler_params=pltpu.CompilerParams(
            collective_id=0, has_side_effects=True, vmem_limit_bytes=58 * 1024 * 1024
        ),
    )(attn_out.reshape(4, 4, 128, 512), w_out, residual)


LANE = 896
GROUPS = ((0, 0), (1, 1), (2, 3), (3, 2))


def moe_kernel(
    hid_ref, gain_ref, rout_ref, cho_ref, wg_ref, wu_ref, wd_ref,
    back_ref, coeff_ref, count_ref,
    wg, wu, wd, rt, normed, gain, snd, land, rows, ybuf, r1, sbuf, half_in, full_in, rsend, ret, cnt, cnt_tp, cnt_ep,
    loc, d_s, d_r, ax_s, ax_r, af_s, af_r, ac_s, ac_r, k_s, k_r, l_s, l_r, rt_s, rt_r, rs_s, rs_r,
    p_s, p_r, h_s, h_r, q_s, q_r, b_s, b_r,
):
    z, y, x, c = place()
    tp = z * 4 + y
    ep = x * 2 + c
    sib = at(z, y, x, c + 1)
    width = hid_ref.shape[1]
    half = pl.ds(pl.multiple_of(c * (width // 2), width // 2), width // 2)
    loads = [pltpu.make_async_copy(s, d, loc.at[i]) for i, (s, d) in enumerate(((wg_ref, wg), (wu_ref, wu), (wd_ref, wd)))]
    for load in loads:
        load.start()
    tp_peers = [(dz, dy) for dz in (0, 1, 3, 2) for dy in (1, 3, 2, 0) if (dz, dy) != (0, 0)]
    ep_peers = [(dx, dc) for dx in (0, 1, 3, 2) for dc in (0, 1) if (dx, dc) != (0, 0)]

    def tp_at(dz, dy):
        return ring(z + dz) * 4 + ring(y + dy)

    def ep_at(dx, dc):
        return ring(x + dx) * 2 + lax.rem(c + dc, 2)

    barrier = pltpu.get_barrier_semaphore()
    for p in tp_peers:
        pl.semaphore_signal(barrier, inc=1, device_id=(tp_at(*p), ep), device_id_type=MESH)
    for p in ep_peers:
        pl.semaphore_signal(barrier, inc=1, device_id=(tp, ep_at(*p)), device_id_type=MESH)

    def cut(j):
        return slice(j * LANE, (j + 1) * LANE)

    row = lax.broadcasted_iota(jnp.int32, (256, 128), 0)
    lane = lax.broadcasted_iota(jnp.int32, (256, 128), 1)
    expert = row // 16
    member = jnp.zeros((256, 128), jnp.float32)
    named = jnp.zeros((256, 128), jnp.float32)
    for k in range(TOP):
        ck = cho_ref[k : k + 1, :]
        member += jnp.where(ck == expert, 1.0, 0.0)
        named += jnp.where(ck == row, 1.0, 0.0)
    before = jnp.where(row[:128] < lane[:128], 1.0, 0.0).astype(jnp.bfloat16)
    rank = jnp.dot(member.astype(jnp.bfloat16), before, preferred_element_type=jnp.float32)
    slot = ((row // 8) % 2).astype(jnp.float32)
    pick = jnp.where(rank == slot, member, 0.0)
    feature = row % 8
    picked = jnp.zeros((256, LANE), jnp.float32)
    for j in range(8):
        pj = jnp.where(feature == j, pick, 0.0).astype(jnp.bfloat16)
        picked += jnp.dot(pj, hid_ref[:, cut(j)], preferred_element_type=jnp.float32)
    gains = gain_ref[...].astype(jnp.float32)
    for j in range(8):
        for i in range(7):
            gain[j : j + 1, i * 128 : (i + 1) * 128] = gains[j * 7 + i : j * 7 + i + 1, :]
    picked = picked.reshape(32, 8, LANE)
    ssq = jnp.sum(jnp.sum(picked * picked, axis=2, keepdims=True), axis=1, keepdims=True)
    outgoing = picked * lax.rsqrt(ssq / width + norm_eps) * gain[...][None]
    snd[...] = outgoing.astype(jnp.bfloat16).reshape(16, 16, LANE)
    contract_last = (((1,), (1,)), ((), ()))
    cnt[...] = lax.dot_general(
        jnp.ones((8, 128), jnp.bfloat16), named.astype(jnp.bfloat16), contract_last, preferred_element_type=jnp.float32
    )
    pl.semaphore_wait(barrier, len(tp_peers) + len(ep_peers))

    def d_copy(p):
        peer = tp_at(*p)
        return remote(snd.at[peer], land.at[ep, tp], d_s.at[peer], d_r.at[tp], (peer, ep))

    own_rows = pltpu.make_async_copy(snd.at[tp], land.at[ep, tp], loc.at[3])
    own_rows.start()
    for p in tp_peers:
        d_copy(p).start()

    def k_copy(p):
        peer = tp_at(*p)
        return remote(cnt, cnt_tp.at[tp], k_s.at[peer], k_r.at[tp], (peer, ep))

    for p in tp_peers:
        k_copy(p).start()

    def group(dz):
        return pl.ds(pl.multiple_of(ring(z + dz) * 4, 4), 4)

    def x_copy(g, dz, way):
        part = land.at[ep, group(dz)]
        return remote(part, part, ax_s.at[g, way], ax_r.at[g, way], (tp, ep_at(1 - 2 * way, 0)))

    def x_land(g, dz, way):
        part = land.at[ep_at(2 * way - 1, 0), group(dz)]
        return remote(part, part, ax_s.at[g, way], ax_r.at[g, way], (tp, ep_at(1, 0)))

    def f_rows(dx, dz, way):
        return land.at[ep_at(dx, 0), pl.ds(pl.multiple_of(ring(z + dz) * 4 + 2 * way, 2), 2)]

    def f_copy(g, dz, way):
        part = f_rows(2 * way - 1, dz, way)
        return remote(part, part, af_s.at[g, way], af_r.at[g, way], (tp, ep_at(1 - 2 * way, 0)))

    def f_land(g, dz, way):
        part = f_rows(2, dz, way)
        return remote(part, part, af_s.at[g, way], af_r.at[g, way], (tp, ep_at(1, 0)))

    def c_copy(g, dz, q):
        part = land.at[ep_at(q, 0), group(dz)]
        return remote(part, part, ac_s.at[g, q], ac_r.at[g, q], sib)

    def c_land(g, dz, q):
        part = land.at[ep_at(q, 1), group(dz)]
        return remote(part, part, ac_s.at[g, q], ac_r.at[g, q], sib)

    def d_land(p):
        src = tp_at(*p)
        return remote(snd.at[src], land.at[ep, src], d_s.at[src], d_r.at[src], (src, ep))

    for g, dz in GROUPS:
        for p in tp_peers:
            if p[0] == dz:
                d_land(p).wait_recv()
        if dz == 0:
            own_rows.wait()
        for way in (0, 1):
            x_copy(g, dz, way).start()
        c_copy(g, dz, 0).start()

    def rt_copy(p):
        peer = tp_at(*p)
        return remote(rout_ref.at[:, half], rt.at[tp, :, half], rt_s.at[peer], rt_r.at[tp], (peer, ep))

    own_rt = pltpu.make_async_copy(rout_ref.at[:, half], rt.at[tp, :, half], loc.at[4])
    own_rt.start()
    for p in tp_peers:
        rt_copy(p).start()

    for p in tp_peers:
        src = tp_at(*p)
        remote(cnt, cnt_tp.at[src], k_s.at[src], k_r.at[src], (src, ep)).wait_recv()
    cnt_tp[tp] = cnt[...]
    part_sum = cnt_tp[0]
    for i in range(1, 16):
        part_sum += cnt_tp[i]
    cnt_ep[ep] = part_sum

    def l_copy(p):
        peer = ep_at(*p)
        return remote(cnt_ep.at[ep], cnt_ep.at[ep], l_s.at[peer], l_r.at[ep], (tp, peer))

    for p in ep_peers:
        l_copy(p).start()

    out_row = lax.broadcasted_iota(jnp.int32, (128, 128), 0)
    in_row = lax.broadcasted_iota(jnp.int32, (128, 128), 1)
    source = ((out_row % 16) // 2) * 16 + (out_row % 2) * 8 + out_row // 16
    perm = jnp.where(in_row == source, 1.0, 0.0).astype(jnp.bfloat16)

    def turn_rows(group_of):
        for part in range(2):
            block = land[group_of, part * 8 : part * 8 + 8].reshape(128, LANE)
            turned = jnp.dot(perm, block, preferred_element_type=jnp.float32).astype(jnp.bfloat16)
            to = pl.ds(pl.multiple_of(group_of * 32 + part * 16, 16), 16)
            rows[:, to, :] = turned.reshape(8, 16, LANE)

    turn_rows(ep)
    for g, dz in GROUPS:
        for way in (0, 1):
            x_land(g, dz, way).wait_recv()
            f_copy(g, dz, way).start()
            c_copy(g, dz, 3 - 2 * way).start()
    for q in (0, 3, 1):
        if q:
            turn_rows(ep_at(q, 0))
        if q == 1:
            for g, dz in GROUPS:
                for way in (0, 1):
                    f_land(g, dz, way).wait_recv()
                c_copy(g, dz, 2).start()
        for g, dz in GROUPS:
            c_land(g, dz, q).wait_recv()
        turn_rows(ep_at(q, 1))
    turn_rows(ep_at(2, 0))
    for g, dz in GROUPS:
        c_land(g, dz, 2).wait_recv()
    turn_rows(ep_at(2, 1))

    for load in loads:
        load.wait()
    gate_val = jnp.zeros((256, 256), jnp.float32)
    up_val = jnp.zeros((256, 256), jnp.float32)
    for j in range(8):
        gate_val += jnp.dot(rows[j], wg[cut(j), :], preferred_element_type=jnp.float32)
        up_val += jnp.dot(rows[j], wu[cut(j), :], preferred_element_type=jnp.float32)
    active = (gate_val / (1.0 + jnp.exp(-gate_val)) * up_val).astype(jnp.bfloat16)

    def p_copy(n):
        return remote(ybuf.at[n, :, 1 - c], r1.at[n], p_s.at[n], p_r.at[n], sib)

    def h_copy(n, way):
        rows_of = pl.ds(16 * way, 16)
        return remote(
            sbuf.at[n, ring(x + 2), rows_of], half_in.at[n, way],
            h_s.at[n, way], h_r.at[n, way], (tp, ep_at(1 - 2 * way, 0)),
        )

    def q_copy(n, way):
        to = 1 - 2 * way
        return remote(
            sbuf.at[n, ring(x + to)], full_in.at[n, way], q_s.at[n, way], q_r.at[n, way], (tp, ep_at(to, 0))
        )

    def forward(n):
        for way in (0, 1):
            to = ring(x + 1 - 2 * way)
            h_copy(n, way).wait_recv()
            rows_of = slice(16 * way, 16 * way + 16)
            both = sbuf[n, to, rows_of].astype(jnp.float32) + half_in[n, way].astype(jnp.float32)
            sbuf[n, to, rows_of] = both.astype(jnp.bfloat16)
            q_copy(n, way).start()

    for n in range(4):
        part = jnp.dot(active, wd[:, n * 2 * LANE : (n + 1) * 2 * LANE], preferred_element_type=jnp.float32)
        ybuf[n] = part.astype(jnp.bfloat16).reshape(4, 2, 32, 2 * LANE)
        p_copy(n).start()
    for n in range(4):
        p_copy(n).wait_recv()
        for i in range(4):
            both = ybuf[n, i, c].astype(jnp.float32) + r1[n, i].astype(jnp.float32)
            sbuf[n, i] = both.astype(jnp.bfloat16)
        for way in (0, 1):
            h_copy(n, way).start()
        if n:
            forward(n - 1)
    forward(3)

    for p in ep_peers:
        peer = ep_at(*p)
        remote(cnt_ep.at[peer], cnt_ep.at[peer], l_s.at[peer], l_r.at[peer], (tp, peer)).wait_recv()
    counts = cnt_ep[0]
    for i in range(1, 8):
        counts += cnt_ep[i]
    count_ref[...] = counts

    for p in tp_peers:
        src = tp_at(*p)
        remote(rout_ref.at[:, half], rt.at[src, :, half], rt_s.at[src], rt_r.at[src], (src, ep)).wait_recv()
    own_rt.wait()
    mine = rt.at[:, :, half]
    rt_sib = remote(mine, mine, rs_s.at[0], rs_r.at[0], sib)
    rt_sib.start()
    other = rt.at[:, :, pl.ds(pl.multiple_of((1 - c) * (width // 2), width // 2), width // 2)]
    ssq = jnp.zeros((128, 1), jnp.float32)
    for j in range(8):
        h = hid_ref[:, cut(j)].astype(jnp.float32)
        ssq += jnp.sum(h * h, axis=1, keepdims=True)
    scale = lax.rsqrt(ssq / width + norm_eps)
    for j in range(8):
        h = hid_ref[:, cut(j)].astype(jnp.float32)
        normed[:, cut(j)] = (h * scale * gain[j : j + 1, :]).astype(jnp.bfloat16)
    remote(other, other, rs_s.at[0], rs_r.at[0], sib).wait_recv()
    logits = jnp.zeros((256, 128), jnp.float32)
    for j in range(8):
        logits += lax.dot_general(
            rt[:, :, cut(j)].reshape(256, LANE), normed[:, cut(j)], contract_last, preferred_element_type=jnp.float32
        )
    scores = 1.0 / (1.0 + jnp.exp(-logits))
    chosen = []
    for k in range(TOP):
        hit = cho_ref[k : k + 1, :] == row
        chosen.append(jnp.sum(jnp.where(hit, scores, 0.0), axis=0, keepdims=True))
    norm_by = chosen[0]
    for k in range(1, TOP):
        norm_by = norm_by + chosen[k]
    weight = jnp.zeros((256, 128), jnp.float32)
    for k in range(TOP):
        weight += jnp.where(cho_ref[k : k + 1, :] == expert, route_scale * chosen[k] / norm_by, 0.0)
    coeff_ref[...] = jnp.where(pick > 0.0, weight, 0.0).T

    back_row = lax.broadcasted_iota(jnp.int32, (256, 32), 0)
    back_col = lax.broadcasted_iota(jnp.int32, (256, 32), 1)
    returned = jnp.zeros((256, LANE), jnp.float32)
    for n in range(4):
        total = sbuf[n, x].astype(jnp.float32)
        for way in (0, 1):
            q_copy(n, way).wait_recv()
            total += full_in[n, way].astype(jnp.float32)
        total = total.astype(jnp.bfloat16)
        for i in range(2):
            turn = jnp.where((back_row // 8 == back_col) & (back_row % 8 == 2 * n + i), 1.0, 0.0).astype(jnp.bfloat16)
            returned += jnp.dot(turn, total[:, cut(i)], preferred_element_type=jnp.float32)
    rsend[...] = returned.astype(jnp.bfloat16).reshape(16, 16, LANE)

    def b_copy(p):
        peer = tp_at(*p)
        return remote(rsend.at[peer], ret.at[tp], b_s.at[peer], b_r.at[tp], (peer, ep))

    own_back = pltpu.make_async_copy(rsend.at[tp], ret.at[tp], loc.at[5])
    own_back.start()
    for p in tp_peers:
        b_copy(p).start()
    own_back.wait()
    for p in tp_peers:
        src = tp_at(*p)
        remote(rsend.at[src], ret.at[src], b_s.at[src], b_r.at[src], (src, ep)).wait_recv()
    back_ref[...] = ret[...]

    for p in tp_peers:
        d_copy(p).wait_send()
        k_copy(p).wait_send()
        rt_copy(p).wait_send()
        b_copy(p).wait_send()
    for p in ep_peers:
        l_copy(p).wait_send()
    rt_sib.wait_send()
    for g, dz in GROUPS:
        for way in (0, 1):
            x_copy(g, dz, way).wait_send()
            f_copy(g, dz, way).wait_send()
        for q in range(4):
            c_copy(g, dz, q).wait_send()
    for n in range(4):
        p_copy(n).wait_send()
        for way in (0, 1):
            h_copy(n, way).wait_send()
            q_copy(n, way).wait_send()


def mix_kernel(hid_ref, back_ref, coeff_ref, count_ref, bias_ref, kept_ref, moe_ref, load_ref, next_ref):
    i = pl.program_id(0)
    kept_ref[...] = hid_ref[...]

    @pl.when(i == 0)
    def _():
        slots = 128.0 * 128.0 * TOP
        for k in range(2):
            counts = count_ref[0:1, k * 128 : (k + 1) * 128]
            load_ref[k : k + 1, :] = counts * 256.0 / slots
            gap = slots - counts * 256.0
            sign = jnp.where(gap > 0.0, 1.0, jnp.where(gap < 0.0, -1.0, 0.0))
            next_ref[k : k + 1, :] = bias_ref[k : k + 1, :] + bias_rate * sign

    back = back_ref[...].reshape(256, LANE)
    coeff = coeff_ref[...]
    lane_cut = lax.broadcasted_iota(jnp.int32, (128, 256), 1) % 8
    for k in range(2):
        here = lane_cut == 2 * i + k
        mixed = jnp.dot(jnp.where(here, coeff, 0.0).astype(jnp.bfloat16), back, preferred_element_type=jnp.float32)
        moe_ref[:, k * LANE : (k + 1) * LANE] = mixed.astype(jnp.bfloat16)


def experts(hidden_out, norm_gain, router, router_bias, choices, w_gate, w_up, w_down):
    dma = pltpu.SemaphoreType.DMA
    bf16, f32 = jnp.bfloat16, jnp.float32
    vmem = pl.BlockSpec(memory_space=VMEM)
    anywhere = pl.BlockSpec(memory_space=pl.ANY)
    back, coeff, counts = pl.pallas_call(
        moe_kernel,
        name="experts",
        out_shape=(
            jax.ShapeDtypeStruct((16, 16, LANE), bf16),
            jax.ShapeDtypeStruct((128, 256), f32),
            jax.ShapeDtypeStruct((8, 256), f32),
        ),
        in_specs=[vmem] * 4 + [anywhere] * 3,
        out_specs=(vmem,) * 3,
        scratch_shapes=[
            VMEM((7168, 256), bf16), VMEM((7168, 256), bf16), VMEM((256, 7168), bf16),
            VMEM((16, 16, 7168), bf16), VMEM((128, 7168), bf16), VMEM((8, LANE), f32), VMEM((16, 16, LANE), bf16),
            VMEM((8, 16, 16, LANE), bf16), VMEM((8, 256, LANE), bf16),
            VMEM((4, 4, 2, 32, 2 * LANE), bf16), VMEM((4, 4, 32, 2 * LANE), bf16),
            VMEM((4, 4, 32, 2 * LANE), bf16), VMEM((4, 2, 16, 2 * LANE), bf16), VMEM((4, 2, 32, 2 * LANE), bf16),
            VMEM((16, 16, LANE), bf16), VMEM((16, 16, LANE), bf16),
            VMEM((8, 256), f32), VMEM((16, 8, 256), f32), VMEM((8, 8, 256), f32),
            dma((6,)), dma((16,)), dma((16,)), dma((4, 2)), dma((4, 2)), dma((4, 2)), dma((4, 2)), dma((4, 4)), dma((4, 4)),
            dma((16,)), dma((16,)), dma((8,)), dma((8,)), dma((16,)), dma((16,)), dma((1,)), dma((1,)),
            dma((4,)), dma((4,)), dma((4, 2)), dma((4, 2)), dma((4, 2)), dma((4, 2)), dma((16,)), dma((16,)),
        ],
        compiler_params=pltpu.CompilerParams(
            collective_id=1, has_side_effects=True, vmem_limit_bytes=56 * 1024 * 1024
        ),
    )(
        hidden_out, norm_gain.reshape(-1, 128), router.T, choices.T,
        w_gate[0], w_up[0], w_down[0],
    )
    block = pl.BlockSpec((128, 2 * LANE), lambda i: (0, i))
    hidden_kept, moe_out, load, bias_next = pl.pallas_call(
        mix_kernel,
        name="mix",
        grid=(4,),
        out_shape=(
            jax.ShapeDtypeStruct((128, 7168), bf16),
            jax.ShapeDtypeStruct((128, 7168), bf16),
            jax.ShapeDtypeStruct((2, 128), f32),
            jax.ShapeDtypeStruct((2, 128), f32),
        ),
        in_specs=[block] + [vmem] * 4,
        out_specs=(block, block, vmem, vmem),
    )(hidden_out, back, coeff, counts, router_bias.reshape(2, 128))
    return hidden_kept, moe_out, load.reshape(-1), bias_next.reshape(-1)


def on_device(
    attn_out, residual, w_out, norm_gain, router, router_bias, choices, w_gate, w_up, w_down
):
    hidden_out = project(attn_out, w_out, residual)
    return experts(hidden_out, norm_gain, router, router_bias, choices, w_gate, w_up, w_down)


def solution(mesh):
    placed = (
        P("ep", "tp"),
        P(("ep", "tp"), None),
        P("tp", None),
        P(),
        P(None, "tp"),
        P(),
        P(("ep", "tp"), None),
        P("tp", None, "ep"),
        P("tp", None, "ep"),
        P("tp", "ep", None),
    )
    return jax.shard_map(
        on_device,
        mesh=mesh,
        in_specs=placed,
        out_specs=(P(("ep", "tp"), None), P(("ep", "tp"), None), P(), P()),
        check_vma=False,
    )
```

```python
import jax
import jax.numpy as jnp
from jax import lax
from jax.experimental import pallas as pl
from jax.experimental.pallas import tpu as pltpu
from jax.sharding import PartitionSpec as P

TOP = 8


norm_eps = 1e-06
route_scale = 2.5
bias_rate = 0.001


MESH = pl.DeviceIdType.MESH
VMEM = pltpu.VMEM
ROUNDS = 7
SHARED = 5
CH = 256


def ring(i):
    return lax.rem(i + 8, 4)


def place():
    tp = lax.axis_index("tp")
    ep = lax.axis_index("ep")
    return lax.div(tp, 4), lax.rem(tp, 4), lax.div(ep, 2), lax.rem(ep, 2)


def at(z, y, x, c):
    return (ring(z) * 4 + ring(y), ring(x) * 2 + lax.rem(c, 2))


def greet(peers):
    barrier = pltpu.get_barrier_semaphore()
    for peer in peers:
        pl.semaphore_signal(barrier, inc=1, device_id=peer, device_id_type=MESH)
    pl.semaphore_wait(barrier, len(peers))


def remote(src, dst, send, recv, peer):
    return pltpu.make_async_remote_copy(
        src_ref=src, dst_ref=dst, send_sem=send, recv_sem=recv, device_id=peer, device_id_type=MESH
    )


def project_kernel(
    a_ref, w_ref, res_ref, out_ref,
    ag, wown, wbuf, pbuf, half_in, full_in, resv,
    loc, a_s, a_r, y_s, y_r, g_s, g_r, v_s, v_r, x_s, x_r, f_s, f_r, c_s, c_r, h_s, h_r, z_s, z_r,
):
    z, y, x, c = place()
    half = pl.multiple_of(c * 256, 256)
    own_a = pltpu.make_async_copy(a_ref.at[:, y], ag.at[0, 0], loc.at[0])
    own_b = pltpu.make_async_copy(a_ref.at[z], ag.at[1, 0], loc.at[3])
    own_w = pltpu.make_async_copy(w_ref, wown, loc.at[1])
    own_res = pltpu.make_async_copy(res_ref, resv, loc.at[2])
    own_a.start()
    own_b.start()
    own_w.start()
    own_res.start()
    greet(
        [at(z, y + e, x, c) for e in (1, 2, 3)]
        + [at(z + e, y, x, c) for e in (1, 2, 3)]
        + [at(z, y, x + 1, c), at(z, y, x - 1, c), at(z, y, x, c + 1)]
    )
    sib = at(z, y, x, c + 1)

    def gather_at(kind, i):
        return at(z + i * kind, y + i * (1 - kind), x, c)

    def sum_at(kind, i):
        return at(z + i * (1 - kind), y + i * kind, x, c)

    def sum_place(kind):
        return z * (1 - kind) + y * kind

    def chunk(dx, r):
        return ring(x + dx) * ROUNDS + r

    def y_copy(i, n, way):
        cols = pl.ds(pl.multiple_of(n * CH, CH), CH)
        return remote(
            w_ref.at[pl.ds(half, 256), cols], wbuf.at[n, 2 - 2 * way, pl.ds(half, 256), :],
            y_s.at[i, way], y_r.at[i, way], gather_at(lax.rem(i, 2), 1 - 2 * way),
        )

    def y_land(i, n, way):
        part = wbuf.at[n, 2 - 2 * way, pl.ds(half, 256), :]
        return remote(part, part, y_s.at[i, way], y_r.at[i, way], at(z, y + 1, x, c))

    def g_copy(i, n, way):
        rows = pl.ds(pl.multiple_of(half + 128 * way, 128), 128)
        return remote(
            wbuf.at[n, 2 - 2 * way, rows, :], wbuf.at[n, 1, rows, :],
            g_s.at[i, way], g_r.at[i, way], gather_at(lax.rem(i, 2), 1 - 2 * way),
        )

    def common(u):
        return lax.div(u, 2) * ROUNDS + SHARED + lax.rem(u, 2)

    def v_copy(u):
        part = wbuf.at[common(u), :, pl.ds(half, 256), :]
        return remote(part, part, v_s.at[u], v_r.at[u], sib)

    def v_land(u):
        part = wbuf.at[common(u), :, pl.ds(pl.multiple_of(256 - half, 256), 256), :]
        return remote(part, part, v_s.at[u], v_r.at[u], sib)

    def a_copy(kind, g, e):
        rows = a_ref.at[ring(z + e), g] if kind else a_ref.at[g, ring(y + e)]
        return remote(
            rows, ag.at[kind, 4 - e, g], a_s.at[kind, g, e - 1], a_r.at[kind, g, 3 - e], gather_at(kind, e)
        )

    def x_copy(r, way):
        part = wbuf.at[chunk(0, r), :, pl.ds(half, 256), :]
        return remote(part, part, x_s.at[r, way], x_r.at[r, way], at(z, y, x + 1 - 2 * way, c))

    def x_land(r, way):
        part = wbuf.at[chunk(2 * way - 1, r), :, pl.ds(half, 256), :]
        return remote(part, part, x_s.at[r, way], x_r.at[r, way], at(z, y, x + 1 - 2 * way, c))

    def f_part(dx, r, way):
        return wbuf.at[chunk(dx, r), :, pl.ds(pl.multiple_of(half + 128 * way, 128), 128), :]

    def f_copy(r, way):
        part = f_part(2 * way - 1, r, way)
        return remote(part, part, f_s.at[r, way], f_r.at[r, way], at(z, y, x + 1 - 2 * way, c))

    def f_land(r, way):
        part = f_part(2, r, way)
        return remote(part, part, f_s.at[r, way], f_r.at[r, way], at(z, y, x + 1 - 2 * way, c))

    def hop(q):
        return (0, 3, 1, 2)[q]

    def c_copy(r, q):
        part = wbuf.at[chunk(hop(q), r), :, pl.ds(half, 256), :]
        return remote(part, part, c_s.at[r, q], c_r.at[r, q], sib)

    def c_land(n, r, q):
        other = pl.multiple_of(256 - half, 256)
        part = wbuf.at[n, :, pl.ds(other, 256), :]
        return remote(part, part, c_s.at[r, q], c_r.at[r, q], sib)

    def halves(way):
        return pl.ds(64 * way, 64)

    def h_copy(n, kind, way):
        return remote(
            pbuf.at[n, ring(sum_place(kind) + 2), halves(way)], half_in.at[n, way],
            h_s.at[n, way], h_r.at[n, way], sum_at(kind, 1 - 2 * way),
        )

    def z_copy(n, kind, way):
        return remote(
            pbuf.at[n, ring(sum_place(kind) + 1 - 2 * way)], full_in.at[n, way],
            z_s.at[n, way], z_r.at[n, way], sum_at(kind, 1 - 2 * way),
        )

    def start_y(i, n):
        for way in (0, 1):
            y_copy(i, n, way).start()

    def start_a(g):
        for e in (2, 1, 3):
            for kind in (0, 1):
                a_copy(kind, g, e).start()

    def pass_on(i, n):
        for way in (0, 1):
            y_land(i, n, way).wait_recv()
            g_copy(i, n, way).start()

    def first(r):
        for way in (0, 1):
            g_copy(r, chunk(0, r), way).wait_recv()
        x_copy(r, 0).start()
        x_copy(r, 1).start()
        c_copy(r, 0).start()

    def multiply(n, kind):
        cols = pl.ds(pl.multiple_of(n * CH, CH), CH)
        total = jnp.dot(ag[kind, 0].reshape(512, 512), wown[:, cols], preferred_element_type=jnp.float32)
        for k in range(3):
            total += jnp.dot(ag[kind, k + 1].reshape(512, 512), wbuf[n, k], preferred_element_type=jnp.float32)
        pbuf[n] = total.astype(jnp.bfloat16).reshape(4, 128, CH)
        for way in (0, 1):
            h_copy(n, kind, way).start()

    def combine(n, kind):
        for way in (0, 1):
            to = ring(sum_place(kind) + 1 - 2 * way)
            h_copy(n, kind, way).wait_recv()
            both = pbuf[n, to, halves(way)].astype(jnp.float32) + half_in[n, way].astype(jnp.float32)
            pbuf[n, to, halves(way)] = both.astype(jnp.bfloat16)
            z_copy(n, kind, way).start()

    def finish(n, kind):
        cols = pl.ds(pl.multiple_of(n * CH, CH), CH)
        total = pbuf[n, sum_place(kind)].astype(jnp.float32)
        for way in (0, 1):
            z_copy(n, kind, way).wait_recv()
            total += full_in[n, way].astype(jnp.float32)
        out_ref[:, cols] = (resv[:, cols].astype(jnp.float32) + total).astype(jnp.bfloat16)

    def near(q, r):
        return chunk(q + lax.div(q, 2), r)

    def step(work, r):
        @pl.when((r >= 0) & (r < SHARED))
        def _():
            @pl.loop(0, 3)
            def _(q):
                work(near(q, r), lax.rem(r, 2))

        @pl.when((r >= 2) & (r < 6))
        def _():
            for k in (0, 1):
                work(common(2 * r - 4 + k), 1 - k)

        @pl.when((r >= 1) & (r <= SHARED))
        def _():
            work(chunk(2, r - 1), lax.rem(r - 1, 2))

    start_y(0, chunk(0, 0))
    start_y(1, chunk(0, 1))
    pass_on(0, chunk(0, 0))
    pass_on(1, chunk(0, 1))
    start_a(0)
    start_a(1)
    start_a(2)
    first(0)
    first(1)
    start_y(2, chunk(0, 2))
    start_y(3, chunk(0, 3))
    start_a(3)
    own_a.wait()
    own_b.wait()
    own_w.wait()
    own_res.wait()

    def multiply_near(r):
        @pl.loop(0, 3)
        def _(q):
            n = near(q, r)
            c_land(n, r, lax.rem(3 - q, 3)).wait_recv()
            multiply(n, lax.rem(r, 2))

    @pl.loop(0, SHARED + 4)
    def _(r):
        @pl.when(r < SHARED)
        def _():
            for way in (0, 1):
                x_land(r, way).wait_recv()
                f_copy(r, way).start()
                c_copy(r, 1 + way).start()

        @pl.when(r == 0)
        def _():
            pass_on(2, chunk(0, 2))
            pass_on(3, chunk(0, 3))

        @pl.when((r >= 1) & (r + 3 < SHARED))
        def _():
            pass_on(r + 3, chunk(0, r + 3))

        @pl.when(r + 2 < SHARED)
        def _():
            first(r + 2)

        @pl.when(r == 0)
        def _():
            start_y(4, chunk(0, 4))

        @pl.when(r < 4)
        def _():
            for k in (0, 1):
                start_y(SHARED + 2 * r + k, common(2 * r + k))

        @pl.when((r >= 1) & (r < 5))
        def _():
            for k in (0, 1):
                pass_on(SHARED + 2 * r - 2 + k, common(2 * r - 2 + k))

        @pl.when((r >= 2) & (r < 6))
        def _():
            for k in (0, 1):
                u = 2 * r - 4 + k
                for way in (0, 1):
                    g_copy(SHARED + u, common(u), way).wait_recv()
                v_copy(u).start()

        @pl.when(r == 1)
        def _():
            for g in range(4):
                for k in range(3):
                    for kind in (0, 1):
                        part = ag.at[kind, k + 1, g]
                        remote(part, part, a_s.at[kind, g, k], a_r.at[kind, g, k], at(z, y + 1, x, c)).wait_recv()
            multiply_near(0)

        @pl.when((r >= 1) & (r < SHARED))
        def _():
            multiply_near(r)

        @pl.when((r >= 1) & (r <= SHARED))
        def _():
            for way in (0, 1):
                f_land(r - 1, way).wait_recv()
            c_copy(r - 1, 3).start()

        @pl.when(r >= 2)
        def _():
            step(combine, r - 1)

        @pl.when(r == 2)
        def _():
            @pl.loop(0, 3)
            def _(q):
                combine(near(q, 0), 0)

        @pl.when(r >= 3)
        def _():
            step(finish, r - 3)

        @pl.when((r >= 2) & (r < 6))
        def _():
            for k in (0, 1):
                u = 2 * r - 4 + k
                v_land(u).wait_recv()
                multiply(common(u), 1 - k)

        @pl.when((r >= 1) & (r <= SHARED))
        def _():
            c_land(chunk(2, r - 1), r - 1, 3).wait_recv()
            multiply(chunk(2, r - 1), lax.rem(r - 1, 2))

    for g in range(4):
        for e in (1, 2, 3):
            for kind in (0, 1):
                a_copy(kind, g, e).wait_send()

    @pl.loop(0, SHARED)
    def _(r):
        for way in (0, 1):
            y_copy(r, chunk(0, r), way).wait_send()
            g_copy(r, chunk(0, r), way).wait_send()
            x_copy(r, way).wait_send()
            f_copy(r, way).wait_send()
        for q in range(4):
            c_copy(r, q).wait_send()

    @pl.loop(0, 8)
    def _(u):
        for way in (0, 1):
            y_copy(SHARED + u, common(u), way).wait_send()
            g_copy(SHARED + u, common(u), way).wait_send()
        v_copy(u).wait_send()

    @pl.loop(0, 4 * ROUNDS)
    def _(n):
        for way in (0, 1):
            h_copy(n, 0, way).wait_send()
            z_copy(n, 0, way).wait_send()


def project(attn_out, w_out, residual):
    dma = pltpu.SemaphoreType.DMA
    anywhere = pl.BlockSpec(memory_space=pl.ANY)
    return pl.pallas_call(
        project_kernel,
        name="project",
        out_shape=jax.ShapeDtypeStruct((128, 7168), jnp.bfloat16),
        in_specs=[anywhere] * 3,
        out_specs=pl.BlockSpec(memory_space=VMEM),
        scratch_shapes=[
            VMEM((2, 4, 4, 128, 512), jnp.bfloat16),
            VMEM((512, 7168), jnp.bfloat16),
            VMEM((28, 3, 512, CH), jnp.bfloat16),
            VMEM((28, 4, 128, CH), jnp.bfloat16),
            VMEM((28, 2, 64, CH), jnp.bfloat16),
            VMEM((28, 2, 128, CH), jnp.bfloat16),
            VMEM((128, 7168), jnp.bfloat16),
            dma((4,)), dma((2, 4, 3)), dma((2, 4, 3)), dma((13, 2)), dma((13, 2)), dma((13, 2)), dma((13, 2)),
            dma((8,)), dma((8,)), dma((5, 2)), dma((5, 2)), dma((5, 2)), dma((5, 2)), dma((5, 4)), dma((5, 4)),
            dma((28, 2)), dma((28, 2)), dma((28, 2)), dma((28, 2)),
        ],
        compiler_params=pltpu.CompilerParams(
            collective_id=0, has_side_effects=True, vmem_limit_bytes=58 * 1024 * 1024
        ),
    )(attn_out.reshape(4, 4, 128, 512), w_out, residual)


LANE = 896
GROUPS = ((0, 0), (1, 1), (2, 3), (3, 2))


def moe_kernel(
    hid_ref, gain_ref, rout_ref, cho_ref, wg_ref, wu_ref, wd_ref,
    back_ref, coeff_ref, count_ref,
    wg, wu, wd, rt, normed, gain, snd, land, rows, ybuf, r1, sbuf, half_in, full_in, rsend, ret, cnt, cnt_tp, cnt_ep,
    loc, d_s, d_r, ax_s, ax_r, af_s, af_r, ac_s, ac_r, k_s, k_r, l_s, l_r, rt_s, rt_r, rs_s, rs_r,
    p_s, p_r, h_s, h_r, q_s, q_r, b_s, b_r,
):
    z, y, x, c = place()
    tp = z * 4 + y
    ep = x * 2 + c
    sib = at(z, y, x, c + 1)
    width = hid_ref.shape[1]
    half = pl.ds(pl.multiple_of(c * (width // 2), width // 2), width // 2)
    loads = [pltpu.make_async_copy(s, d, loc.at[i]) for i, (s, d) in enumerate(((wg_ref, wg), (wu_ref, wu), (wd_ref, wd)))]
    for load in loads:
        load.start()
    tp_peers = [(dz, dy) for dz in (0, 1, 3, 2) for dy in (1, 3, 2, 0) if (dz, dy) != (0, 0)]
    ep_peers = [(dx, dc) for dx in (0, 1, 3, 2) for dc in (0, 1) if (dx, dc) != (0, 0)]

    def tp_at(dz, dy):
        return ring(z + dz) * 4 + ring(y + dy)

    def ep_at(dx, dc):
        return ring(x + dx) * 2 + lax.rem(c + dc, 2)

    barrier = pltpu.get_barrier_semaphore()
    for p in tp_peers:
        pl.semaphore_signal(barrier, inc=1, device_id=(tp_at(*p), ep), device_id_type=MESH)
    for p in ep_peers:
        pl.semaphore_signal(barrier, inc=1, device_id=(tp, ep_at(*p)), device_id_type=MESH)

    def cut(j):
        return slice(j * LANE, (j + 1) * LANE)

    row = lax.broadcasted_iota(jnp.int32, (256, 128), 0)
    lane = lax.broadcasted_iota(jnp.int32, (256, 128), 1)
    expert = row // 16
    member = jnp.zeros((256, 128), jnp.float32)
    for k in range(TOP):
        ck = cho_ref[k : k + 1, :]
        member += jnp.where(ck == expert, 1.0, 0.0)
    before = jnp.where(row[:128] < lane[:128], 1.0, 0.0).astype(jnp.bfloat16)
    rank = jnp.dot(member.astype(jnp.bfloat16), before, preferred_element_type=jnp.float32)
    slot = ((row // 8) % 2).astype(jnp.float32)
    pick = jnp.where(rank == slot, member, 0.0)
    feature = row % 8
    picked = jnp.zeros((256, LANE), jnp.float32)
    for j in range(8):
        pj = jnp.where(feature == j, pick, 0.0).astype(jnp.bfloat16)
        picked += jnp.dot(pj, hid_ref[:, cut(j)], preferred_element_type=jnp.float32)
    gains = gain_ref[...].astype(jnp.float32)
    for j in range(8):
        for i in range(7):
            gain[j : j + 1, i * 128 : (i + 1) * 128] = gains[j * 7 + i : j * 7 + i + 1, :]
    picked = picked.reshape(32, 8, LANE)
    ssq = jnp.sum(jnp.sum(picked * picked, axis=2, keepdims=True), axis=1, keepdims=True)
    outgoing = picked * lax.rsqrt(ssq / width + norm_eps) * gain[...][None]
    snd[...] = outgoing.astype(jnp.bfloat16).reshape(16, 16, LANE)
    contract_last = (((1,), (1,)), ((), ()))
    pl.semaphore_wait(barrier, len(tp_peers) + len(ep_peers))

    def d_copy(p):
        peer = tp_at(*p)
        return remote(snd.at[peer], land.at[ep, tp], d_s.at[peer], d_r.at[tp], (peer, ep))

    own_rows = pltpu.make_async_copy(snd.at[tp], land.at[ep, tp], loc.at[3])
    own_rows.start()
    for p in tp_peers:
        d_copy(p).start()

    named = jnp.zeros((256, 128), jnp.float32)
    for k in range(TOP):
        named += jnp.where(cho_ref[k : k + 1, :] == row, 1.0, 0.0)
    cnt[...] = lax.dot_general(
        jnp.ones((8, 128), jnp.bfloat16), named.astype(jnp.bfloat16), contract_last, preferred_element_type=jnp.float32
    )

    def k_copy(p):
        peer = tp_at(*p)
        return remote(cnt, cnt_tp.at[tp], k_s.at[peer], k_r.at[tp], (peer, ep))

    for p in tp_peers:
        k_copy(p).start()

    def group(dz):
        return pl.ds(pl.multiple_of(ring(z + dz) * 4, 4), 4)

    def x_copy(g, dz, way):
        part = land.at[ep, group(dz)]
        return remote(part, part, ax_s.at[g, way], ax_r.at[g, way], (tp, ep_at(1 - 2 * way, 0)))

    def x_land(g, dz, way):
        part = land.at[ep_at(2 * way - 1, 0), group(dz)]
        return remote(part, part, ax_s.at[g, way], ax_r.at[g, way], (tp, ep_at(1, 0)))

    def f_rows(dx, dz, way):
        return land.at[ep_at(dx, 0), pl.ds(pl.multiple_of(ring(z + dz) * 4 + 2 * way, 2), 2)]

    def f_copy(g, dz, way):
        part = f_rows(2 * way - 1, dz, way)
        return remote(part, part, af_s.at[g, way], af_r.at[g, way], (tp, ep_at(1 - 2 * way, 0)))

    def f_land(g, dz, way):
        part = f_rows(2, dz, way)
        return remote(part, part, af_s.at[g, way], af_r.at[g, way], (tp, ep_at(1, 0)))

    def c_copy(g, dz, q):
        part = land.at[ep_at(q, 0), group(dz)]
        return remote(part, part, ac_s.at[g, q], ac_r.at[g, q], sib)

    def c_land(g, dz, q):
        part = land.at[ep_at(q, 1), group(dz)]
        return remote(part, part, ac_s.at[g, q], ac_r.at[g, q], sib)

    def d_land(p):
        src = tp_at(*p)
        return remote(snd.at[src], land.at[ep, src], d_s.at[src], d_r.at[src], (src, ep))

    for g, dz in GROUPS:
        for p in tp_peers:
            if p[0] == dz:
                d_land(p).wait_recv()
        if dz == 0:
            own_rows.wait()
        for way in (0, 1):
            x_copy(g, dz, way).start()
        c_copy(g, dz, 0).start()

    def rt_copy(p):
        peer = tp_at(*p)
        return remote(rout_ref.at[:, half], rt.at[tp, :, half], rt_s.at[peer], rt_r.at[tp], (peer, ep))

    own_rt = pltpu.make_async_copy(rout_ref.at[:, half], rt.at[tp, :, half], loc.at[4])
    own_rt.start()
    for p in tp_peers:
        rt_copy(p).start()

    for p in tp_peers:
        src = tp_at(*p)
        remote(cnt, cnt_tp.at[src], k_s.at[src], k_r.at[src], (src, ep)).wait_recv()
    cnt_tp[tp] = cnt[...]
    part_sum = cnt_tp[0]
    for i in range(1, 16):
        part_sum += cnt_tp[i]
    cnt_ep[ep] = part_sum

    def l_copy(p):
        peer = ep_at(*p)
        return remote(cnt_ep.at[ep], cnt_ep.at[ep], l_s.at[peer], l_r.at[ep], (tp, peer))

    for p in ep_peers:
        l_copy(p).start()

    out_row = lax.broadcasted_iota(jnp.int32, (128, 128), 0)
    in_row = lax.broadcasted_iota(jnp.int32, (128, 128), 1)
    source = ((out_row % 16) // 2) * 16 + (out_row % 2) * 8 + out_row // 16
    perm = jnp.where(in_row == source, 1.0, 0.0).astype(jnp.bfloat16)

    def turn_rows(group_of):
        for part in range(2):
            block = land[group_of, part * 8 : part * 8 + 8].reshape(128, LANE)
            turned = jnp.dot(perm, block, preferred_element_type=jnp.float32).astype(jnp.bfloat16)
            to = pl.ds(pl.multiple_of(group_of * 32 + part * 16, 16), 16)
            rows[:, to, :] = turned.reshape(8, 16, LANE)

    turn_rows(ep)
    for g, dz in GROUPS:
        for way in (0, 1):
            x_land(g, dz, way).wait_recv()
            f_copy(g, dz, way).start()
            c_copy(g, dz, 3 - 2 * way).start()
    for q in (0, 3, 1):
        if q:
            turn_rows(ep_at(q, 0))
        if q == 1:
            for g, dz in GROUPS:
                for way in (0, 1):
                    f_land(g, dz, way).wait_recv()
                c_copy(g, dz, 2).start()
        for g, dz in GROUPS:
            c_land(g, dz, q).wait_recv()
        turn_rows(ep_at(q, 1))
    turn_rows(ep_at(2, 0))
    for g, dz in GROUPS:
        c_land(g, dz, 2).wait_recv()
    turn_rows(ep_at(2, 1))

    for load in loads:
        load.wait()
    gate_val = jnp.zeros((256, 256), jnp.float32)
    up_val = jnp.zeros((256, 256), jnp.float32)
    for j in range(8):
        gate_val += jnp.dot(rows[j], wg[cut(j), :], preferred_element_type=jnp.float32)
        up_val += jnp.dot(rows[j], wu[cut(j), :], preferred_element_type=jnp.float32)
    active = (gate_val / (1.0 + jnp.exp(-gate_val)) * up_val).astype(jnp.bfloat16)

    def p_copy(n):
        return remote(ybuf.at[n, :, 1 - c], r1.at[n], p_s.at[n], p_r.at[n], sib)

    def h_copy(n, way):
        rows_of = pl.ds(16 * way, 16)
        return remote(
            sbuf.at[n, ring(x + 2), rows_of], half_in.at[n, way],
            h_s.at[n, way], h_r.at[n, way], (tp, ep_at(1 - 2 * way, 0)),
        )

    def q_copy(n, way):
        to = 1 - 2 * way
        return remote(
            sbuf.at[n, ring(x + to)], full_in.at[n, way], q_s.at[n, way], q_r.at[n, way], (tp, ep_at(to, 0))
        )

    def forward(n):
        for way in (0, 1):
            to = ring(x + 1 - 2 * way)
            h_copy(n, way).wait_recv()
            rows_of = slice(16 * way, 16 * way + 16)
            both = sbuf[n, to, rows_of].astype(jnp.float32) + half_in[n, way].astype(jnp.float32)
            sbuf[n, to, rows_of] = both.astype(jnp.bfloat16)
            q_copy(n, way).start()

    for n in range(4):
        part = jnp.dot(active, wd[:, n * 2 * LANE : (n + 1) * 2 * LANE], preferred_element_type=jnp.float32)
        ybuf[n] = part.astype(jnp.bfloat16).reshape(4, 2, 32, 2 * LANE)
        p_copy(n).start()
    for n in range(4):
        p_copy(n).wait_recv()
        for i in range(4):
            both = ybuf[n, i, c].astype(jnp.float32) + r1[n, i].astype(jnp.float32)
            sbuf[n, i] = both.astype(jnp.bfloat16)
        for way in (0, 1):
            h_copy(n, way).start()
        if n:
            forward(n - 1)
    forward(3)

    for p in ep_peers:
        peer = ep_at(*p)
        remote(cnt_ep.at[peer], cnt_ep.at[peer], l_s.at[peer], l_r.at[peer], (tp, peer)).wait_recv()
    counts = cnt_ep[0]
    for i in range(1, 8):
        counts += cnt_ep[i]
    count_ref[...] = counts

    for p in tp_peers:
        src = tp_at(*p)
        remote(rout_ref.at[:, half], rt.at[src, :, half], rt_s.at[src], rt_r.at[src], (src, ep)).wait_recv()
    own_rt.wait()
    mine = rt.at[:, :, half]
    rt_sib = remote(mine, mine, rs_s.at[0], rs_r.at[0], sib)
    rt_sib.start()
    other = rt.at[:, :, pl.ds(pl.multiple_of((1 - c) * (width // 2), width // 2), width // 2)]
    ssq = jnp.zeros((128, 1), jnp.float32)
    for j in range(8):
        h = hid_ref[:, cut(j)].astype(jnp.float32)
        ssq += jnp.sum(h * h, axis=1, keepdims=True)
    scale = lax.rsqrt(ssq / width + norm_eps)
    for j in range(8):
        h = hid_ref[:, cut(j)].astype(jnp.float32)
        normed[:, cut(j)] = (h * scale * gain[j : j + 1, :]).astype(jnp.bfloat16)
    remote(other, other, rs_s.at[0], rs_r.at[0], sib).wait_recv()
    logits = jnp.zeros((256, 128), jnp.float32)
    for j in range(8):
        logits += lax.dot_general(
            rt[:, :, cut(j)].reshape(256, LANE), normed[:, cut(j)], contract_last, preferred_element_type=jnp.float32
        )
    scores = 1.0 / (1.0 + jnp.exp(-logits))
    chosen = []
    for k in range(TOP):
        hit = cho_ref[k : k + 1, :] == row
        chosen.append(jnp.sum(jnp.where(hit, scores, 0.0), axis=0, keepdims=True))
    norm_by = chosen[0]
    for k in range(1, TOP):
        norm_by = norm_by + chosen[k]
    weight = jnp.zeros((256, 128), jnp.float32)
    for k in range(TOP):
        weight += jnp.where(cho_ref[k : k + 1, :] == expert, route_scale * chosen[k] / norm_by, 0.0)
    coeff_ref[...] = jnp.where(pick > 0.0, weight, 0.0).T

    back_row = lax.broadcasted_iota(jnp.int32, (256, 32), 0)
    back_col = lax.broadcasted_iota(jnp.int32, (256, 32), 1)
    returned = jnp.zeros((256, LANE), jnp.float32)
    for n in range(4):
        total = sbuf[n, x].astype(jnp.float32)
        for way in (0, 1):
            q_copy(n, way).wait_recv()
            total += full_in[n, way].astype(jnp.float32)
        total = total.astype(jnp.bfloat16)
        for i in range(2):
            turn = jnp.where((back_row // 8 == back_col) & (back_row % 8 == 2 * n + i), 1.0, 0.0).astype(jnp.bfloat16)
            returned += jnp.dot(turn, total[:, cut(i)], preferred_element_type=jnp.float32)
    rsend[...] = returned.astype(jnp.bfloat16).reshape(16, 16, LANE)

    def b_copy(p):
        peer = tp_at(*p)
        return remote(rsend.at[peer], ret.at[tp], b_s.at[peer], b_r.at[tp], (peer, ep))

    own_back = pltpu.make_async_copy(rsend.at[tp], ret.at[tp], loc.at[5])
    own_back.start()
    for p in tp_peers:
        b_copy(p).start()
    own_back.wait()
    for p in tp_peers:
        src = tp_at(*p)
        remote(rsend.at[src], ret.at[src], b_s.at[src], b_r.at[src], (src, ep)).wait_recv()
    back_ref[...] = ret[...]

    for p in tp_peers:
        d_copy(p).wait_send()
        k_copy(p).wait_send()
        rt_copy(p).wait_send()
        b_copy(p).wait_send()
    for p in ep_peers:
        l_copy(p).wait_send()
    rt_sib.wait_send()
    for g, dz in GROUPS:
        for way in (0, 1):
            x_copy(g, dz, way).wait_send()
            f_copy(g, dz, way).wait_send()
        for q in range(4):
            c_copy(g, dz, q).wait_send()
    for n in range(4):
        p_copy(n).wait_send()
        for way in (0, 1):
            h_copy(n, way).wait_send()
            q_copy(n, way).wait_send()


def mix_kernel(hid_ref, back_ref, coeff_ref, count_ref, bias_ref, kept_ref, moe_ref, load_ref, next_ref):
    i = pl.program_id(0)
    kept_ref[...] = hid_ref[...]

    @pl.when(i == 0)
    def _():
        slots = 128.0 * 128.0 * TOP
        for k in range(2):
            counts = count_ref[0:1, k * 128 : (k + 1) * 128]
            load_ref[k : k + 1, :] = counts * 256.0 / slots
            gap = slots - counts * 256.0
            sign = jnp.where(gap > 0.0, 1.0, jnp.where(gap < 0.0, -1.0, 0.0))
            next_ref[k : k + 1, :] = bias_ref[k : k + 1, :] + bias_rate * sign

    back = back_ref[...].reshape(256, LANE)
    coeff = coeff_ref[...]
    lane_cut = lax.broadcasted_iota(jnp.int32, (128, 256), 1) % 8
    for k in range(2):
        here = lane_cut == 2 * i + k
        mixed = jnp.dot(jnp.where(here, coeff, 0.0).astype(jnp.bfloat16), back, preferred_element_type=jnp.float32)
        moe_ref[:, k * LANE : (k + 1) * LANE] = mixed.astype(jnp.bfloat16)


def experts(hidden_out, norm_gain, router, router_bias, choices, w_gate, w_up, w_down):
    dma = pltpu.SemaphoreType.DMA
    bf16, f32 = jnp.bfloat16, jnp.float32
    vmem = pl.BlockSpec(memory_space=VMEM)
    anywhere = pl.BlockSpec(memory_space=pl.ANY)
    back, coeff, counts = pl.pallas_call(
        moe_kernel,
        name="experts",
        out_shape=(
            jax.ShapeDtypeStruct((16, 16, LANE), bf16),
            jax.ShapeDtypeStruct((128, 256), f32),
            jax.ShapeDtypeStruct((8, 256), f32),
        ),
        in_specs=[vmem] * 4 + [anywhere] * 3,
        out_specs=(vmem,) * 3,
        scratch_shapes=[
            VMEM((7168, 256), bf16), VMEM((7168, 256), bf16), VMEM((256, 7168), bf16),
            VMEM((16, 16, 7168), bf16), VMEM((128, 7168), bf16), VMEM((8, LANE), f32), VMEM((16, 16, LANE), bf16),
            VMEM((8, 16, 16, LANE), bf16), VMEM((8, 256, LANE), bf16),
            VMEM((4, 4, 2, 32, 2 * LANE), bf16), VMEM((4, 4, 32, 2 * LANE), bf16),
            VMEM((4, 4, 32, 2 * LANE), bf16), VMEM((4, 2, 16, 2 * LANE), bf16), VMEM((4, 2, 32, 2 * LANE), bf16),
            VMEM((16, 16, LANE), bf16), VMEM((16, 16, LANE), bf16),
            VMEM((8, 256), f32), VMEM((16, 8, 256), f32), VMEM((8, 8, 256), f32),
            dma((6,)), dma((16,)), dma((16,)), dma((4, 2)), dma((4, 2)), dma((4, 2)), dma((4, 2)), dma((4, 4)), dma((4, 4)),
            dma((16,)), dma((16,)), dma((8,)), dma((8,)), dma((16,)), dma((16,)), dma((1,)), dma((1,)),
            dma((4,)), dma((4,)), dma((4, 2)), dma((4, 2)), dma((4, 2)), dma((4, 2)), dma((16,)), dma((16,)),
        ],
        compiler_params=pltpu.CompilerParams(
            collective_id=1, has_side_effects=True, vmem_limit_bytes=56 * 1024 * 1024
        ),
    )(
        hidden_out, norm_gain.reshape(-1, 128), router.T, choices.T,
        w_gate[0], w_up[0], w_down[0],
    )
    block = pl.BlockSpec((128, 2 * LANE), lambda i: (0, i))
    hidden_kept, moe_out, load, bias_next = pl.pallas_call(
        mix_kernel,
        name="mix",
        grid=(4,),
        out_shape=(
            jax.ShapeDtypeStruct((128, 7168), bf16),
            jax.ShapeDtypeStruct((128, 7168), bf16),
            jax.ShapeDtypeStruct((2, 128), f32),
            jax.ShapeDtypeStruct((2, 128), f32),
        ),
        in_specs=[block] + [vmem] * 4,
        out_specs=(block, block, vmem, vmem),
    )(hidden_out, back, coeff, counts, router_bias.reshape(2, 128))
    return hidden_kept, moe_out, load.reshape(-1), bias_next.reshape(-1)


def on_device(
    attn_out, residual, w_out, norm_gain, router, router_bias, choices, w_gate, w_up, w_down
):
    hidden_out = project(attn_out, w_out, residual)
    return experts(hidden_out, norm_gain, router, router_bias, choices, w_gate, w_up, w_down)


def solution(mesh):
    placed = (
        P("ep", "tp"),
        P(("ep", "tp"), None),
        P("tp", None),
        P(),
        P(None, "tp"),
        P(),
        P(("ep", "tp"), None),
        P("tp", None, "ep"),
        P("tp", None, "ep"),
        P("tp", "ep", None),
    )
    return jax.shard_map(
        on_device,
        mesh=mesh,
        in_specs=placed,
        out_specs=(P(("ep", "tp"), None), P(("ep", "tp"), None), P(), P()),
        check_vma=False,
    )
```

```python
import jax
import jax.numpy as jnp
from jax import lax
from jax.experimental import pallas as pl
from jax.experimental.pallas import tpu as pltpu
from jax.sharding import PartitionSpec as P

TOP = 8


norm_eps = 1e-06
route_scale = 2.5
bias_rate = 0.001


MESH = pl.DeviceIdType.MESH
VMEM = pltpu.VMEM
ROUNDS = 7
SHARED = 5
CH = 256


def ring(i):
    return lax.rem(i + 8, 4)


def place():
    tp = lax.axis_index("tp")
    ep = lax.axis_index("ep")
    return lax.div(tp, 4), lax.rem(tp, 4), lax.div(ep, 2), lax.rem(ep, 2)


def at(z, y, x, c):
    return (ring(z) * 4 + ring(y), ring(x) * 2 + lax.rem(c, 2))


def greet(peers):
    barrier = pltpu.get_barrier_semaphore()
    for peer in peers:
        pl.semaphore_signal(barrier, inc=1, device_id=peer, device_id_type=MESH)
    pl.semaphore_wait(barrier, len(peers))


def remote(src, dst, send, recv, peer):
    return pltpu.make_async_remote_copy(
        src_ref=src, dst_ref=dst, send_sem=send, recv_sem=recv, device_id=peer, device_id_type=MESH
    )


def project_kernel(
    a_ref, w_ref, res_ref, out_ref,
    ag, wown, wbuf, pbuf, half_in, full_in, resv,
    loc, a_s, a_r, y_s, y_r, g_s, g_r, v_s, v_r, x_s, x_r, f_s, f_r, c_s, c_r, h_s, h_r, z_s, z_r,
):
    z, y, x, c = place()
    half = pl.multiple_of(c * 256, 256)
    own_a = pltpu.make_async_copy(a_ref.at[:, y], ag.at[0, 0], loc.at[0])
    own_b = pltpu.make_async_copy(a_ref.at[z], ag.at[1, 0], loc.at[3])
    own_w = pltpu.make_async_copy(w_ref, wown, loc.at[1])
    own_res = pltpu.make_async_copy(res_ref, resv, loc.at[2])
    own_a.start()
    own_b.start()
    own_w.start()
    own_res.start()
    greet(
        [at(z, y + e, x, c) for e in (1, 2, 3)]
        + [at(z + e, y, x, c) for e in (1, 2, 3)]
        + [at(z, y, x + 1, c), at(z, y, x - 1, c), at(z, y, x, c + 1)]
    )
    sib = at(z, y, x, c + 1)

    def gather_at(kind, i):
        return at(z + i * kind, y + i * (1 - kind), x, c)

    def sum_at(kind, i):
        return at(z + i * (1 - kind), y + i * kind, x, c)

    def sum_place(kind):
        return z * (1 - kind) + y * kind

    def chunk(dx, r):
        return ring(x + dx) * ROUNDS + r

    def y_copy(i, n, way):
        cols = pl.ds(pl.multiple_of(n * CH, CH), CH)
        return remote(
            w_ref.at[pl.ds(half, 256), cols], wbuf.at[n, 2 - 2 * way, pl.ds(half, 256), :],
            y_s.at[i, way], y_r.at[i, way], gather_at(lax.rem(i, 2), 1 - 2 * way),
        )

    def y_land(i, n, way):
        part = wbuf.at[n, 2 - 2 * way, pl.ds(half, 256), :]
        return remote(part, part, y_s.at[i, way], y_r.at[i, way], at(z, y + 1, x, c))

    def g_copy(i, n, way):
        rows = pl.ds(pl.multiple_of(half + 128 * way, 128), 128)
        return remote(
            wbuf.at[n, 2 - 2 * way, rows, :], wbuf.at[n, 1, rows, :],
            g_s.at[i, way], g_r.at[i, way], gather_at(lax.rem(i, 2), 1 - 2 * way),
        )

    def common(u):
        return lax.div(u, 2) * ROUNDS + SHARED + lax.rem(u, 2)

    def v_copy(u):
        part = wbuf.at[common(u), :, pl.ds(half, 256), :]
        return remote(part, part, v_s.at[u], v_r.at[u], sib)

    def v_land(u):
        part = wbuf.at[common(u), :, pl.ds(pl.multiple_of(256 - half, 256), 256), :]
        return remote(part, part, v_s.at[u], v_r.at[u], sib)

    def a_copy(kind, g, e):
        rows = a_ref.at[ring(z + e), g] if kind else a_ref.at[g, ring(y + e)]
        return remote(
            rows, ag.at[kind, 4 - e, g], a_s.at[kind, g, e - 1], a_r.at[kind, g, 3 - e], gather_at(kind, e)
        )

    def x_copy(r, way):
        part = wbuf.at[chunk(0, r), :, pl.ds(half, 256), :]
        return remote(part, part, x_s.at[r, way], x_r.at[r, way], at(z, y, x + 1 - 2 * way, c))

    def x_land(r, way):
        part = wbuf.at[chunk(2 * way - 1, r), :, pl.ds(half, 256), :]
        return remote(part, part, x_s.at[r, way], x_r.at[r, way], at(z, y, x + 1 - 2 * way, c))

    def f_part(dx, r, way):
        return wbuf.at[chunk(dx, r), :, pl.ds(pl.multiple_of(half + 128 * way, 128), 128), :]

    def f_copy(r, way):
        part = f_part(2 * way - 1, r, way)
        return remote(part, part, f_s.at[r, way], f_r.at[r, way], at(z, y, x + 1 - 2 * way, c))

    def f_land(r, way):
        part = f_part(2, r, way)
        return remote(part, part, f_s.at[r, way], f_r.at[r, way], at(z, y, x + 1 - 2 * way, c))

    def hop(q):
        return (0, 3, 1, 2)[q]

    def c_copy(r, q):
        part = wbuf.at[chunk(hop(q), r), :, pl.ds(half, 256), :]
        return remote(part, part, c_s.at[r, q], c_r.at[r, q], sib)

    def c_land(n, r, q):
        other = pl.multiple_of(256 - half, 256)
        part = wbuf.at[n, :, pl.ds(other, 256), :]
        return remote(part, part, c_s.at[r, q], c_r.at[r, q], sib)

    def halves(way):
        return pl.ds(64 * way, 64)

    def h_copy(n, kind, way):
        return remote(
            pbuf.at[n, ring(sum_place(kind) + 2), halves(way)], half_in.at[n, way],
            h_s.at[n, way], h_r.at[n, way], sum_at(kind, 1 - 2 * way),
        )

    def z_copy(n, kind, way):
        return remote(
            pbuf.at[n, ring(sum_place(kind) + 1 - 2 * way)], full_in.at[n, way],
            z_s.at[n, way], z_r.at[n, way], sum_at(kind, 1 - 2 * way),
        )

    def start_y(i, n):
        for way in (0, 1):
            y_copy(i, n, way).start()

    def start_a(g):
        for e in (2, 1, 3):
            for kind in (0, 1):
                a_copy(kind, g, e).start()

    def pass_on(i, n):
        for way in (0, 1):
            y_land(i, n, way).wait_recv()
            g_copy(i, n, way).start()

    def first(r):
        for way in (0, 1):
            g_copy(r, chunk(0, r), way).wait_recv()
        x_copy(r, 0).start()
        x_copy(r, 1).start()
        c_copy(r, 0).start()

    def multiply(n, kind):
        cols = pl.ds(pl.multiple_of(n * CH, CH), CH)
        total = jnp.dot(ag[kind, 0].reshape(512, 512), wown[:, cols], preferred_element_type=jnp.float32)
        for k in range(3):
            total += jnp.dot(ag[kind, k + 1].reshape(512, 512), wbuf[n, k], preferred_element_type=jnp.float32)
        pbuf[n] = total.astype(jnp.bfloat16).reshape(4, 128, CH)
        for way in (0, 1):
            h_copy(n, kind, way).start()

    def combine(n, kind):
        for way in (0, 1):
            to = ring(sum_place(kind) + 1 - 2 * way)
            h_copy(n, kind, way).wait_recv()
            both = pbuf[n, to, halves(way)].astype(jnp.float32) + half_in[n, way].astype(jnp.float32)
            pbuf[n, to, halves(way)] = both.astype(jnp.bfloat16)
            z_copy(n, kind, way).start()

    def finish(n, kind):
        cols = pl.ds(pl.multiple_of(n * CH, CH), CH)
        total = pbuf[n, sum_place(kind)].astype(jnp.float32)
        for way in (0, 1):
            z_copy(n, kind, way).wait_recv()
            total += full_in[n, way].astype(jnp.float32)
        out_ref[:, cols] = (resv[:, cols].astype(jnp.float32) + total).astype(jnp.bfloat16)

    def near(q, r):
        return chunk(q + lax.div(q, 2), r)

    def step(work, r):
        @pl.when((r >= 0) & (r < SHARED))
        def _():
            @pl.loop(0, 3)
            def _(q):
                work(near(q, r), lax.rem(r, 2))

        @pl.when((r >= 2) & (r < 6))
        def _():
            for k in (0, 1):
                work(common(2 * r - 4 + k), 1 - k)

        @pl.when((r >= 1) & (r <= SHARED))
        def _():
            work(chunk(2, r - 1), lax.rem(r - 1, 2))

    start_y(0, chunk(0, 0))
    start_y(1, chunk(0, 1))
    pass_on(0, chunk(0, 0))
    pass_on(1, chunk(0, 1))
    start_a(0)
    start_a(1)
    start_a(2)
    first(0)
    first(1)
    start_y(2, chunk(0, 2))
    start_y(3, chunk(0, 3))
    start_a(3)
    own_a.wait()
    own_b.wait()
    own_w.wait()
    own_res.wait()

    def multiply_near(r):
        @pl.loop(0, 3)
        def _(q):
            n = near(q, r)
            c_land(n, r, lax.rem(3 - q, 3)).wait_recv()
            multiply(n, lax.rem(r, 2))

    @pl.loop(0, SHARED + 4)
    def _(r):
        @pl.when(r < SHARED)
        def _():
            for way in (0, 1):
                x_land(r, way).wait_recv()
                f_copy(r, way).start()
                c_copy(r, 1 + way).start()

        @pl.when(r == 0)
        def _():
            pass_on(2, chunk(0, 2))
            pass_on(3, chunk(0, 3))

        @pl.when((r >= 1) & (r + 3 < SHARED))
        def _():
            pass_on(r + 3, chunk(0, r + 3))

        @pl.when(r + 2 < SHARED)
        def _():
            first(r + 2)

        @pl.when(r == 0)
        def _():
            start_y(4, chunk(0, 4))

        @pl.when(r < 4)
        def _():
            for k in (0, 1):
                start_y(SHARED + 2 * r + k, common(2 * r + k))

        @pl.when((r >= 1) & (r < 5))
        def _():
            for k in (0, 1):
                pass_on(SHARED + 2 * r - 2 + k, common(2 * r - 2 + k))

        @pl.when((r >= 2) & (r < 6))
        def _():
            for k in (0, 1):
                u = 2 * r - 4 + k
                for way in (0, 1):
                    g_copy(SHARED + u, common(u), way).wait_recv()
                v_copy(u).start()

        @pl.when(r == 1)
        def _():
            for g in range(4):
                for k in range(3):
                    for kind in (0, 1):
                        part = ag.at[kind, k + 1, g]
                        remote(part, part, a_s.at[kind, g, k], a_r.at[kind, g, k], at(z, y + 1, x, c)).wait_recv()
            multiply_near(0)

        @pl.when((r >= 1) & (r < SHARED))
        def _():
            multiply_near(r)

        @pl.when((r >= 1) & (r <= SHARED))
        def _():
            for way in (0, 1):
                f_land(r - 1, way).wait_recv()
            c_copy(r - 1, 3).start()

        @pl.when(r >= 2)
        def _():
            step(combine, r - 1)

        @pl.when(r == 2)
        def _():
            @pl.loop(0, 3)
            def _(q):
                combine(near(q, 0), 0)

        @pl.when(r >= 3)
        def _():
            step(finish, r - 3)

        @pl.when((r >= 2) & (r < 6))
        def _():
            for k in (0, 1):
                u = 2 * r - 4 + k
                v_land(u).wait_recv()
                multiply(common(u), 1 - k)

        @pl.when((r >= 1) & (r <= SHARED))
        def _():
            c_land(chunk(2, r - 1), r - 1, 3).wait_recv()
            multiply(chunk(2, r - 1), lax.rem(r - 1, 2))

    for g in range(4):
        for e in (1, 2, 3):
            for kind in (0, 1):
                a_copy(kind, g, e).wait_send()

    @pl.loop(0, SHARED)
    def _(r):
        for way in (0, 1):
            y_copy(r, chunk(0, r), way).wait_send()
            g_copy(r, chunk(0, r), way).wait_send()
            x_copy(r, way).wait_send()
            f_copy(r, way).wait_send()
        for q in range(4):
            c_copy(r, q).wait_send()

    @pl.loop(0, 8)
    def _(u):
        for way in (0, 1):
            y_copy(SHARED + u, common(u), way).wait_send()
            g_copy(SHARED + u, common(u), way).wait_send()
        v_copy(u).wait_send()

    @pl.loop(0, 4 * ROUNDS)
    def _(n):
        for way in (0, 1):
            h_copy(n, 0, way).wait_send()
            z_copy(n, 0, way).wait_send()


def project(attn_out, w_out, residual):
    dma = pltpu.SemaphoreType.DMA
    anywhere = pl.BlockSpec(memory_space=pl.ANY)
    return pl.pallas_call(
        project_kernel,
        name="project",
        out_shape=jax.ShapeDtypeStruct((128, 7168), jnp.bfloat16),
        in_specs=[anywhere] * 3,
        out_specs=pl.BlockSpec(memory_space=VMEM),
        scratch_shapes=[
            VMEM((2, 4, 4, 128, 512), jnp.bfloat16),
            VMEM((512, 7168), jnp.bfloat16),
            VMEM((28, 3, 512, CH), jnp.bfloat16),
            VMEM((28, 4, 128, CH), jnp.bfloat16),
            VMEM((28, 2, 64, CH), jnp.bfloat16),
            VMEM((28, 2, 128, CH), jnp.bfloat16),
            VMEM((128, 7168), jnp.bfloat16),
            dma((4,)), dma((2, 4, 3)), dma((2, 4, 3)), dma((13, 2)), dma((13, 2)), dma((13, 2)), dma((13, 2)),
            dma((8,)), dma((8,)), dma((5, 2)), dma((5, 2)), dma((5, 2)), dma((5, 2)), dma((5, 4)), dma((5, 4)),
            dma((28, 2)), dma((28, 2)), dma((28, 2)), dma((28, 2)),
        ],
        compiler_params=pltpu.CompilerParams(
            collective_id=0, has_side_effects=True, vmem_limit_bytes=58 * 1024 * 1024
        ),
    )(attn_out.reshape(4, 4, 128, 512), w_out, residual)


LANE = 896
GROUPS = ((0, 0), (1, 1), (2, 3), (3, 2))


def moe_kernel(
    hid_ref, gain_ref, rout_ref, cho_ref, wg_ref, wu_ref, wd_ref,
    back_ref, coeff_ref, count_ref,
    wg, wu, wd, rt, normed, gain, snd, land, rows, ybuf, r1, sbuf, half_in, full_in, rsend, ret, cnt, cnt_tp, cnt_ep,
    loc, d_s, d_r, ax_s, ax_r, af_s, af_r, ac_s, ac_r, k_s, k_r, l_s, l_r, rt_s, rt_r, rs_s, rs_r,
    p_s, p_r, h_s, h_r, q_s, q_r, b_s, b_r,
):
    z, y, x, c = place()
    tp = z * 4 + y
    ep = x * 2 + c
    sib = at(z, y, x, c + 1)
    width = hid_ref.shape[1]
    half = pl.ds(pl.multiple_of(c * (width // 2), width // 2), width // 2)
    loads = [pltpu.make_async_copy(s, d, loc.at[i]) for i, (s, d) in enumerate(((wg_ref, wg), (wu_ref, wu), (wd_ref, wd)))]
    for load in loads:
        load.start()
    tp_peers = [(dz, dy) for dz in (0, 1, 3, 2) for dy in (1, 3, 2, 0) if (dz, dy) != (0, 0)]
    ep_peers = [(dx, dc) for dx in (0, 1, 3, 2) for dc in (0, 1) if (dx, dc) != (0, 0)]

    def tp_at(dz, dy):
        return ring(z + dz) * 4 + ring(y + dy)

    def ep_at(dx, dc):
        return ring(x + dx) * 2 + lax.rem(c + dc, 2)

    barrier = pltpu.get_barrier_semaphore()
    for p in tp_peers:
        pl.semaphore_signal(barrier, inc=1, device_id=(tp_at(*p), ep), device_id_type=MESH)
    for p in ep_peers:
        pl.semaphore_signal(barrier, inc=1, device_id=(tp, ep_at(*p)), device_id_type=MESH)

    def cut(j):
        return slice(j * LANE, (j + 1) * LANE)

    row = lax.broadcasted_iota(jnp.int32, (256, 128), 0)
    lane = lax.broadcasted_iota(jnp.int32, (256, 128), 1)
    expert = row // 16
    member = jnp.zeros((256, 128), jnp.float32)
    for k in range(TOP):
        ck = cho_ref[k : k + 1, :]
        member += jnp.where(ck == expert, 1.0, 0.0)
    before = jnp.where(row[:128] < lane[:128], 1.0, 0.0).astype(jnp.bfloat16)
    rank = jnp.dot(member.astype(jnp.bfloat16), before, preferred_element_type=jnp.float32)
    slot = ((row // 8) % 2).astype(jnp.float32)
    pick = jnp.where(rank == slot, member, 0.0)
    feature = row % 8
    picked = jnp.zeros((256, LANE), jnp.float32)
    for j in range(8):
        pj = jnp.where(feature == j, pick, 0.0).astype(jnp.bfloat16)
        picked += jnp.dot(pj, hid_ref[:, cut(j)], preferred_element_type=jnp.float32)
    gains = gain_ref[...].astype(jnp.float32)
    for j in range(8):
        for i in range(7):
            gain[j : j + 1, i * 128 : (i + 1) * 128] = gains[j * 7 + i : j * 7 + i + 1, :]
    picked = picked.reshape(32, 8, LANE)
    ssq = jnp.sum(jnp.sum(picked * picked, axis=2, keepdims=True), axis=1, keepdims=True)
    outgoing = picked * lax.rsqrt(ssq / width + norm_eps) * gain[...][None]
    snd[...] = outgoing.astype(jnp.bfloat16).reshape(16, 16, LANE)
    contract_last = (((1,), (1,)), ((), ()))
    pl.semaphore_wait(barrier, len(tp_peers) + len(ep_peers))

    def d_copy(p):
        peer = tp_at(*p)
        return remote(snd.at[peer], land.at[ep, tp], d_s.at[peer], d_r.at[tp], (peer, ep))

    own_rows = pltpu.make_async_copy(snd.at[tp], land.at[ep, tp], loc.at[3])
    own_rows.start()
    for p in tp_peers:
        d_copy(p).start()

    named = jnp.zeros((256, 128), jnp.float32)
    for k in range(TOP):
        named += jnp.where(cho_ref[k : k + 1, :] == row, 1.0, 0.0)
    cnt[...] = lax.dot_general(
        jnp.ones((8, 128), jnp.bfloat16), named.astype(jnp.bfloat16), contract_last, preferred_element_type=jnp.float32
    )

    def k_copy(p):
        peer = tp_at(*p)
        return remote(cnt, cnt_tp.at[tp], k_s.at[peer], k_r.at[tp], (peer, ep))

    for p in tp_peers:
        k_copy(p).start()

    def group(dz):
        return pl.ds(pl.multiple_of(ring(z + dz) * 4, 4), 4)

    def x_copy(g, dz, way):
        part = land.at[ep, group(dz)]
        return remote(part, part, ax_s.at[g, way], ax_r.at[g, way], (tp, ep_at(1 - 2 * way, 0)))

    def x_land(g, dz, way):
        part = land.at[ep_at(2 * way - 1, 0), group(dz)]
        return remote(part, part, ax_s.at[g, way], ax_r.at[g, way], (tp, ep_at(1, 0)))

    def f_rows(dx, dz, way):
        return land.at[ep_at(dx, 0), pl.ds(pl.multiple_of(ring(z + dz) * 4 + 2 * way, 2), 2)]

    def f_copy(g, dz, way):
        part = f_rows(2 * way - 1, dz, way)
        return remote(part, part, af_s.at[g, way], af_r.at[g, way], (tp, ep_at(1 - 2 * way, 0)))

    def f_land(g, dz, way):
        part = f_rows(2, dz, way)
        return remote(part, part, af_s.at[g, way], af_r.at[g, way], (tp, ep_at(1, 0)))

    def c_copy(g, dz, q):
        part = land.at[ep_at(q, 0), group(dz)]
        return remote(part, part, ac_s.at[g, q], ac_r.at[g, q], sib)

    def c_land(g, dz, q):
        part = land.at[ep_at(q, 1), group(dz)]
        return remote(part, part, ac_s.at[g, q], ac_r.at[g, q], sib)

    def d_land(p):
        src = tp_at(*p)
        return remote(snd.at[src], land.at[ep, src], d_s.at[src], d_r.at[src], (src, ep))

    for g, dz in GROUPS:
        for p in tp_peers:
            if p[0] == dz:
                d_land(p).wait_recv()
        if dz == 0:
            own_rows.wait()
        for way in (0, 1):
            x_copy(g, dz, way).start()
        c_copy(g, dz, 0).start()

    def rt_copy(p):
        peer = tp_at(*p)
        return remote(rout_ref.at[:, half], rt.at[tp, :, half], rt_s.at[peer], rt_r.at[tp], (peer, ep))

    own_rt = pltpu.make_async_copy(rout_ref.at[:, half], rt.at[tp, :, half], loc.at[4])
    own_rt.start()
    for p in tp_peers:
        rt_copy(p).start()

    for p in tp_peers:
        src = tp_at(*p)
        remote(cnt, cnt_tp.at[src], k_s.at[src], k_r.at[src], (src, ep)).wait_recv()
    cnt_tp[tp] = cnt[...]
    part_sum = cnt_tp[0]
    for i in range(1, 16):
        part_sum += cnt_tp[i]
    cnt_ep[ep] = part_sum

    def l_copy(p):
        peer = ep_at(*p)
        return remote(cnt_ep.at[ep], cnt_ep.at[ep], l_s.at[peer], l_r.at[ep], (tp, peer))

    for p in ep_peers:
        l_copy(p).start()

    out_row = lax.broadcasted_iota(jnp.int32, (128, 128), 0)
    in_row = lax.broadcasted_iota(jnp.int32, (128, 128), 1)
    source = ((out_row % 16) // 2) * 16 + (out_row % 2) * 8 + out_row // 16
    perm = jnp.where(in_row == source, 1.0, 0.0).astype(jnp.bfloat16)

    def turn_rows(group_of):
        for part in range(2):
            block = land[group_of, part * 8 : part * 8 + 8].reshape(128, LANE)
            turned = jnp.dot(perm, block, preferred_element_type=jnp.float32).astype(jnp.bfloat16)
            to = pl.ds(pl.multiple_of(group_of * 32 + part * 16, 16), 16)
            rows[:, to, :] = turned.reshape(8, 16, LANE)

    turn_rows(ep)
    for g, dz in GROUPS:
        for way in (0, 1):
            x_land(g, dz, way).wait_recv()
            f_copy(g, dz, way).start()
            c_copy(g, dz, 3 - 2 * way).start()
    for q in (0, 3, 1):
        if q:
            turn_rows(ep_at(q, 0))
        if q == 1:
            for g, dz in GROUPS:
                for way in (0, 1):
                    f_land(g, dz, way).wait_recv()
                c_copy(g, dz, 2).start()
        for g, dz in GROUPS:
            c_land(g, dz, q).wait_recv()
        turn_rows(ep_at(q, 1))
    turn_rows(ep_at(2, 0))
    for g, dz in GROUPS:
        c_land(g, dz, 2).wait_recv()
    turn_rows(ep_at(2, 1))

    for load in loads:
        load.wait()
    gate_val = jnp.zeros((256, 256), jnp.float32)
    up_val = jnp.zeros((256, 256), jnp.float32)
    for j in range(8):
        gate_val += jnp.dot(rows[j], wg[cut(j), :], preferred_element_type=jnp.float32)
        up_val += jnp.dot(rows[j], wu[cut(j), :], preferred_element_type=jnp.float32)
    active = (gate_val / (1.0 + jnp.exp(-gate_val)) * up_val).astype(jnp.bfloat16)

    def p_copy(n):
        return remote(ybuf.at[n, :, 1 - c], r1.at[n], p_s.at[n], p_r.at[n], sib)

    def h_copy(n, way):
        rows_of = pl.ds(16 * way, 16)
        return remote(
            sbuf.at[n, ring(x + 2), rows_of], half_in.at[n, way],
            h_s.at[n, way], h_r.at[n, way], (tp, ep_at(1 - 2 * way, 0)),
        )

    def q_copy(n, way):
        to = 1 - 2 * way
        return remote(
            sbuf.at[n, ring(x + to)], full_in.at[n, way], q_s.at[n, way], q_r.at[n, way], (tp, ep_at(to, 0))
        )

    def forward(n):
        for way in (0, 1):
            to = ring(x + 1 - 2 * way)
            h_copy(n, way).wait_recv()
            rows_of = slice(16 * way, 16 * way + 16)
            both = sbuf[n, to, rows_of].astype(jnp.float32) + half_in[n, way].astype(jnp.float32)
            sbuf[n, to, rows_of] = both.astype(jnp.bfloat16)
            q_copy(n, way).start()

    for n in range(4):
        part = jnp.dot(active, wd[:, n * 2 * LANE : (n + 1) * 2 * LANE], preferred_element_type=jnp.float32)
        ybuf[n] = part.astype(jnp.bfloat16).reshape(4, 2, 32, 2 * LANE)
        p_copy(n).start()
    for n in range(4):
        p_copy(n).wait_recv()
        for i in range(4):
            both = ybuf[n, i, c].astype(jnp.float32) + r1[n, i].astype(jnp.float32)
            sbuf[n, i] = both.astype(jnp.bfloat16)
        for way in (0, 1):
            h_copy(n, way).start()
        if n:
            forward(n - 1)
    forward(3)

    for p in ep_peers:
        peer = ep_at(*p)
        remote(cnt_ep.at[peer], cnt_ep.at[peer], l_s.at[peer], l_r.at[peer], (tp, peer)).wait_recv()
    counts = cnt_ep[0]
    for i in range(1, 8):
        counts += cnt_ep[i]
    count_ref[...] = counts

    for p in tp_peers:
        src = tp_at(*p)
        remote(rout_ref.at[:, half], rt.at[src, :, half], rt_s.at[src], rt_r.at[src], (src, ep)).wait_recv()
    own_rt.wait()
    mine = rt.at[:, :, half]
    rt_sib = remote(mine, mine, rs_s.at[0], rs_r.at[0], sib)
    rt_sib.start()
    other = rt.at[:, :, pl.ds(pl.multiple_of((1 - c) * (width // 2), width // 2), width // 2)]
    ssq = jnp.zeros((128, 1), jnp.float32)
    for j in range(8):
        h = hid_ref[:, cut(j)].astype(jnp.float32)
        ssq += jnp.sum(h * h, axis=1, keepdims=True)
    scale = lax.rsqrt(ssq / width + norm_eps)
    for j in range(8):
        h = hid_ref[:, cut(j)].astype(jnp.float32)
        normed[:, cut(j)] = (h * scale * gain[j : j + 1, :]).astype(jnp.bfloat16)
    remote(other, other, rs_s.at[0], rs_r.at[0], sib).wait_recv()
    logits = jnp.zeros((256, 128), jnp.float32)
    for j in range(8):
        logits += lax.dot_general(
            rt[:, :, cut(j)].reshape(256, LANE), normed[:, cut(j)], contract_last, preferred_element_type=jnp.float32
        )
    scores = 1.0 / (1.0 + jnp.exp(-logits))
    chosen = []
    for k in range(TOP):
        hit = cho_ref[k : k + 1, :] == row
        chosen.append(jnp.sum(jnp.where(hit, scores, 0.0), axis=0, keepdims=True))
    norm_by = chosen[0]
    for k in range(1, TOP):
        norm_by = norm_by + chosen[k]
    weight = jnp.zeros((256, 128), jnp.float32)
    for k in range(TOP):
        weight += jnp.where(cho_ref[k : k + 1, :] == expert, route_scale * chosen[k] / norm_by, 0.0)
    coeff_ref[...] = jnp.where(pick > 0.0, weight, 0.0).T

    back_row = lax.broadcasted_iota(jnp.int32, (256, 32), 0)
    back_col = lax.broadcasted_iota(jnp.int32, (256, 32), 1)
    returned = jnp.zeros((256, LANE), jnp.float32)
    for n in range(4):
        total = sbuf[n, x].astype(jnp.float32)
        for way in (0, 1):
            q_copy(n, way).wait_recv()
            total += full_in[n, way].astype(jnp.float32)
        total = total.astype(jnp.bfloat16)
        for i in range(2):
            turn = jnp.where((back_row // 8 == back_col) & (back_row % 8 == 2 * n + i), 1.0, 0.0).astype(jnp.bfloat16)
            returned += jnp.dot(turn, total[:, cut(i)], preferred_element_type=jnp.float32)
    rsend[...] = returned.astype(jnp.bfloat16).reshape(16, 16, LANE)

    def b_copy(p):
        peer = tp_at(*p)
        return remote(rsend.at[peer], ret.at[tp], b_s.at[peer], b_r.at[tp], (peer, ep))

    own_back = pltpu.make_async_copy(rsend.at[tp], ret.at[tp], loc.at[5])
    own_back.start()
    for p in tp_peers:
        b_copy(p).start()
    own_back.wait()
    for p in tp_peers:
        src = tp_at(*p)
        remote(rsend.at[src], ret.at[src], b_s.at[src], b_r.at[src], (src, ep)).wait_recv()
    back_ref[...] = ret[...]

    for p in tp_peers:
        d_copy(p).wait_send()
        k_copy(p).wait_send()
        rt_copy(p).wait_send()
        b_copy(p).wait_send()
    for p in ep_peers:
        l_copy(p).wait_send()
    rt_sib.wait_send()
    for g, dz in GROUPS:
        for way in (0, 1):
            x_copy(g, dz, way).wait_send()
            f_copy(g, dz, way).wait_send()
        for q in range(4):
            c_copy(g, dz, q).wait_send()
    for n in range(4):
        p_copy(n).wait_send()
        for way in (0, 1):
            h_copy(n, way).wait_send()
            q_copy(n, way).wait_send()


def mix_kernel(hid_ref, back_ref, coeff_ref, count_ref, bias_ref, kept_ref, moe_ref, load_ref, next_ref):
    i = pl.program_id(0)
    kept_ref[...] = hid_ref[...]

    @pl.when(i == 0)
    def _():
        slots = 128.0 * 128.0 * TOP
        for k in range(2):
            counts = count_ref[0:1, k * 128 : (k + 1) * 128]
            load_ref[k : k + 1, :] = counts * 256.0 / slots
            gap = slots - counts * 256.0
            sign = jnp.where(gap > 0.0, 1.0, jnp.where(gap < 0.0, -1.0, 0.0))
            next_ref[k : k + 1, :] = bias_ref[k : k + 1, :] + bias_rate * sign

    back = back_ref[...].reshape(256, LANE)
    coeff = coeff_ref[...]
    lane_cut = lax.broadcasted_iota(jnp.int32, (128, 256), 1) % 8
    for k in range(4):
        here = lane_cut == 4 * i + k
        mixed = jnp.dot(jnp.where(here, coeff, 0.0).astype(jnp.bfloat16), back, preferred_element_type=jnp.float32)
        moe_ref[:, k * LANE : (k + 1) * LANE] = mixed.astype(jnp.bfloat16)


def experts(hidden_out, norm_gain, router, router_bias, choices, w_gate, w_up, w_down):
    dma = pltpu.SemaphoreType.DMA
    bf16, f32 = jnp.bfloat16, jnp.float32
    vmem = pl.BlockSpec(memory_space=VMEM)
    anywhere = pl.BlockSpec(memory_space=pl.ANY)
    back, coeff, counts = pl.pallas_call(
        moe_kernel,
        name="experts",
        out_shape=(
            jax.ShapeDtypeStruct((16, 16, LANE), bf16),
            jax.ShapeDtypeStruct((128, 256), f32),
            jax.ShapeDtypeStruct((8, 256), f32),
        ),
        in_specs=[vmem] * 4 + [anywhere] * 3,
        out_specs=(vmem,) * 3,
        scratch_shapes=[
            VMEM((7168, 256), bf16), VMEM((7168, 256), bf16), VMEM((256, 7168), bf16),
            VMEM((16, 16, 7168), bf16), VMEM((128, 7168), bf16), VMEM((8, LANE), f32), VMEM((16, 16, LANE), bf16),
            VMEM((8, 16, 16, LANE), bf16), VMEM((8, 256, LANE), bf16),
            VMEM((4, 4, 2, 32, 2 * LANE), bf16), VMEM((4, 4, 32, 2 * LANE), bf16),
            VMEM((4, 4, 32, 2 * LANE), bf16), VMEM((4, 2, 16, 2 * LANE), bf16), VMEM((4, 2, 32, 2 * LANE), bf16),
            VMEM((16, 16, LANE), bf16), VMEM((16, 16, LANE), bf16),
            VMEM((8, 256), f32), VMEM((16, 8, 256), f32), VMEM((8, 8, 256), f32),
            dma((6,)), dma((16,)), dma((16,)), dma((4, 2)), dma((4, 2)), dma((4, 2)), dma((4, 2)), dma((4, 4)), dma((4, 4)),
            dma((16,)), dma((16,)), dma((8,)), dma((8,)), dma((16,)), dma((16,)), dma((1,)), dma((1,)),
            dma((4,)), dma((4,)), dma((4, 2)), dma((4, 2)), dma((4, 2)), dma((4, 2)), dma((16,)), dma((16,)),
        ],
        compiler_params=pltpu.CompilerParams(
            collective_id=1, has_side_effects=True, vmem_limit_bytes=56 * 1024 * 1024
        ),
    )(
        hidden_out, norm_gain.reshape(-1, 128), router.T, choices.T,
        w_gate[0], w_up[0], w_down[0],
    )
    block = pl.BlockSpec((128, 4 * LANE), lambda i: (0, i))
    hidden_kept, moe_out, load, bias_next = pl.pallas_call(
        mix_kernel,
        name="mix",
        grid=(2,),
        out_shape=(
            jax.ShapeDtypeStruct((128, 7168), bf16),
            jax.ShapeDtypeStruct((128, 7168), bf16),
            jax.ShapeDtypeStruct((2, 128), f32),
            jax.ShapeDtypeStruct((2, 128), f32),
        ),
        in_specs=[block] + [vmem] * 4,
        out_specs=(block, block, vmem, vmem),
    )(hidden_out, back, coeff, counts, router_bias.reshape(2, 128))
    return hidden_kept, moe_out, load.reshape(-1), bias_next.reshape(-1)


def on_device(
    attn_out, residual, w_out, norm_gain, router, router_bias, choices, w_gate, w_up, w_down
):
    hidden_out = project(attn_out, w_out, residual)
    return experts(hidden_out, norm_gain, router, router_bias, choices, w_gate, w_up, w_down)


def solution(mesh):
    placed = (
        P("ep", "tp"),
        P(("ep", "tp"), None),
        P("tp", None),
        P(),
        P(None, "tp"),
        P(),
        P(("ep", "tp"), None),
        P("tp", None, "ep"),
        P("tp", None, "ep"),
        P("tp", "ep", None),
    )
    return jax.shard_map(
        on_device,
        mesh=mesh,
        in_specs=placed,
        out_specs=(P(("ep", "tp"), None), P(("ep", "tp"), None), P(), P()),
        check_vma=False,
    )
```
